128 devices in a mesh: wide: 32 (over x, z, core), narrow: 4 (over y).
Axes of the slice: x: 4, y: 4, z: 4, core: 2. Of those that a mesh axis runs over, the one named last changes fastest.
Arguments:
- ref_local: float32 [3, 128, 16, 128], P(None, 'wide', 'narrow'), may hold values from 0 to 8, as said below
- displacement: float32 [3, 128, 16, 128], P(None, 'wide', 'narrow'), may hold values from -0.3125 to 0.3125
- velocity: float32 [3, 128, 16, 128], P(None, 'wide', 'narrow'), may hold values from -4 to 4
- acceleration: float32 [3, 128, 16, 128], P(None, 'wide', 'narrow'), may hold values from -12 to 12
- history: float32 [128, 16, 6, 128, 128], P('wide', 'narrow'), may hold values from 0 to 1.5
- critical: float32 [128, 16, 6], P('wide', 'narrow'), may hold values from 0.003 to 0.03
- active: int32 [128, 16, 6], P('wide', 'narrow'), may hold values 0 or 1
- partners: int32 [128, 16, 6], P('wide', 'narrow'), may hold values from 0 to 8, as said below
- move_src: int32 [32, 4, 2, 2], P('wide', 'narrow'), may hold values from -1 to 15, as said below
- move_dst: int32 [32, 4, 2, 2], P('wide', 'narrow'), may hold values from -1 to 15, as said below
Outputs:
- ref_out: float32 [3, 128, 16, 128], P(None, 'wide', 'narrow')
- disp_out: float32 [3, 128, 16, 128], P(None, 'wide', 'narrow')
- vel_out: float32 [3, 128, 16, 128], P(None, 'wide', 'narrow')
- acc_out: float32 [3, 128, 16, 128], P(None, 'wide', 'narrow')
- hist_out: float32 [128, 16, 6, 128, 128], P('wide', 'narrow')
The draws below stay inside these ranges and needn't reach their ends.
Inputs may be any that keep to these rules, and one draw needn't show every extreme that they name: ref_local[:, i, j, p] lies in [0, 4] x [0, 4] x [0, 8]; two points of the grid are at least 0.6 apart. `partners`: slot 0 names the cluster itself (offset 4); the other slots of a cluster name distinct offsets other than 4. move_src[w, n, 0, :] lists the clusters tile (w, n) hands to tile (w + 1, n), move_src[w, n, 1, :] those it hands to tile (w - 1, n), used entries first and -1 after them; a tile hands on distinct clusters. Across each boundary between tiles (w, n) and (w + 1, n) equally many clusters go each way, 1 to 2, and 2 across some boundary of every n. `move_dst`: -1 exactly where move_src is -1; the slots that a tile hands on are exactly the slots that arriving clusters take, one each.
All inputs are finite; a program needn't handle non-finite values. No bound on the sum of `active` on one device may be relied on, other than what follows from the above.
Results may differ from the reference program's by a relative error of at most 0.0003.
Values sent between devices are 32-bit elements; how exact they have to be, the bound alone decides.
A program may use at most 128 MiB of HBM per device.

```python
import math
import jax
import jax.numpy as jnp
from jax import lax

CLUS_W = 4
CLUS_N = 4
LAYERS = 8
BLOCK_SLOTS = 6
MOVE_CAP = 2
POINTS = 128
CLUSTERS = 16
TILES_W = 32
TILES_N = 4
GRID_W = 128
GRID_N = 16


def move_plan(key):
    key_count, key_peak, key_order = jax.random.split(key, 3)
    edge_counts = jax.random.randint(key_count, (TILES_W - 1, TILES_N), 1, MOVE_CAP + 1)
    peak_edge = jax.random.randint(key_peak, (TILES_N,), 0, TILES_W - 1)
    edge_ids = jnp.arange(TILES_W - 1, dtype=jnp.int32)[:, None]
    edge_counts = jnp.where(edge_ids == peak_edge[None, :], MOVE_CAP, edge_counts).astype(jnp.int32)
    zero_row = jnp.zeros((1, TILES_N), jnp.int32)
    right_count = jnp.concatenate([edge_counts, zero_row], 0)
    left_count = jnp.concatenate([zero_row, edge_counts], 0)
    scores = jax.random.randint(key_order, (TILES_W, TILES_N, CLUSTERS), 0, 1 << 16) * CLUSTERS + jnp.arange(CLUSTERS, dtype=jnp.int32)
    shuffle = jnp.argsort(scores, axis=2).astype(jnp.int32)
    step_ids = jnp.broadcast_to(jnp.arange(MOVE_CAP, dtype=jnp.int32)[None, None, :], (TILES_W, TILES_N, MOVE_CAP))
    right_src = jnp.where(step_ids < right_count[..., None], jnp.take_along_axis(shuffle, step_ids, axis=2), -1)
    left_pos = jnp.minimum(right_count[..., None] + step_ids, CLUSTERS - 1)
    left_src = jnp.where(step_ids < left_count[..., None], jnp.take_along_axis(shuffle, left_pos, axis=2), -1)
    both_count = right_count + left_count
    shuffle_next = jnp.concatenate([shuffle[1:], shuffle[:1]], 0)
    both_next = jnp.concatenate([both_count[1:], both_count[:1]], 0)
    right_pos = jnp.clip(both_next[..., None] - 1 - step_ids, 0, CLUSTERS - 1)
    right_dst = jnp.where(right_src >= 0, jnp.take_along_axis(shuffle_next, right_pos, axis=2), -1)
    shuffle_prev = jnp.concatenate([shuffle[-1:], shuffle[:-1]], 0)
    right_prev = jnp.concatenate([right_count[-1:], right_count[:-1]], 0)
    back_pos = jnp.clip(right_prev[..., None] - 1 - step_ids, 0, CLUSTERS - 1)
    left_dst = jnp.where(left_src >= 0, jnp.take_along_axis(shuffle_prev, back_pos, axis=2), -1)
    return (jnp.stack([right_src, left_src], 2).astype(jnp.int32), jnp.stack([right_dst, left_dst], 2).astype(jnp.int32))


def draw_move_src(key, part):
    return move_plan(key)[0]


def draw_move_dst(key, part):
    return move_plan(key)[1]


def draw_partners(key, part):
    key = jax.random.fold_in(key, 11)
    scores = jax.random.randint(key, (GRID_W, GRID_N, 8), 0, 1 << 16) * 8 + jnp.arange(8, dtype=jnp.int32)
    picked = jnp.argsort(scores, axis=2)[..., :BLOCK_SLOTS - 1].astype(jnp.int32)
    others = jnp.where(picked >= 4, picked + 1, picked)
    selfs = jnp.full((GRID_W, GRID_N, 1), 4, jnp.int32)
    return jnp.concatenate([selfs, others], 2).astype(jnp.int32)


def draw_ref_local(key, part):
    key = jax.random.fold_in(key, 5)
    point_ids = jnp.arange(POINTS, dtype=jnp.int32)
    along_w = point_ids // (4 * LAYERS)
    along_n = point_ids // LAYERS % 4
    along_t = point_ids % LAYERS
    lattice = jnp.stack([along_w, along_n, along_t], 0).astype(jnp.float32) + 0.5
    jitter = jax.random.uniform(key, (3, GRID_W, GRID_N, POINTS), jnp.float32, -0.2, 0.2)
    return lattice[:, None, None, :] + jitter


def plant(result, rng, low, high):
    longest = result.shape.index(max(result.shape))
    spots = []
    for shift in (0, 1):
        where = [jax.random.randint(jax.random.fold_in(rng, axis), (), 0, length) for axis, length in enumerate(result.shape)]
        where[longest] = (where[longest] + shift) % result.shape[longest]
        spots.append(tuple(where))
    return result.at[spots[0]].set(low).at[spots[1]].set(high)


def steps_of(key, extent, pieces, least, high):
    level, own = 1.0, jax.random.fold_in(key, 6)
    for axis_at, parts in pieces:
        heights = jnp.exp(jax.random.uniform(jax.random.fold_in(own, axis_at), (parts,), jnp.float32, least / len(pieces), high / len(pieces)))
        level = level * jnp.repeat(heights, extent[axis_at] // parts).reshape([-1 if axis == axis_at else 1 for axis in range(len(extent))])
    return level


def normal_values(rng, shape, spread, most, pieces=(), held_as=jnp.bfloat16):
    array = spread * jax.random.normal(rng, shape, jnp.float32)
    if pieces:
        array = array * steps_of(rng, shape, pieces, -0.22, 0.18)
    return jnp.clip(array, -most, most).astype(held_as)


def setup_inputs(seed: int = 0) -> dict:
    keys = jax.random.split(jax.random.key(seed), 11)
    return {
        "ref_local": draw_ref_local(jax.random.fold_in(keys[10], 71), 0),
        "displacement": normal_values(keys[1], (3, GRID_W, GRID_N, POINTS), 0.02, 0.3125, ((1, 32), (2, 4)), jnp.float32),
        "velocity": normal_values(keys[2], (3, GRID_W, GRID_N, POINTS), 0.3, 4.0, ((1, 32), (2, 4)), jnp.float32),
        "acceleration": normal_values(keys[3], (3, GRID_W, GRID_N, POINTS), 2.0, 12.0, ((1, 32), (2, 4)), jnp.float32),
        "history": jnp.clip(1.5 * jax.random.uniform(keys[4], (GRID_W, GRID_N, BLOCK_SLOTS, POINTS, POINTS), jnp.float32) ** steps_of(keys[4], (GRID_W, GRID_N, BLOCK_SLOTS, POINTS, POINTS), ((0, 32), (1, 4)), -0.2, 0.2), 0.0, 1.5),
        "critical": jnp.clip(jnp.exp(math.log(0.03) - 2.3025851 * jax.random.uniform(keys[5], (GRID_W, GRID_N, BLOCK_SLOTS), jnp.float32) ** steps_of(keys[5], (GRID_W, GRID_N, BLOCK_SLOTS), ((0, 32), (1, 4)), -0.2, 0.2)), 0.003, 0.03),
        "active": plant((jax.random.randint(keys[6], (GRID_W, GRID_N, BLOCK_SLOTS), 0, 8) < 7).astype(jnp.int32), jax.random.fold_in(keys[6], 1), 0, 1),
        "partners": draw_partners(jax.random.fold_in(keys[10], 71), 0),
        "move_src": draw_move_src(jax.random.fold_in(keys[10], 71), 0),
        "move_dst": draw_move_dst(jax.random.fold_in(keys[10], 71), 0),
    }


STIFFNESS = 8.0
DAMPING = 0.8
TIME_STEP = 0.1
RANGE_SQ = 9.0
CELL_SPAN = 4.0

def advance(displacement, velocity, acceleration):
    disp_new = displacement + TIME_STEP * velocity + 0.5 * TIME_STEP * TIME_STEP * acceleration
    vel_half = velocity + 0.5 * TIME_STEP * acceleration
    return (disp_new, vel_half)

def bond_terms(own_rows, other_rows, shift_w, shift_n, history_rows, limit_rows, switch, same_cluster):
    points = own_rows.shape[2]
    unit_eye = jnp.eye(points, dtype=jnp.float32)
    live_mask = switch[:, None, None] * (1.0 - same_cluster[:, None, None] * unit_eye[None])
    anchors = (CELL_SPAN * shift_w, CELL_SPAN * shift_n, jnp.zeros_like(shift_w))
    ref_sq = jnp.zeros(live_mask.shape, jnp.float32)
    cur_sq = jnp.zeros(live_mask.shape, jnp.float32)
    closing = jnp.zeros(live_mask.shape, jnp.float32)
    cur_gaps = []
    for axis_id in range(3):
        anchor = anchors[axis_id][:, None, None]
        ref_gap = other_rows[axis_id][:, None, :] + anchor - own_rows[axis_id][:, :, None]
        cur_gap = other_rows[3 + axis_id][:, None, :] + anchor - own_rows[3 + axis_id][:, :, None]
        vel_gap = other_rows[6 + axis_id][:, None, :] - own_rows[6 + axis_id][:, :, None]
        ref_sq = ref_sq + ref_gap * ref_gap
        cur_sq = cur_sq + cur_gap * cur_gap
        closing = closing + vel_gap * cur_gap
        cur_gaps.append(cur_gap)
    bonded = live_mask > 0.5
    rest_len = jnp.where(bonded, jnp.sqrt(ref_sq), 1.0)
    now_len = jnp.where(bonded, jnp.sqrt(cur_sq), 1.0)
    stretch = jnp.where(bonded, (now_len - rest_len) / rest_len, 0.0)
    safe_limit = jnp.where(limit_rows > 0.0, limit_rows, 1.0)
    history_new = jnp.where(bonded, jnp.maximum(history_rows, stretch / safe_limit[:, None, None]), history_rows)
    intact = jnp.clip(2.0 - history_new, 0.0, 1.0)
    weight = jnp.exp(-ref_sq / RANGE_SQ) * intact * live_mask
    factor = weight * (STIFFNESS * stretch + DAMPING * closing / now_len) / now_len
    slot_pulls = jnp.stack([lax.optimization_barrier(jnp.sum(factor * gap_axis, axis=2)) for gap_axis in cur_gaps], 0)
    return (slot_pulls, history_new)

def row_terms(packed):
    return bond_terms(packed[0], packed[1], packed[2], packed[3], packed[4], packed[5], packed[6], packed[7])

def reference(ref_local, displacement, velocity, acceleration, history, critical, active, partners, move_src, move_dst):
    disp_new, vel_half = advance(displacement, velocity, acceleration)
    grid_field = jnp.concatenate([ref_local, ref_local + disp_new, vel_half], 0)
    padded = jnp.pad(grid_field, ((0, 0), (1, 1), (1, 1), (0, 0)))
    row_ids = jnp.arange(GRID_W, dtype=jnp.int32)[:, None]
    col_ids = jnp.arange(GRID_N, dtype=jnp.int32)[None, :]
    own_rows = jnp.moveaxis(grid_field, 1, 0)
    pulls_total = jnp.zeros((GRID_W, 3, GRID_N, POINTS), jnp.float32)
    hist_list = []
    for slot_id in range(BLOCK_SLOTS):
        offset = partners[:, :, slot_id]
        shift_w = offset // 3 - 1
        shift_n = offset % 3 - 1
        other_rows = padded[:, row_ids + 1 + shift_w, col_ids + 1 + shift_n, :]
        inside = (row_ids + shift_w >= 0) & (row_ids + shift_w < GRID_W) & (col_ids + shift_n >= 0) & (col_ids + shift_n < GRID_N)
        switch = (inside & (active[:, :, slot_id] > 0)).astype(jnp.float32)
        same_cluster = (offset == 4).astype(jnp.float32)
        slot_pulls, hist_slot = lax.map(row_terms, (own_rows, jnp.moveaxis(other_rows, 1, 0), shift_w.astype(jnp.float32), shift_n.astype(jnp.float32), history[:, :, slot_id], critical[:, :, slot_id], switch, same_cluster))
        pulls_total = pulls_total + slot_pulls
        hist_list.append(hist_slot)
    acc_new = jnp.moveaxis(pulls_total, 0, 1)
    vel_new = vel_half + 0.5 * TIME_STEP * acc_new
    hist_new = jnp.stack(hist_list, 2)
    cell_total = GRID_W * GRID_N
    tile_w = jnp.arange(TILES_W, dtype=jnp.int32)[:, None, None, None]
    tile_n = jnp.arange(TILES_N, dtype=jnp.int32)[None, :, None, None]
    heading = jnp.arange(2, dtype=jnp.int32)[None, None, :, None]
    from_cell = (tile_w * CLUS_W + move_src // CLUS_N) * GRID_N + tile_n * CLUS_N + move_src % CLUS_N
    to_cell = ((tile_w + 1 - 2 * heading) * CLUS_W + move_dst // CLUS_N) * GRID_N + tile_n * CLUS_N + move_dst % CLUS_N
    to_cell = jnp.where(move_src >= 0, to_cell, cell_total).astype(jnp.int32)
    source = jnp.arange(cell_total, dtype=jnp.int32).at[to_cell.reshape(-1)].set(from_cell.reshape(-1).astype(jnp.int32), mode='drop')

    def relocate(state_rows):
        return jnp.take(state_rows.reshape(3, cell_total, POINTS), source, axis=1).reshape(state_rows.shape)
    hist_out = jnp.take(hist_new.reshape(cell_total, BLOCK_SLOTS, POINTS, POINTS), source, axis=0).reshape(hist_new.shape)
    return (relocate(ref_local), relocate(disp_new), relocate(vel_new), relocate(acc_new), hist_out)
```

```python
import functools

import jax
import jax.numpy as jnp
import numpy as np
from jax import lax
from jax.experimental import pallas as pl
from jax.experimental.pallas import tpu as pltpu
from jax.sharding import PartitionSpec as P

STIFFNESS = 8.0
DAMPING = 0.8
TIME_STEP = 0.1
CELL_SPAN = 4.0
FALLOFF = float(-np.log2(np.e) / 9.0)
FAR = 1000.0
APART = 1.0e6

F32 = jnp.float32
MESH = pl.DeviceIdType.MESH
CW = CN = 4
CLUSTERS = CW * CN
SLOTS = 6
POINTS = 128
HALO = CN + 2
STAYS = 15
CHUNK = 32
SIDES = tuple((i, j) for i in (-1, 0, 1) for j in (-1, 0, 1) if (i, j) != (0, 0))


def sorted_four(a, b, c, d):
    lo, hi = jnp.minimum, jnp.maximum
    a, b, c, d = lo(a, b), hi(a, b), lo(c, d), hi(c, d)
    a, c, b, d = lo(a, c), hi(a, c), lo(b, d), hi(b, d)
    return (a, lo(b, c), hi(b, c), d)


def moved_ids(move_src):
    ids = [move_src[0, 0, d, m] for d in range(2) for m in range(2)]
    return sorted_four(*[jnp.where(i >= 0, i, 99) for i in ids])


def step_kernel(
    wide_size, narrow_size,
    ref_local, displacement, velocity, acceleration, critical, active, partners, move_src, move_dst, history,
    hist_rows, state_rows,
    held, table, columns, pulls, partner_rows, apart,
    load_sem, halo_send, halo_recv, hist_send, hist_recv, state_send, state_recv,
):
    me_w, me_n = lax.axis_index("wide"), lax.axis_index("narrow")
    loads = [pltpu.make_async_copy(history.at[c], held.at[c], load_sem.at[c]) for c in range(CLUSTERS)]
    for copy in loads:
        copy.start()

    def device(dw, dn):
        return (lax.rem(me_w + dw + wide_size, wide_size), lax.rem(me_n + dn + narrow_size, narrow_size))

    barrier = pltpu.get_barrier_semaphore()
    for dw, dn in SIDES:
        pl.semaphore_signal(barrier, inc=1, device_id=device(dw, dn), device_id_type=MESH)

    for a in range(CW):
        for b in range(CN):
            spot = (a + 1) * HALO + b + 1
            for d in range(3):
                r = ref_local[d, a, b:b + 1]
                v = velocity[d, a, b:b + 1]
                acc = acceleration[d, a, b:b + 1]
                u = displacement[d, a, b:b + 1] + TIME_STEP * v + 0.5 * TIME_STEP * TIME_STEP * acc
                table[spot, d:d + 1] = r
                table[spot, 3 + d:4 + d] = r + u
                table[spot, 6 + d:7 + d] = v + 0.5 * TIME_STEP * acc
                table[spot, 9 + d:10 + d] = u
            table[spot, 12:16] = jnp.zeros((4, POINTS), F32)

    pl.semaphore_wait(barrier, len(SIDES))
    halos = []
    for n, (dw, dn) in enumerate(SIDES):
        rows = range(1, CW + 1) if dw == 0 else (CW if dw > 0 else 1,)
        for m, row in enumerate(rows):
            to_row = row if dw == 0 else (0 if dw > 0 else CW + 1)
            if dn == 0:
                first, to_first, count = 1, 1, CN
            else:
                first, to_first, count = (CN, 0, 1) if dn > 0 else (1, CN + 1, 1)
            halos.append(pltpu.make_async_remote_copy(
                src_ref=table.at[pl.ds(row * HALO + first, count)],
                dst_ref=table.at[pl.ds(to_row * HALO + to_first, count)],
                send_sem=halo_send.at[n, m], recv_sem=halo_recv.at[n, m],
                device_id=device(dw, dn), device_id_type=MESH,
            ))
    for copy in halos:
        copy.start()

    sub = lax.broadcasted_iota(jnp.int32, (POINTS, POINTS), 0)
    lane = lax.broadcasted_iota(jnp.int32, (POINTS, POINTS), 1)
    apart[...] = jnp.where(sub == lane, APART, 0.0).astype(F32)

    for copy in loads:
        copy.wait()
    for copy in halos:
        copy.wait()

    def cluster(c, out, after_chunk):
        a, b = c // CN, lax.rem(c, CN)
        own = table[(a + 1) * HALO + b + 1]
        columns[...] = jnp.transpose(own)
        for k in range(SLOTS):
            o = partners[a, b, k]
            dw, dn = o // 3 - 1, lax.rem(o, 3) - 1
            gw, gn = me_w * CW + a + dw, me_n * CN + b + dn
            inside = (gw >= 0) & (gw < wide_size * CW) & (gn >= 0) & (gn < narrow_size * CN)
            on = inside & (active[a, b, k] > 0)
            other = table[(a + 1 + dw) * HALO + b + 1 + dn]
            shift = (CELL_SPAN * dw.astype(F32), CELL_SPAN * dn.astype(F32), jnp.where(on, 0.0, FAR))
            for f in range(9):
                row = other[f:f + 1]
                if f < 6:
                    row = row + shift[f % 3]
                partner_rows[k, f] = jnp.broadcast_to(row, (8, POINTS))
            limit = jnp.full((8, POINTS), critical[a, b, k], F32)
            partner_rows[k, 9] = jnp.where(on, 1.0, 0.0) / limit

        def chunk(i, carry):
            for u in range(CHUNK // 8):
                r = pl.ds(pl.multiple_of(i * CHUNK + u * 8, 8), 8)
                mine = columns[r, :]
                mine = [jnp.broadcast_to(mine[:, f:f + 1], (8, POINTS)) for f in range(9)]
                total = None
                for k in range(SLOTS):
                    q = [partner_rows[k, f] for f in range(10)]
                    x = [q[d] - mine[d] for d in range(3)]
                    e = [q[3 + d] - mine[3 + d] for d in range(3)]
                    v = [q[6 + d] - mine[6 + d] for d in range(3)]
                    rest_sq = x[0] * x[0] + x[1] * x[1] + x[2] * x[2]
                    now_sq = e[0] * e[0] + e[1] * e[1] + e[2] * e[2]
                    rate = v[0] * e[0] + v[1] * e[1] + v[2] * e[2]
                    if k == 0:
                        same = apart[r, :]
                        rest_sq = rest_sq + same
                        now_sq = now_sq + same
                    rest_inv = lax.rsqrt(rest_sq)
                    now_inv = lax.rsqrt(now_sq)
                    stretch = now_sq * now_inv * rest_inv - 1.0
                    scaled = stretch * q[9]
                    if k == 0:
                        scaled = scaled - same
                    hist = jnp.maximum(held[c, k, r, :], scaled)
                    hist_rows[out, k, r, :] = hist
                    weight = jnp.exp2(rest_sq * FALLOFF) * jnp.minimum(jnp.maximum(2.0 - hist, 0.0), 1.0)
                    factor = weight * (stretch + (DAMPING / STIFFNESS) * (rate * now_inv)) * now_inv
                    term = [factor * e[d] for d in range(3)]
                    total = term if total is None else [total[d] + term[d] for d in range(3)]
                for d in range(3):
                    pulls[r, d:d + 1] = STIFFNESS * jnp.sum(total[d], axis=1, keepdims=True)
            after_chunk(i)
            return carry

        lax.fori_loop(0, POINTS // CHUNK, chunk, 0)
        acc = jnp.transpose(pulls[...])[0:3]
        state_rows[out, 0:3] = own[0:3]
        state_rows[out, 3:6] = own[9:12]
        state_rows[out, 6:9] = own[6:9] + 0.5 * TIME_STEP * acc
        state_rows[out, 9:12] = acc

    def hist_copy(e, i):
        part = pl.ds(pl.multiple_of(i * CHUNK, 8), CHUNK)
        return pltpu.make_async_remote_copy(
            src_ref=hist_rows.at[STAYS + 4 + e, :, part, :], dst_ref=hist_rows.at[STAYS + e, :, part, :],
            send_sem=hist_send.at[e, i], recv_sem=hist_recv.at[e, i],
            device_id=device(1 - 2 * lax.rem(e, 2), 0), device_id_type=MESH,
        )

    def state_copy(e):
        return pltpu.make_async_remote_copy(
            src_ref=state_rows.at[STAYS + 4 + e], dst_ref=state_rows.at[STAYS + e],
            send_sem=state_send.at[e], recv_sem=state_recv.at[e],
            device_id=device(1 - 2 * lax.rem(e, 2), 0), device_id_type=MESH,
        )

    def hand_on(e, carry):
        d, m = lax.rem(e, 2), e // 2
        c = jnp.maximum(move_src[0, 0, d, m], 0)
        cluster(c, STAYS + 4 + e, lambda i: hist_copy(e, i).start())
        tag = jnp.full((4, POINTS), move_dst[0, 0, d, m], jnp.int32).astype(F32)
        state_rows[STAYS + 4 + e, 12:16] = tag
        state_copy(e).start()
        return carry

    lax.fori_loop(0, 4, hand_on, 0)

    moved = moved_ids(move_src)

    def stay(j, carry):
        c = j
        for m in moved:
            c = jnp.where(m <= c, c + 1, c)
        cluster(jnp.minimum(c, CLUSTERS - 1), j, lambda i: None)
        state_rows[j, 12:16] = jnp.zeros((4, POINTS), F32)
        return carry

    lax.fori_loop(0, jnp.where((me_w == 0) | (me_w == wide_size - 1), STAYS, STAYS - 1), stay, 0)

    for e in range(4):
        for i in range(POINTS // CHUNK):
            hist_copy(e, i).wait()
        state_copy(e).wait()


def place_kernel(hist_rows, state_rows, move_src, ref_out, disp_out, vel_out, acc_out, hist_out, sem):
    moved = moved_ids(move_src)
    tags = [jnp.max(state_rows[STAYS + e, 12:13, :]).astype(jnp.int32) for e in range(4)]
    copies = []
    for o in range(CLUSTERS):
        source = o
        for m in moved:
            source = jnp.where(m < o, source - 1, source)
        for e in range(4):
            source = jnp.where(tags[e] == o, STAYS + e, source)
        copies.append(pltpu.make_async_copy(hist_rows.at[source], hist_out.at[o], sem.at[o]))
        copies[-1].start()
        rows = state_rows[source]
        for f, ref in enumerate((ref_out, disp_out, vel_out, acc_out)):
            for d in range(3):
                ref[d, o // CN, o % CN:o % CN + 1] = rows[3 * f + d:3 * f + d + 1]
    for copy in copies:
        copy.wait()


def per_device(
    wide_size, narrow_size,
    ref_local, displacement, velocity, acceleration, history, critical, active, partners, move_src, move_dst,
):
    vmem, smem, anywhere = (pl.BlockSpec(memory_space=m) for m in (pltpu.VMEM, pltpu.SMEM, pl.ANY))
    total = STAYS + 8
    hist_shape, state_shape = (total, SLOTS, POINTS, POINTS), (total, 16, POINTS)
    hist_rows, state_rows = pl.pallas_call(
        functools.partial(step_kernel, wide_size, narrow_size),
        out_shape=(pltpu.VMEM(hist_shape, F32), pltpu.VMEM(state_shape, F32)),
        in_specs=[vmem] * 4 + [smem] * 5 + [anywhere],
        out_specs=(vmem, vmem),
        scratch_shapes=[
            pltpu.VMEM((CLUSTERS, SLOTS, POINTS, POINTS), F32),
            pltpu.VMEM((HALO * HALO, 16, POINTS), F32),
            pltpu.VMEM((POINTS, 16), F32),
            pltpu.VMEM((POINTS, 8), F32),
            pltpu.VMEM((SLOTS, 10, 8, POINTS), F32),
            pltpu.VMEM((POINTS, POINTS), F32),
            pltpu.SemaphoreType.DMA((CLUSTERS,)),
            pltpu.SemaphoreType.DMA((8, 4)),
            pltpu.SemaphoreType.DMA((8, 4)),
            pltpu.SemaphoreType.DMA((4, POINTS // CHUNK)),
            pltpu.SemaphoreType.DMA((4, POINTS // CHUNK)),
            pltpu.SemaphoreType.DMA((4,)),
            pltpu.SemaphoreType.DMA((4,)),
        ],
        compiler_params=pltpu.CompilerParams(
            collective_id=0, has_side_effects=True, vmem_limit_bytes=16 << 20
        ),
        name="step",
    )(
        ref_local, displacement, velocity, acceleration, critical, active, partners, move_src, move_dst,
        history.reshape(CLUSTERS, SLOTS, POINTS, POINTS),
    )
    hist_rows = pltpu.with_memory_space_constraint(hist_rows, pltpu.VMEM)
    state_rows = pltpu.with_memory_space_constraint(state_rows, pltpu.VMEM)
    state = jax.ShapeDtypeStruct(ref_local.shape, F32)
    outs = pl.pallas_call(
        place_kernel,
        out_shape=(state,) * 4 + (jax.ShapeDtypeStruct((CLUSTERS, SLOTS, POINTS, POINTS), F32),),
        in_specs=[anywhere, vmem, smem],
        out_specs=(vmem,) * 4 + (anywhere,),
        scratch_shapes=[pltpu.SemaphoreType.DMA((CLUSTERS,))],
        compiler_params=pltpu.CompilerParams(vmem_limit_bytes=8 << 20),
        name="place",
    )(hist_rows, state_rows, move_src)
    return outs[:4] + (outs[4].reshape(history.shape),)


def solution(mesh):
    field = P(None, "wide", "narrow", None)
    blocks = P("wide", "narrow", None)
    hist = P("wide", "narrow", None, None, None)
    moves = P("wide", "narrow", None, None)
    return jax.shard_map(
        functools.partial(per_device, mesh.shape["wide"], mesh.shape["narrow"]),
        mesh=mesh,
        in_specs=(field,) * 4 + (hist,) + (blocks,) * 3 + (moves,) * 2,
        out_specs=(field,) * 4 + (hist,),
        check_vma=False,
    )
```

```python
import functools

import jax
import jax.numpy as jnp
import numpy as np
from jax import lax
from jax.experimental import pallas as pl
from jax.experimental.pallas import tpu as pltpu
from jax.sharding import PartitionSpec as P

STIFFNESS = 8.0
DAMPING = 0.8
TIME_STEP = 0.1
CELL_SPAN = 4.0
FALLOFF = float(-np.log2(np.e) / 9.0)
FAR = 1024.0
APART = 1.0e6
TINY = 1.0e-12

F32 = jnp.float32
BF16 = jnp.bfloat16
MESH = pl.DeviceIdType.MESH
CW = CN = 4
CLUSTERS = CW * CN
SLOTS = 6
POINTS = 128
STAYS = 15
TILES = CLUSTERS + 20
SIDES = ((-1, 0), (1, 0), (0, -1), (0, 1), (-1, -1), (-1, 1), (1, -1), (1, 1))
SIDE_AT = (16, 20, 24, 28, 32, 33, 34, 35)
SIDE_COUNT = (4, 4, 4, 4, 1, 1, 1, 1)

ROW_R, ROW_U, ROW_V, ROW_Y, ROW_SQ, ROW_ONE = 0, 3, 6, 9, 12, 15
PARTS = ((0, 0), (1, 0), (0, 1), (1, 1), (2, 0), (0, 2))


def pairing():
    s = np.zeros((3, 96, 48), np.float32)
    for block, (q, p) in enumerate(PARTS):
        for d in range(3):
            s[0, block * 16 + ROW_R + d, p * 16 + ROW_R + d] = -2
            s[1, block * 16 + ROW_U + d, p * 16 + ROW_Y + d] = -2
            s[1, block * 16 + ROW_R + d, p * 16 + ROW_U + d] = -2
            s[2, block * 16 + ROW_Y + d, p * 16 + ROW_V + d] = -1
            s[2, block * 16 + ROW_V + d, p * 16 + ROW_Y + d] = -1
    for g in range(3):
        for part in range(3):
            s[g, PARTS.index((part, 0)) * 16 + ROW_SQ + g, ROW_ONE] = 1
            s[g, PARTS.index((0, part)) * 16 + ROW_ONE, part * 16 + ROW_SQ + g] = 1
    return s


def dot(a, b):
    return lax.dot_general(a, b, (((1,), (0,)), ((), ())), preferred_element_type=F32)


def dot_t(a, b):
    return lax.dot_general(a, b, (((1,), (1,)), ((), ())), preferred_element_type=F32)


def sorted_four(a, b, c, d):
    lo, hi = jnp.minimum, jnp.maximum
    a, b, c, d = lo(a, b), hi(a, b), lo(c, d), hi(c, d)
    a, c, b, d = lo(a, c), hi(a, c), lo(b, d), hi(b, d)
    return (a, lo(b, c), hi(b, c), d)


def moved_ids(move_src):
    ids = [move_src[0, 0, d, m] for d in range(2) for m in range(2)]
    return sorted_four(*[jnp.where(i >= 0, i, 99) for i in ids])


def tile_index(i, j):
    if 0 <= i < CW and 0 <= j < CN:
        return i * CN + j
    if 0 <= j < CN:
        return (16 if i < 0 else 20) + j
    if 0 <= i < CW:
        return (24 if j < 0 else 28) + i
    return 32 + 2 * (i > 0) + (j > 0)


def step_kernel(
    wide_size, narrow_size,
    ref_hbm, disp_hbm, vel_hbm, acc_hbm, critical_hbm, active_hbm, partners_hbm, src_hbm, dst_hbm, pairs_hbm, history,
    hist_rows, state_rows,
    held, ref_local, displacement, velocity, acceleration, critical, active, partners, move_src, move_dst, pairs, where_is,
    plain, table, leaving, split, left, forms, apart,
    small_sem, load_sem, halo_send, halo_recv, hist_send, hist_recv, state_send, state_recv,
):
    me_w, me_n = lax.axis_index("wide"), lax.axis_index("narrow")
    small = [
        pltpu.make_async_copy(source, target, small_sem.at[n])
        for n, (source, target) in enumerate((
            (ref_hbm, ref_local), (disp_hbm, displacement), (vel_hbm, velocity), (acc_hbm, acceleration),
            (pairs_hbm, pairs), (critical_hbm, critical), (active_hbm, active), (partners_hbm, partners),
            (src_hbm, move_src), (dst_hbm, move_dst),
        ))
    ]
    for copy in small:
        copy.start()
    loads = [pltpu.make_async_copy(history.at[c], held.at[c], load_sem.at[c]) for c in range(CLUSTERS)]
    for copy in loads:
        copy.start()

    def device(dw, dn):
        return (lax.rem(me_w + dw + wide_size, wide_size), lax.rem(me_n + dn + narrow_size, narrow_size))

    barrier = pltpu.get_barrier_semaphore()
    for dw, dn in SIDES:
        pl.semaphore_signal(barrier, inc=1, device_id=device(dw, dn), device_id_type=MESH)

    sub = lax.broadcasted_iota(jnp.int32, (POINTS, POINTS), 0)
    lane = lax.broadcasted_iota(jnp.int32, (POINTS, POINTS), 1)
    apart[...] = jnp.where(sub == lane, APART, 0.0).astype(F32)
    eye = jnp.where(sub == lane, 1.0, 0.0).astype(BF16)
    far_row = lax.broadcasted_iota(jnp.int32, (48, POINTS), 0)
    far = jnp.where((far_row == ROW_R) | (far_row == ROW_Y), FAR, 0.0)
    far = jnp.where(far_row == ROW_SQ, FAR * FAR, far)
    far = jnp.where(far_row == ROW_ONE, 1.0, far)
    split[TILES] = far.astype(BF16)
    for i in range(CW + 2):
        for j in range(CN + 2):
            where_is[i * (CN + 2) + j] = tile_index(i - 1, j - 1)

    for copy in small[:4]:
        copy.wait()
    column = lax.broadcasted_iota(jnp.int32, (CN, POINTS), 0)
    anchor_n = column.astype(F32) * CELL_SPAN - CELL_SPAN * CN / 2
    hop_n = jnp.where(column == 0, CELL_SPAN * CN, jnp.where(column == CN - 1, -CELL_SPAN * CN, 0.0))

    def fill(target, spots, a, up_w, up_n, fields):
        base, u, v = fields
        r = [base[0] + (CELL_SPAN * (a - CW / 2) + up_w), base[1] + (anchor_n + up_n), base[2] - CELL_SPAN]
        y = [r[d] + u[d] for d in range(3)]
        squares = [
            r[0] * r[0] + r[1] * r[1] + r[2] * r[2],
            u[0] * (r[0] + y[0]) + u[1] * (r[1] + y[1]) + u[2] * (r[2] + y[2]),
            v[0] * y[0] + v[1] * y[1] + v[2] * y[2],
        ]
        rows = r + u + v + y + squares + [jnp.ones_like(u[0])]
        for b, spot in spots:
            for f, row in enumerate(rows):
                target[spot, f:f + 1] = row[b:b + 1]

    for a in range(CW):
        base, u, v = [], [], []
        for d in range(3):
            ref = ref_local[d, a]
            speed = velocity[d, a]
            push = acceleration[d, a]
            move = displacement[d, a] + TIME_STEP * speed + 0.5 * TIME_STEP * TIME_STEP * push
            half = speed + 0.5 * TIME_STEP * push
            base.append(ref)
            u.append(move)
            v.append(half * (DAMPING / STIFFNESS))
            for b in range(CN):
                for f, row in ((d, ref), (3 + d, move), (6 + d, half)):
                    plain[a * CN + b, f:f + 1] = row[b:b + 1]
        fields = (base, u, v)
        fill(table, [(b, a * CN + b) for b in range(CN)], a, 0.0, 0.0, fields)
        fill(leaving, [(0, 24 + a - 16), (CN - 1, 28 + a - 16)], a, 0.0, hop_n, fields)
        if a in (0, CW - 1):
            hop_w = CELL_SPAN * CW if a == 0 else -CELL_SPAN * CW
            at = 0 if a == 0 else 4
            fill(leaving, [(b, at + b) for b in range(CN)], a, hop_w, 0.0, fields)
            at = 16 if a == 0 else 18
            fill(leaving, [(0, at), (CN - 1, at + 1)], a, hop_w, hop_n, fields)

    pl.semaphore_wait(barrier, len(SIDES))
    halos = []
    for n, (dw, dn) in enumerate(SIDES):
        landing = SIDE_AT[SIDES.index((-dw, -dn))]
        halos.append(pltpu.make_async_remote_copy(
            src_ref=leaving.at[pl.ds(SIDE_AT[n] - CLUSTERS, SIDE_COUNT[n])],
            dst_ref=table.at[pl.ds(landing, SIDE_COUNT[n])],
            send_sem=halo_send.at[n], recv_sem=halo_recv.at[n],
            device_id=device(dw, dn), device_id_type=MESH,
        ))
    for copy in halos:
        copy.start()

    def split_tile(t, carry):
        tile = table[t]
        high = tile.astype(BF16)
        rest = tile - high.astype(F32)
        middle = rest.astype(BF16)
        split[t, 0:16] = high
        split[t, 16:32] = middle
        split[t, 32:48] = (rest - middle.astype(F32)).astype(BF16)
        return carry

    lax.fori_loop(0, CLUSTERS, split_tile, 0)
    for copy in small[4:]:
        copy.wait()

    def left_side(c, carry):
        for g in range(3):
            rows = dot(pairs[g], split[c]).astype(BF16)
            left[c, g * POINTS:(g + 1) * POINTS, :] = dot_t(eye, rows).astype(BF16)
        return carry

    lax.fori_loop(0, CLUSTERS, left_side, 0)
    for copy in loads:
        copy.wait()
    for copy in halos:
        copy.wait()
    lax.fori_loop(CLUSTERS, TILES, split_tile, 0)

    def cluster(c, out):
        a, b = c // CN, lax.rem(c, CN)
        mine = left[c]
        tiles, inverse = [], []
        for k in range(SLOTS):
            o = partners[a, b, k]
            dw, dn = o // 3 - 1, lax.rem(o, 3) - 1
            gw, gn = me_w * CW + a + dw, me_n * CN + b + dn
            inside = (gw >= 0) & (gw < wide_size * CW) & (gn >= 0) & (gn < narrow_size * CN)
            on = inside & (active[a, b, k] > 0)
            spot = where_is[(a + 1 + dw) * (CN + 2) + b + 1 + dn]
            tiles.append(jnp.where(on, spot, TILES))
            inverse.append(jnp.where(on, 1.0, 0.0) / jnp.full((1, POINTS), critical[a, b, k], F32))
        for pair in range(SLOTS // 2):
            theirs = []
            for k in (2 * pair, 2 * pair + 1):
                tile = split[tiles[k]]
                theirs.append(jnp.concatenate([tile[q * 16:q * 16 + 16] for q, _ in PARTS], 0))
            forms[pair] = dot(mine, jnp.concatenate(theirs, 1))
        sums = None
        for k in range(SLOTS):
            pair, at = k // 2, pl.ds((k % 2) * POINTS, POINTS)
            rest_sq = forms[pair, 0:POINTS, at]
            if k == 0:
                rest_sq = rest_sq + apart[...]
            now_sq = jnp.maximum(rest_sq + forms[pair, POINTS:2 * POINTS, at], TINY)
            rate = forms[pair, 2 * POINTS:3 * POINTS, at]
            rest_inv = lax.rsqrt(rest_sq)
            now_inv = lax.rsqrt(now_sq)
            stretch = now_sq * now_inv * rest_inv - 1.0
            scaled = stretch * inverse[k]
            if k == 0:
                scaled = scaled - apart[...]
            hist = jnp.maximum(held[c, k], scaled)
            hist_rows[out, k] = hist
            weight = jnp.exp2(rest_sq * FALLOFF) * jnp.minimum(jnp.maximum(2.0 - hist, 0.0), 1.0)
            factor = weight * (stretch + rate * now_inv) * now_inv
            high = factor.astype(BF16)
            low = (factor - high.astype(F32)).astype(BF16)
            tile = split[tiles[k]]
            term = dot_t(jnp.concatenate([high, low], 1), jnp.concatenate([tile, tile], 1))
            sums = term if sums is None else sums + term
        sums = jnp.transpose(sums)
        sums = sums[0:16] + sums[16:32] + sums[32:48]
        here = table[c]
        own = plain[c]
        acc = STIFFNESS * (sums[ROW_Y:ROW_Y + 3] - here[ROW_Y:ROW_Y + 3] * sums[ROW_ONE:ROW_ONE + 1])
        state_rows[out, 0:6] = own[0:6]
        state_rows[out, 6:9] = own[6:9] + 0.5 * TIME_STEP * acc
        state_rows[out, 9:12] = acc

    def hist_copy(e):
        return pltpu.make_async_remote_copy(
            src_ref=hist_rows.at[STAYS + 4 + e], dst_ref=hist_rows.at[STAYS + e],
            send_sem=hist_send.at[e], recv_sem=hist_recv.at[e],
            device_id=device(1 - 2 * lax.rem(e, 2), 0), device_id_type=MESH,
        )

    def state_copy(e):
        return pltpu.make_async_remote_copy(
            src_ref=state_rows.at[STAYS + 4 + e], dst_ref=state_rows.at[STAYS + e],
            send_sem=state_send.at[e], recv_sem=state_recv.at[e],
            device_id=device(1 - 2 * lax.rem(e, 2), 0), device_id_type=MESH,
        )

    def hand_on(e, carry):
        d, m = lax.rem(e, 2), e // 2
        cluster(jnp.maximum(move_src[0, 0, d, m], 0), STAYS + 4 + e)
        hist_copy(e).start()
        tag = jnp.full((4, POINTS), move_dst[0, 0, d, m], jnp.int32).astype(F32)
        state_rows[STAYS + 4 + e, 12:16] = tag
        state_copy(e).start()
        return carry

    lax.fori_loop(0, 4, hand_on, 0)

    moved = moved_ids(move_src)

    def stay(j, carry):
        c = j
        for m in moved:
            c = jnp.where(m <= c, c + 1, c)
        cluster(jnp.minimum(c, CLUSTERS - 1), j)
        state_rows[j, 12:16] = jnp.zeros((4, POINTS), F32)
        return carry

    lax.fori_loop(0, jnp.where((me_w == 0) | (me_w == wide_size - 1), STAYS, STAYS - 1), stay, 0)

    for e in range(4):
        hist_copy(e).wait()
        state_copy(e).wait()


def place_kernel(hist_rows, state_rows, src_hbm, ref_out, disp_out, vel_out, acc_out, hist_out, move_src, src_sem, sem):
    ids = pltpu.make_async_copy(src_hbm, move_src, src_sem)
    ids.start()
    tags = [jnp.max(state_rows[STAYS + e, 12:13, :]).astype(jnp.int32) for e in range(4)]
    ids.wait()
    moved = moved_ids(move_src)
    copies = []
    for o in range(CLUSTERS):
        source = o
        for m in moved:
            source = jnp.where(m < o, source - 1, source)
        for e in range(4):
            source = jnp.where(tags[e] == o, STAYS + e, source)
        copies.append(pltpu.make_async_copy(hist_rows.at[source], hist_out.at[o], sem.at[o]))
        copies[-1].start()
        rows = state_rows[source]
        for f, ref in enumerate((ref_out, disp_out, vel_out, acc_out)):
            for d in range(3):
                ref[d, o // CN, o % CN:o % CN + 1] = rows[3 * f + d:3 * f + d + 1]
    for copy in copies:
        copy.wait()


def per_device(
    wide_size, narrow_size,
    ref_local, displacement, velocity, acceleration, history, critical, active, partners, move_src, move_dst,
):
    vmem, anywhere = (pl.BlockSpec(memory_space=m) for m in (pltpu.VMEM, pl.ANY))
    total = STAYS + 8
    hist_shape, state_shape = (total, SLOTS, POINTS, POINTS), (total, 16, POINTS)
    operands = [
        ref_local, displacement, velocity, acceleration, critical, active, partners, move_src, move_dst,
        jnp.asarray(pairing(), BF16), history.reshape(CLUSTERS, SLOTS, POINTS, POINTS),
    ]
    operands = [pltpu.with_memory_space_constraint(x, pltpu.HBM) for x in operands]
    hist_rows, state_rows = pl.pallas_call(
        functools.partial(step_kernel, wide_size, narrow_size),
        out_shape=(pltpu.VMEM(hist_shape, F32), pltpu.VMEM(state_shape, F32)),
        in_specs=[anywhere] * len(operands),
        out_specs=(vmem, vmem),
        scratch_shapes=[
            pltpu.VMEM((CLUSTERS, SLOTS, POINTS, POINTS), F32),
            *[pltpu.VMEM(ref_local.shape, F32)] * 4,
            pltpu.SMEM(critical.shape, F32),
            pltpu.SMEM(active.shape, jnp.int32),
            pltpu.SMEM(partners.shape, jnp.int32),
            pltpu.SMEM(move_src.shape, jnp.int32),
            pltpu.SMEM(move_dst.shape, jnp.int32),
            pltpu.VMEM((3, 96, 48), BF16),
            pltpu.SMEM(((CW + 2) * (CN + 2),), jnp.int32),
            pltpu.VMEM((CLUSTERS, 16, POINTS), F32),
            pltpu.VMEM((TILES, 16, POINTS), F32),
            pltpu.VMEM((TILES - CLUSTERS, 16, POINTS), F32),
            pltpu.VMEM((TILES + 1, 48, POINTS), BF16),
            pltpu.VMEM((CLUSTERS, 3 * POINTS, 96), BF16),
            pltpu.VMEM((SLOTS // 2, 3 * POINTS, 2 * POINTS), F32),
            pltpu.VMEM((POINTS, POINTS), F32),
            pltpu.SemaphoreType.DMA((10,)),
            pltpu.SemaphoreType.DMA((CLUSTERS,)),
            pltpu.SemaphoreType.DMA((8,)),
            pltpu.SemaphoreType.DMA((8,)),
            pltpu.SemaphoreType.DMA((4,)),
            pltpu.SemaphoreType.DMA((4,)),
            pltpu.SemaphoreType.DMA((4,)),
            pltpu.SemaphoreType.DMA((4,)),
        ],
        compiler_params=pltpu.CompilerParams(
            collective_id=0, has_side_effects=True, vmem_limit_bytes=20 << 20
        ),
        name="step",
    )(*operands)
    hist_rows = pltpu.with_memory_space_constraint(hist_rows, pltpu.VMEM)
    state_rows = pltpu.with_memory_space_constraint(state_rows, pltpu.VMEM)
    state = jax.ShapeDtypeStruct(ref_local.shape, F32)
    outs = pl.pallas_call(
        place_kernel,
        out_shape=(state,) * 4 + (jax.ShapeDtypeStruct((CLUSTERS, SLOTS, POINTS, POINTS), F32),),
        in_specs=[anywhere, vmem, anywhere],
        out_specs=(vmem,) * 4 + (anywhere,),
        scratch_shapes=[
            pltpu.SMEM(move_src.shape, jnp.int32),
            pltpu.SemaphoreType.DMA,
            pltpu.SemaphoreType.DMA((CLUSTERS,)),
        ],
        compiler_params=pltpu.CompilerParams(vmem_limit_bytes=8 << 20),
        name="place",
    )(hist_rows, state_rows, pltpu.with_memory_space_constraint(move_src, pltpu.HBM))
    return outs[:4] + (outs[4].reshape(history.shape),)


def solution(mesh):
    field = P(None, "wide", "narrow", None)
    blocks = P("wide", "narrow", None)
    hist = P("wide", "narrow", None, None, None)
    moves = P("wide", "narrow", None, None)
    return jax.shard_map(
        functools.partial(per_device, mesh.shape["wide"], mesh.shape["narrow"]),
        mesh=mesh,
        in_specs=(field,) * 4 + (hist,) + (blocks,) * 3 + (moves,) * 2,
        out_specs=(field,) * 4 + (hist,),
        check_vma=False,
    )
```

```python
import functools

import jax
import jax.numpy as jnp
import numpy as np
from jax import lax
from jax.experimental import pallas as pl
from jax.experimental.pallas import tpu as pltpu
from jax.sharding import PartitionSpec as P

STIFFNESS = 8.0
DAMPING = 0.8
TIME_STEP = 0.1
CELL_SPAN = 4.0
FALLOFF = float(-np.log2(np.e) / 9.0)
FAR = 1024.0
APART = 1.0e6
TINY = 1.0e-12

F32 = jnp.float32
BF16 = jnp.bfloat16
MESH = pl.DeviceIdType.MESH
CW = CN = 4
CLUSTERS = CW * CN
SLOTS = 6
POINTS = 128
STAYS = 15
TILES = CLUSTERS + 22
SIDES = ((-1, 0), (1, 0), (0, -1), (0, 1), (-1, -1), (-1, 1), (1, -1), (1, 1))
SIDE_AT = (16, 21, 26, 30, 34, 35, 36, 37)
SIDE_COUNT = (5, 5, 4, 4, 1, 1, 1, 1)
TAGS_AT = (20, 25)

ROW_R, ROW_U, ROW_V, ROW_Y, ROW_SQ, ROW_ONE = 0, 3, 6, 9, 12, 15
PARTS = ((0, 0), (1, 0), (0, 1), (1, 1), (2, 0), (0, 2))


def pairing():
    s = np.zeros((3, 96, 48), np.float32)
    for block, (q, p) in enumerate(PARTS):
        for d in range(3):
            s[0, block * 16 + ROW_R + d, p * 16 + ROW_R + d] = -2
            s[1, block * 16 + ROW_U + d, p * 16 + ROW_Y + d] = -2
            s[1, block * 16 + ROW_R + d, p * 16 + ROW_U + d] = -2
            s[2, block * 16 + ROW_Y + d, p * 16 + ROW_V + d] = -1
            s[2, block * 16 + ROW_V + d, p * 16 + ROW_Y + d] = -1
    for g in range(3):
        for part in range(3):
            s[g, PARTS.index((part, 0)) * 16 + ROW_SQ + g, ROW_ONE] = 1
            s[g, PARTS.index((0, part)) * 16 + ROW_ONE, part * 16 + ROW_SQ + g] = 1
    return s


def around(i, size):
    i = jnp.where(i < 0, i + size, i)
    return jnp.where(i >= size, i - size, i)


def dot(a, b):
    return lax.dot_general(a, b, (((1,), (0,)), ((), ())), preferred_element_type=F32)


def dot_t(a, b):
    return lax.dot_general(a, b, (((1,), (1,)), ((), ())), preferred_element_type=F32)


def sorted_four(a, b, c, d):
    lo, hi = jnp.minimum, jnp.maximum
    a, b, c, d = lo(a, b), hi(a, b), lo(c, d), hi(c, d)
    a, c, b, d = lo(a, c), hi(a, c), lo(b, d), hi(b, d)
    return (a, lo(b, c), hi(b, c), d)


def moved_ids(move_src):
    ids = [move_src[0, 0, d, m] for d in range(2) for m in range(2)]
    return sorted_four(*[jnp.where(i >= 0, i, 99) for i in ids])


def tile_index(i, j):
    if 0 <= i < CW and 0 <= j < CN:
        return i * CN + j
    if 0 <= j < CN:
        return (16 if i < 0 else 21) + j
    if 0 <= i < CW:
        return (26 if j < 0 else 30) + i
    return 34 + 2 * (i > 0) + (j > 0)


def step_kernel(
    wide_size, narrow_size,
    ref_hbm, disp_hbm, vel_hbm, acc_hbm, critical_hbm, active_hbm, partners_hbm, src_hbm, dst_hbm, pairs_hbm, history,
    hist_rows, state_rows, sources,
    held, ref_local, displacement, velocity, acceleration, critical, active, partners, move_src, move_dst, pairs, where_is,
    plain, table, leaving, split, left, forms, apart, tags,
    small_sem, tag_sem, load_sem, halo_send, halo_recv, hist_send, hist_recv, state_send, state_recv,
):
    me_w, me_n = lax.axis_index("wide"), lax.axis_index("narrow")
    small = [
        pltpu.make_async_copy(source, target, small_sem.at[n])
        for n, (source, target) in enumerate((
            (ref_hbm, ref_local), (disp_hbm, displacement), (vel_hbm, velocity), (acc_hbm, acceleration),
            (dst_hbm, move_dst), (pairs_hbm, pairs), (critical_hbm, critical), (active_hbm, active), (partners_hbm, partners),
            (src_hbm, move_src),
        ))
    ]
    for copy in small:
        copy.start()
    loads = [pltpu.make_async_copy(history.at[c], held.at[c], load_sem.at[c]) for c in range(CLUSTERS)]
    for copy in loads:
        copy.start()

    def device(dw, dn):
        return (around(me_w + dw, wide_size), around(me_n + dn, narrow_size))

    barrier = pltpu.get_barrier_semaphore()
    for dw, dn in SIDES:
        pl.semaphore_signal(barrier, inc=1, device_id=device(dw, dn), device_id_type=MESH)

    sub = lax.broadcasted_iota(jnp.int32, (POINTS, POINTS), 0)
    lane = lax.broadcasted_iota(jnp.int32, (POINTS, POINTS), 1)
    apart[...] = jnp.where(sub == lane, APART, 0.0).astype(F32)
    eye = jnp.where(sub == lane, 1.0, 0.0).astype(BF16)
    far_row = lax.broadcasted_iota(jnp.int32, (48, POINTS), 0)
    far = jnp.where((far_row == ROW_R) | (far_row == ROW_Y), FAR, 0.0)
    far = jnp.where(far_row == ROW_SQ, FAR * FAR, far)
    far = jnp.where(far_row == ROW_ONE, 1.0, far)
    split[TILES] = far.astype(BF16)
    for i in range(CW + 2):
        for j in range(CN + 2):
            where_is[i * (CN + 2) + j] = tile_index(i - 1, j - 1)

    for copy in small[:5]:
        copy.wait()
    column = lax.broadcasted_iota(jnp.int32, (CN, POINTS), 0)
    anchor_n = column.astype(F32) * CELL_SPAN - CELL_SPAN * CN / 2
    hop_n = jnp.where(column == 0, CELL_SPAN * CN, jnp.where(column == CN - 1, -CELL_SPAN * CN, 0.0))

    def advanced(a):
        base, u, half, v = [], [], [], []
        for d in range(3):
            speed, push = velocity[d, a], acceleration[d, a]
            base.append(ref_local[d, a])
            u.append(displacement[d, a] + TIME_STEP * speed + 0.5 * TIME_STEP * TIME_STEP * push)
            half.append(speed + 0.5 * TIME_STEP * push)
            v.append(half[d] * (DAMPING / STIFFNESS))
        return base, u, half, v

    def tile_rows(a, up_w, up_n, base, u, v):
        r = [base[0] + (CELL_SPAN * (a - CW / 2) + up_w), base[1] + (anchor_n + up_n), base[2] - CELL_SPAN]
        y = [r[d] + u[d] for d in range(3)]
        squares = [
            r[0] * r[0] + r[1] * r[1] + r[2] * r[2],
            u[0] * (r[0] + y[0]) + u[1] * (r[1] + y[1]) + u[2] * (r[2] + y[2]),
            v[0] * y[0] + v[1] * y[1] + v[2] * y[2],
        ]
        return r + u + v + y + squares + [jnp.ones_like(u[0])]

    for a in range(CW):
        base, u, half, v = advanced(a)
        for f, row in enumerate(tile_rows(a, 0.0, hop_n, base, u, v)):
            leaving[SIDE_AT[2] - CLUSTERS + a, f:f + 1] = row[0:1]
            leaving[SIDE_AT[3] - CLUSTERS + a, f:f + 1] = row[CN - 1:CN]
        if a in (0, CW - 1):
            side, hop_w = (0, CELL_SPAN * CW) if a == 0 else (1, -CELL_SPAN * CW)
            at = SIDE_AT[side] - CLUSTERS
            for f, row in enumerate(tile_rows(a, hop_w, 0.0, base, u, v)):
                leaving[at:at + CN, f] = row
            at = SIDE_AT[4 + 2 * side] - CLUSTERS
            for f, row in enumerate(tile_rows(a, hop_w, hop_n, base, u, v)):
                leaving[at, f:f + 1] = row[0:1]
                leaving[at + 1, f:f + 1] = row[CN - 1:CN]
    for side in range(2):
        for m in range(2):
            tag = jnp.full((8, POINTS), move_dst[0, 0, 1 - side, m], jnp.int32).astype(F32)
            leaving[TAGS_AT[side] - CLUSTERS, 8 * m:8 * m + 8] = tag

    pl.semaphore_wait(barrier, len(SIDES))
    halos = []
    for n, (dw, dn) in enumerate(SIDES):
        landing = SIDE_AT[SIDES.index((-dw, -dn))]
        halos.append(pltpu.make_async_remote_copy(
            src_ref=leaving.at[pl.ds(SIDE_AT[n] - CLUSTERS, SIDE_COUNT[n])],
            dst_ref=table.at[pl.ds(landing, SIDE_COUNT[n])],
            send_sem=halo_send.at[n], recv_sem=halo_recv.at[n],
            device_id=device(dw, dn), device_id_type=MESH,
        ))
    for copy in halos:
        copy.start()

    for a in range(CW):
        base, u, half, v = advanced(a)
        here = pl.ds(a * CN, CN)
        for f, row in enumerate(base + u + half):
            plain[here, f] = row
        for f in range(9, 16):
            plain[here, f] = jnp.zeros((CN, POINTS), F32)
        for f, row in enumerate(tile_rows(a, 0.0, 0.0, base, u, v)):
            table[here, f] = row

    def split_tile(t, carry):
        tile = table[t]
        high = tile.astype(BF16)
        rest = tile - high.astype(F32)
        middle = rest.astype(BF16)
        split[t, 0:16] = high
        split[t, 16:32] = middle
        split[t, 32:48] = (rest - middle.astype(F32)).astype(BF16)
        return carry

    lax.fori_loop(0, CLUSTERS, split_tile, 0, unroll=4)
    for copy in small[5:]:
        copy.wait()

    def left_side(c, carry):
        for g in range(3):
            rows = dot(pairs[g], split[c]).astype(BF16)
            left[c, g * POINTS:(g + 1) * POINTS, :] = dot_t(eye, rows).astype(BF16)
        return carry

    lax.fori_loop(0, CLUSTERS, left_side, 0, unroll=4)
    for copy in loads:
        copy.wait()
    for copy in halos:
        copy.wait()
    tag_copies = [
        pltpu.make_async_copy(table.at[TAGS_AT[side]], tags.at[side], tag_sem.at[side]) for side in range(2)
    ]
    for copy in tag_copies:
        copy.start()
    lax.fori_loop(CLUSTERS, TILES, split_tile, 0, unroll=2)

    def cluster(c, out):
        a, b = c // CN, lax.rem(c, CN)
        mine = left[c]
        tiles, inverse = [], []
        for k in range(SLOTS):
            o = partners[a, b, k]
            dw, dn = o // 3 - 1, lax.rem(o, 3) - 1
            gw, gn = me_w * CW + a + dw, me_n * CN + b + dn
            inside = (gw >= 0) & (gw < wide_size * CW) & (gn >= 0) & (gn < narrow_size * CN)
            on = inside & (active[a, b, k] > 0)
            spot = where_is[(a + 1 + dw) * (CN + 2) + b + 1 + dn]
            tiles.append(jnp.where(on, spot, TILES))
            inverse.append(jnp.where(on, 1.0, 0.0) / jnp.full((1, POINTS), critical[a, b, k], F32))
        for pair in range(SLOTS // 2):
            theirs = []
            for k in (2 * pair, 2 * pair + 1):
                tile = split[tiles[k]]
                theirs.append(jnp.concatenate([tile[q * 16:q * 16 + 16] for q, _ in PARTS], 0))
            forms[pair] = dot(mine, jnp.concatenate(theirs, 1))
        sums = None
        for k in range(SLOTS):
            pair, at = k // 2, pl.ds((k % 2) * POINTS, POINTS)
            rest_sq = forms[pair, 0:POINTS, at]
            if k == 0:
                rest_sq = rest_sq + apart[...]
            now_sq = jnp.maximum(rest_sq + forms[pair, POINTS:2 * POINTS, at], TINY)
            rate = forms[pair, 2 * POINTS:3 * POINTS, at]
            rest_inv = lax.rsqrt(rest_sq)
            now_inv = lax.rsqrt(now_sq)
            stretch = now_sq * now_inv * rest_inv - 1.0
            scaled = stretch * inverse[k]
            if k == 0:
                scaled = scaled - apart[...]
            hist = jnp.maximum(held[c, k], scaled)
            hist_rows[out, k] = hist
            weight = jnp.exp2(rest_sq * FALLOFF) * jnp.minimum(jnp.maximum(2.0 - hist, 0.0), 1.0)
            factor = weight * (stretch + rate * now_inv) * now_inv
            high = factor.astype(BF16)
            low = (factor - high.astype(F32)).astype(BF16)
            tile = split[tiles[k]]
            term = dot_t(jnp.concatenate([high, low], 1), jnp.concatenate([tile, tile], 1))
            sums = term if sums is None else sums + term
        sums = jnp.transpose(sums)
        sums = sums[0:16] + sums[16:32] + sums[32:48]
        here = table[c]
        own = plain[c]
        acc = STIFFNESS * (sums[ROW_Y:ROW_Y + 3] - here[ROW_Y:ROW_Y + 3] * sums[ROW_ONE:ROW_ONE + 1])
        state_rows[out, 0:6] = own[0:6]
        state_rows[out, 6:9] = own[6:9] + 0.5 * TIME_STEP * acc
        state_rows[out, 9:12] = acc
        state_rows[out, 12:16] = own[12:16]

    def hist_copy(e):
        return pltpu.make_async_remote_copy(
            src_ref=hist_rows.at[STAYS + 4 + e], dst_ref=hist_rows.at[STAYS + e],
            send_sem=hist_send.at[e], recv_sem=hist_recv.at[e],
            device_id=device(1 - 2 * lax.rem(e, 2), 0), device_id_type=MESH,
        )

    def state_copy(e):
        return pltpu.make_async_remote_copy(
            src_ref=state_rows.at[STAYS + 4 + e], dst_ref=state_rows.at[STAYS + e],
            send_sem=state_send.at[e], recv_sem=state_recv.at[e],
            device_id=device(1 - 2 * lax.rem(e, 2), 0), device_id_type=MESH,
        )

    def hand_on(e, carry):
        d, m = lax.rem(e, 2), e // 2
        cluster(jnp.maximum(move_src[0, 0, d, m], 0), STAYS + 4 + e)
        hist_copy(e).start()
        state_copy(e).start()
        return carry

    lax.fori_loop(0, 4, hand_on, 0)

    moved = moved_ids(move_src)

    def stay(j, carry):
        c = j
        for m in moved:
            c = jnp.where(m <= c, c + 1, c)
        cluster(jnp.minimum(c, CLUSTERS - 1), j)
        return carry

    lax.fori_loop(0, jnp.where((me_w == 0) | (me_w == wide_size - 1), STAYS, STAYS - 1), stay, 0)

    for copy in tag_copies:
        copy.wait()
    for o in range(CLUSTERS):
        source = o
        for m in moved:
            source = jnp.where(m < o, source - 1, source)
        for e in range(4):
            source = jnp.where(tags[e % 2, 8 * (e // 2), 0] == float(o), STAYS + e, source)
        sources[o] = source

    for e in range(4):
        hist_copy(e).wait()
        state_copy(e).wait()


def place_kernel(hist_rows, state_rows, sources, ref_out, disp_out, vel_out, acc_out, hist_out, states, state_sem, sem):
    copies = []
    for o in range(CLUSTERS):
        copies.append(pltpu.make_async_copy(hist_rows.at[sources[o]], hist_out.at[o], sem.at[o]))
        copies[-1].start()
    for o in range(CLUSTERS):
        rows = state_rows[sources[o]]
        for f in range(4):
            for d in range(3):
                states[f, d, o // CN, o % CN:o % CN + 1] = rows[3 * f + d:3 * f + d + 1]
    for f, ref in enumerate((ref_out, disp_out, vel_out, acc_out)):
        copies.append(pltpu.make_async_copy(states.at[f], ref, state_sem.at[f]))
        copies[-1].start()
    for copy in copies:
        copy.wait()


def per_device(
    wide_size, narrow_size,
    ref_local, displacement, velocity, acceleration, history, critical, active, partners, move_src, move_dst,
):
    vmem, smem, anywhere = (pl.BlockSpec(memory_space=m) for m in (pltpu.VMEM, pltpu.SMEM, pl.ANY))
    total = STAYS + 8
    hist_shape, state_shape = (total, SLOTS, POINTS, POINTS), (total, 16, POINTS)
    operands = [
        ref_local, displacement, velocity, acceleration, critical, active, partners, move_src, move_dst,
        jnp.asarray(pairing(), BF16), history.reshape(CLUSTERS, SLOTS, POINTS, POINTS),
    ]
    operands = [pltpu.with_memory_space_constraint(x, pltpu.HBM) for x in operands]
    hist_rows, state_rows, sources = pl.pallas_call(
        functools.partial(step_kernel, wide_size, narrow_size),
        out_shape=(pltpu.VMEM(hist_shape, F32), pltpu.VMEM(state_shape, F32), pltpu.SMEM((CLUSTERS,), jnp.int32)),
        in_specs=[anywhere] * len(operands),
        out_specs=(vmem, vmem, smem),
        scratch_shapes=[
            pltpu.VMEM((CLUSTERS, SLOTS, POINTS, POINTS), F32),
            *[pltpu.VMEM(ref_local.shape, F32)] * 4,
            pltpu.SMEM(critical.shape, F32),
            pltpu.SMEM(active.shape, jnp.int32),
            pltpu.SMEM(partners.shape, jnp.int32),
            pltpu.SMEM(move_src.shape, jnp.int32),
            pltpu.SMEM(move_dst.shape, jnp.int32),
            pltpu.VMEM((3, 96, 48), BF16),
            pltpu.SMEM(((CW + 2) * (CN + 2),), jnp.int32),
            pltpu.VMEM((CLUSTERS, 16, POINTS), F32),
            pltpu.VMEM((TILES, 16, POINTS), F32),
            pltpu.VMEM((TILES - CLUSTERS, 16, POINTS), F32),
            pltpu.VMEM((TILES + 1, 48, POINTS), BF16),
            pltpu.VMEM((CLUSTERS, 3 * POINTS, 96), BF16),
            pltpu.VMEM((SLOTS // 2, 3 * POINTS, 2 * POINTS), F32),
            pltpu.VMEM((POINTS, POINTS), F32),
            pltpu.SMEM((2, 16, POINTS), F32),
            pltpu.SemaphoreType.DMA((10,)),
            pltpu.SemaphoreType.DMA((2,)),
            pltpu.SemaphoreType.DMA((CLUSTERS,)),
            pltpu.SemaphoreType.DMA((8,)),
            pltpu.SemaphoreType.DMA((8,)),
            pltpu.SemaphoreType.DMA((4,)),
            pltpu.SemaphoreType.DMA((4,)),
            pltpu.SemaphoreType.DMA((4,)),
            pltpu.SemaphoreType.DMA((4,)),
        ],
        compiler_params=pltpu.CompilerParams(
            collective_id=0, has_side_effects=True, vmem_limit_bytes=20 << 20
        ),
        name="step",
    )(*operands)
    hist_rows = pltpu.with_memory_space_constraint(hist_rows, pltpu.VMEM)
    state_rows = pltpu.with_memory_space_constraint(state_rows, pltpu.VMEM)
    sources = pltpu.with_memory_space_constraint(sources, pltpu.SMEM)
    state = jax.ShapeDtypeStruct(ref_local.shape, F32)
    outs = pl.pallas_call(
        place_kernel,
        out_shape=(state,) * 4 + (jax.ShapeDtypeStruct((CLUSTERS, SLOTS, POINTS, POINTS), F32),),
        in_specs=[anywhere, vmem, smem],
        out_specs=(anywhere,) * 5,
        scratch_shapes=[
            pltpu.VMEM((4,) + ref_local.shape, F32),
            pltpu.SemaphoreType.DMA((4,)),
            pltpu.SemaphoreType.DMA((CLUSTERS,)),
        ],
        compiler_params=pltpu.CompilerParams(vmem_limit_bytes=8 << 20),
        name="place",
    )(hist_rows, state_rows, sources)
    return outs[:4] + (outs[4].reshape(history.shape),)


def solution(mesh):
    field = P(None, "wide", "narrow", None)
    blocks = P("wide", "narrow", None)
    hist = P("wide", "narrow", None, None, None)
    moves = P("wide", "narrow", None, None)
    return jax.shard_map(
        functools.partial(per_device, mesh.shape["wide"], mesh.shape["narrow"]),
        mesh=mesh,
        in_specs=(field,) * 4 + (hist,) + (blocks,) * 3 + (moves,) * 2,
        out_specs=(field,) * 4 + (hist,),
        check_vma=False,
    )
```

```python
import functools

import jax
import jax.numpy as jnp
import numpy as np
from jax import lax
from jax.experimental import pallas as pl
from jax.experimental.pallas import tpu as pltpu
from jax.sharding import PartitionSpec as P

STIFFNESS = 8.0
DAMPING = 0.8
TIME_STEP = 0.1
CELL_SPAN = 4.0
FALLOFF = float(-np.log2(np.e) / 9.0)
FAR = 1024.0
APART = 1.0e6
TINY = 1.0e-12

F32 = jnp.float32
BF16 = jnp.bfloat16
MESH = pl.DeviceIdType.MESH
CW = CN = 4
CLUSTERS = CW * CN
SLOTS = 6
POINTS = 128
TILES = CLUSTERS + 22
SIDES = ((-1, 0), (1, 0), (0, -1), (0, 1), (-1, -1), (-1, 1), (1, -1), (1, 1))
SIDE_AT = (16, 21, 26, 30, 34, 35, 36, 37)
SIDE_COUNT = (5, 5, 4, 4, 1, 1, 1, 1)
TAGS_AT = (20, 25)

ROW_R, ROW_U, ROW_V, ROW_Y, ROW_SQ, ROW_ONE = 0, 3, 8, 11, (6, 7, 14), 15
PACK_ROWS = 16 + 8 * SLOTS + 8
PARTS = ((0, 0), (1, 0), (0, 1), (1, 1), (2, 0), (0, 2))


def pairing():
    s = np.zeros((3, 96, 48), np.float32)
    for block, (q, p) in enumerate(PARTS):
        for d in range(3):
            s[0, block * 16 + ROW_R + d, p * 16 + ROW_R + d] = -2
            s[1, block * 16 + ROW_U + d, p * 16 + ROW_Y + d] = -2
            s[1, block * 16 + ROW_R + d, p * 16 + ROW_U + d] = -2
            s[2, block * 16 + ROW_Y + d, p * 16 + ROW_V + d] = -1
            s[2, block * 16 + ROW_V + d, p * 16 + ROW_Y + d] = -1
    for g in range(3):
        for part in range(3):
            s[g, PARTS.index((part, 0)) * 16 + ROW_SQ[g], ROW_ONE] = 1
            s[g, PARTS.index((0, part)) * 16 + ROW_ONE, part * 16 + ROW_SQ[g]] = 1
    return s


def around(i, size):
    i = jnp.where(i < 0, i + size, i)
    return jnp.where(i >= size, i - size, i)


def dot(a, b):
    return lax.dot_general(a, b, (((1,), (0,)), ((), ())), preferred_element_type=F32)


def dot_t(a, b):
    return lax.dot_general(a, b, (((1,), (1,)), ((), ())), preferred_element_type=F32)


def tile_index(i, j):
    if 0 <= i < CW and 0 <= j < CN:
        return i * CN + j
    if 0 <= j < CN:
        return (16 if i < 0 else 21) + j
    if 0 <= i < CW:
        return (26 if j < 0 else 30) + i
    return 34 + 2 * (i > 0) + (j > 0)


def step_kernel(
    wide_size, narrow_size,
    ref_hbm, disp_hbm, vel_hbm, acc_hbm, critical_hbm, active_hbm, partners_hbm, src_hbm, dst_hbm, pairs_hbm, history,
    hist_rows, state_rows, state_in, sources,
    held, ref_local, displacement, velocity, acceleration, critical, active, partners, move_src, move_dst, pairs, where_is,
    plain, table, leaving, split, left, forms, apart, tags, raw, pack, packed, sent_state,
    small_sem, tag_sem, load_sem, halo_send, halo_recv, hist_send, hist_recv, pack_send, pack_recv, state_send, state_recv,
):
    me_w, me_n = lax.axis_index("wide"), lax.axis_index("narrow")
    small = [
        pltpu.make_async_copy(source, target, small_sem.at[n])
        for n, (source, target) in enumerate((
            (ref_hbm, ref_local), (disp_hbm, displacement), (vel_hbm, velocity), (acc_hbm, acceleration),
            (dst_hbm, move_dst), (pairs_hbm, pairs), (critical_hbm, critical), (active_hbm, active), (partners_hbm, partners),
            (src_hbm, move_src),
        ))
    ]
    for copy in small:
        copy.start()
    loads = [pltpu.make_async_copy(history.at[c], held.at[c], load_sem.at[c]) for c in range(CLUSTERS)]
    for copy in loads:
        copy.start()

    def device(dw, dn):
        return (around(me_w + dw, wide_size), around(me_n + dn, narrow_size))

    barrier = pltpu.get_barrier_semaphore()
    for dw, dn in SIDES:
        pl.semaphore_signal(barrier, inc=1, device_id=device(dw, dn), device_id_type=MESH)

    sub = lax.broadcasted_iota(jnp.int32, (POINTS, POINTS), 0)
    lane = lax.broadcasted_iota(jnp.int32, (POINTS, POINTS), 1)
    apart[...] = jnp.where(sub == lane, APART, 0.0).astype(F32)
    eye = jnp.where(sub == lane, 1.0, 0.0).astype(BF16)
    row = lax.broadcasted_iota(jnp.int32, (16, POINTS), 0)
    far = jnp.where((row == ROW_R) | (row == ROW_Y), FAR, 0.0)
    far = jnp.where(row == ROW_SQ[0], FAR * FAR, far)
    table[TILES] = jnp.where(row == ROW_ONE, 1.0, far)
    for i in range(CW + 2):
        for j in range(CN + 2):
            where_is[i * (CN + 2) + j] = tile_index(i - 1, j - 1)

    for copy in small[:5]:
        copy.wait()
    column = lax.broadcasted_iota(jnp.int32, (CN, POINTS), 0)
    anchor_n = column.astype(F32) * CELL_SPAN - CELL_SPAN * CN / 2
    hop_n = jnp.where(column == 0, CELL_SPAN * CN, jnp.where(column == CN - 1, -CELL_SPAN * CN, 0.0))

    def advanced(a):
        base, u, half, v = [], [], [], []
        for d in range(3):
            speed, push = velocity[d, a], acceleration[d, a]
            base.append(ref_local[d, a])
            u.append(displacement[d, a] + TIME_STEP * speed + 0.5 * TIME_STEP * TIME_STEP * push)
            half.append(speed + 0.5 * TIME_STEP * push)
            v.append(half[d] * (DAMPING / STIFFNESS))
        return base, u, half, v

    def tile_rows(a, up_w, up_n, base, u, v):
        r = [base[0] + (CELL_SPAN * (a - CW / 2) + up_w), base[1] + (anchor_n + up_n), base[2] - CELL_SPAN]
        y = [r[d] + u[d] for d in range(3)]
        squares = [
            r[0] * r[0] + r[1] * r[1] + r[2] * r[2],
            u[0] * (r[0] + y[0]) + u[1] * (r[1] + y[1]) + u[2] * (r[2] + y[2]),
            v[0] * y[0] + v[1] * y[1] + v[2] * y[2],
        ]
        return r + u + squares[:2] + v + y + squares[2:] + [jnp.ones_like(u[0])]

    for a in range(CW):
        base, u, half, v = advanced(a)
        for f, row in enumerate(tile_rows(a, 0.0, hop_n, base, u, v)):
            leaving[SIDE_AT[2] - CLUSTERS + a, f:f + 1] = row[0:1]
            leaving[SIDE_AT[3] - CLUSTERS + a, f:f + 1] = row[CN - 1:CN]
        if a in (0, CW - 1):
            side, hop_w = (0, CELL_SPAN * CW) if a == 0 else (1, -CELL_SPAN * CW)
            at = SIDE_AT[side] - CLUSTERS
            for f, row in enumerate(tile_rows(a, hop_w, 0.0, base, u, v)):
                leaving[at:at + CN, f] = row
            at = SIDE_AT[4 + 2 * side] - CLUSTERS
            for f, row in enumerate(tile_rows(a, hop_w, hop_n, base, u, v)):
                leaving[at, f:f + 1] = row[0:1]
                leaving[at + 1, f:f + 1] = row[CN - 1:CN]
    for side in range(2):
        for m in range(2):
            tag = jnp.full((8, POINTS), move_dst[0, 0, 1 - side, m], jnp.int32).astype(F32)
            leaving[TAGS_AT[side] - CLUSTERS, 8 * m:8 * m + 8] = tag

    pl.semaphore_wait(barrier, len(SIDES))
    halos = []
    for n, (dw, dn) in enumerate(SIDES):
        landing = SIDE_AT[SIDES.index((-dw, -dn))]
        halos.append(pltpu.make_async_remote_copy(
            src_ref=leaving.at[pl.ds(SIDE_AT[n] - CLUSTERS, SIDE_COUNT[n])],
            dst_ref=table.at[pl.ds(landing, SIDE_COUNT[n])],
            send_sem=halo_send.at[n], recv_sem=halo_recv.at[n],
            device_id=device(dw, dn), device_id_type=MESH,
        ))
    for copy in halos:
        copy.start()

    for a in range(CW):
        base, u, half, v = advanced(a)
        here = pl.ds(a * CN, CN)
        for f, row in enumerate(base + u + half):
            plain[here, f] = row
        for f in range(9, 16):
            plain[here, f] = jnp.zeros((CN, POINTS), F32)
        for f, row in enumerate(tile_rows(a, 0.0, 0.0, base, u, v)):
            table[here, f] = row

    def split_parts(tile):
        high = tile.astype(BF16)
        rest = tile - high.astype(F32)
        middle = rest.astype(BF16)
        return high, middle, (rest - middle.astype(F32)).astype(BF16)

    def split_tile(t, carry):
        for n, part in enumerate(split_parts(table[t])):
            split[t, n * 16:n * 16 + 16] = part
        return carry

    def toward(e):
        return device(1 - 2 * lax.rem(e, 2), 0)

    def hist_copy(e):
        return pltpu.make_async_remote_copy(
            src_ref=raw.at[e], dst_ref=hist_rows.at[CLUSTERS + e], send_sem=hist_send.at[e], recv_sem=hist_recv.at[e],
            device_id=toward(e), device_id_type=MESH,
        )

    def pack_copy(e):
        return pltpu.make_async_remote_copy(
            src_ref=pack.at[e], dst_ref=packed.at[e], send_sem=pack_send.at[e], recv_sem=pack_recv.at[e],
            device_id=toward(e), device_id_type=MESH,
        )

    def state_copy(e):
        return pltpu.make_async_remote_copy(
            src_ref=sent_state.at[e], dst_ref=state_in.at[e],
            send_sem=state_send.at[e], recv_sem=state_recv.at[e],
            device_id=toward(e), device_id_type=MESH,
        )

    def leaver(e):
        return jnp.maximum(move_src[0, 0, lax.rem(e, 2), e // 2], 0)

    for copy in small[5:]:
        copy.wait()
    for copy in loads:
        copy.wait()

    def send_hist(e, carry):
        c = leaver(e)
        for k in range(SLOTS):
            raw[e, k] = held[c, k]
        hist_copy(e).start()
        return carry

    lax.fori_loop(0, 4, send_hist, 0)

    lax.fori_loop(0, CLUSTERS, split_tile, 0, unroll=4)
    split_tile(TILES, 0)

    def left_side(c, carry):
        for g in range(3):
            rows = dot(pairs[g], split[c]).astype(BF16)
            left[c, g * POINTS:(g + 1) * POINTS, :] = dot_t(eye, rows).astype(BF16)
        return carry

    lax.fori_loop(0, CLUSTERS, left_side, 0, unroll=4)

    def partner_tiles(c):
        a, b = c // CN, lax.rem(c, CN)
        tiles, inverse = [], []
        for k in range(SLOTS):
            o = partners[a, b, k]
            dw, dn = o // 3 - 1, lax.rem(o, 3) - 1
            gw, gn = me_w * CW + a + dw, me_n * CN + b + dn
            inside = (gw >= 0) & (gw < wide_size * CW) & (gn >= 0) & (gn < narrow_size * CN)
            on = inside & (active[a, b, k] > 0)
            spot = where_is[(a + 1 + dw) * (CN + 2) + b + 1 + dn]
            tiles.append(jnp.where(on, spot, TILES))
            inverse.append(jnp.where(on, 1.0, 0.0) / jnp.full((1, POINTS), critical[a, b, k], F32))
        return tiles, inverse

    def right_side(tile):
        return jnp.concatenate([tile[q * 16:q * 16 + 16] for q, _ in PARTS], 0)

    def cluster(c):
        mine = left[c]
        tiles, inverse = partner_tiles(c)
        for pair in range(SLOTS // 2):
            theirs = [right_side(split[tiles[k]]) for k in (2 * pair, 2 * pair + 1)]
            forms[pair] = dot(mine, jnp.concatenate(theirs, 1))
        sums = None
        for k in range(SLOTS):
            pair, at = k // 2, pl.ds((k % 2) * POINTS, POINTS)
            rest_sq = forms[pair, 0:POINTS, at]
            if k == 0:
                rest_sq = rest_sq + apart[...]
            now_sq = jnp.maximum(rest_sq + forms[pair, POINTS:2 * POINTS, at], TINY)
            rate = forms[pair, 2 * POINTS:3 * POINTS, at]
            rest_inv = lax.rsqrt(rest_sq)
            now_inv = lax.rsqrt(now_sq)
            stretch = now_sq * now_inv * rest_inv - 1.0
            scaled = stretch * inverse[k]
            if k == 0:
                scaled = scaled - apart[...]
            hist = jnp.maximum(held[c, k], scaled)
            hist_rows[c, k] = hist
            weight = jnp.exp2(rest_sq * FALLOFF) * jnp.minimum(jnp.maximum(2.0 - hist, 0.0), 1.0)
            factor = weight * (stretch + rate * now_inv) * now_inv
            high = factor.astype(BF16)
            low = (factor - high.astype(F32)).astype(BF16)
            tile = split[tiles[k]]
            term = dot_t(jnp.concatenate([high, low], 1), jnp.concatenate([tile, tile], 1))
            sums = term if sums is None else sums + term
        sums = jnp.transpose(sums)
        sums = sums[0:16] + sums[16:32] + sums[32:48]
        here = table[c]
        own = plain[c]
        acc = STIFFNESS * (sums[ROW_Y:ROW_Y + 3] - here[ROW_Y:ROW_Y + 3] * sums[ROW_ONE:ROW_ONE + 1])
        state_rows[c, 0:6] = own[0:6]
        state_rows[c, 6:9] = own[6:9] + 0.5 * TIME_STEP * acc
        state_rows[c, 9:12] = acc
        state_rows[c, 12:16] = own[12:16]

    tag_copies = [
        pltpu.make_async_copy(table.at[TAGS_AT[side]], tags.at[side], tag_sem.at[side]) for side in range(2)
    ]

    def send_pack(e, carry):
        c = leaver(e)
        tiles, inverse = partner_tiles(c)
        pack[e, 0:16] = table[c]
        for k in range(SLOTS):
            pack[e, 16 + 8 * k:24 + 8 * k] = table[tiles[k], 0:8]
            pack[e, 16 + 8 * SLOTS + k:17 + 8 * SLOTS + k] = inverse[k]
        pack[e, 16 + 9 * SLOTS:PACK_ROWS] = jnp.zeros((8 - SLOTS, POINTS), F32)
        pack_copy(e).start()
        return carry

    def one(i, carry):
        @pl.when(i == 4)
        def _():
            for copy in halos:
                copy.wait()
            for copy in tag_copies:
                copy.start()
            lax.fori_loop(CLUSTERS, TILES, split_tile, 0, unroll=2)
            lax.fori_loop(0, 4, send_pack, 0)

        inner = 5 + lax.rem(i, 2) + 4 * (i // 2)
        side = 4 + 4 * ((i - 8) // 2) + 3 * lax.rem(i, 2)
        c = jnp.where(i < 4, inner, jnp.where(i < 8, i - 4, jnp.where(i < 12, side, i)))
        cluster(c)
        return carry

    lax.fori_loop(0, CLUSTERS, one, 0)

    def send_state(e, carry):
        sent_state[e] = state_rows[leaver(e)]
        state_copy(e).start()
        return carry

    lax.fori_loop(0, 4, send_state, 0)

    tail = jnp.where(lax.broadcasted_iota(jnp.int32, (8, POINTS), 0) == ROW_ONE - 8, 1.0, 0.0)

    def arrive(e, carry):
        pack_copy(e).wait()
        own = jnp.concatenate(split_parts(packed[e, 0:16]), 0)
        mine = []
        for g in range(2):
            mine.append(dot_t(eye, dot(pairs[g], own).astype(BF16)).astype(BF16))
        mine = jnp.concatenate(mine, 0)
        for pair in range(SLOTS // 2):
            theirs = []
            for k in (2 * pair, 2 * pair + 1):
                tile = jnp.concatenate([packed[e, 16 + 8 * k:24 + 8 * k], tail], 0)
                theirs.append(right_side(jnp.concatenate(split_parts(tile), 0)))
            forms[pair, 0:2 * POINTS] = dot(mine, jnp.concatenate(theirs, 1))
        hist_copy(e).wait()
        for k in range(SLOTS):
            pair, at = k // 2, pl.ds((k % 2) * POINTS, POINTS)
            rest_sq = forms[pair, 0:POINTS, at]
            if k == 0:
                rest_sq = rest_sq + apart[...]
            now_sq = jnp.maximum(rest_sq + forms[pair, POINTS:2 * POINTS, at], TINY)
            stretch = now_sq * lax.rsqrt(now_sq) * lax.rsqrt(rest_sq) - 1.0
            scaled = stretch * packed[e, 16 + 8 * SLOTS + k:17 + 8 * SLOTS + k]
            if k == 0:
                scaled = scaled - apart[...]
            hist_rows[CLUSTERS + e, k] = jnp.maximum(hist_rows[CLUSTERS + e, k], scaled)
        return carry

    lax.fori_loop(0, 4, arrive, 0)

    for copy in tag_copies:
        copy.wait()
    for o in range(CLUSTERS):
        source = o
        for e in range(4):
            source = jnp.where(tags[e % 2, 8 * (e // 2), 0] == float(o), CLUSTERS + e, source)
        sources[o] = source
    for e in range(4):
        state_copy(e).wait()


def place_kernel(hist_rows, state_rows, state_in, sources, ref_out, disp_out, vel_out, acc_out, hist_out, states, state_sem, sem):
    copies = []
    for o in range(CLUSTERS):
        copies.append(pltpu.make_async_copy(hist_rows.at[sources[o]], hist_out.at[o], sem.at[o]))
        copies[-1].start()
    for o in range(CLUSTERS):
        source = sources[o]
        rows = jnp.where(source < CLUSTERS, state_rows[o], state_in[jnp.maximum(source - CLUSTERS, 0)])
        for f in range(4):
            for d in range(3):
                states[f, d, o // CN, o % CN:o % CN + 1] = rows[3 * f + d:3 * f + d + 1]
    for f, ref in enumerate((ref_out, disp_out, vel_out, acc_out)):
        copies.append(pltpu.make_async_copy(states.at[f], ref, state_sem.at[f]))
        copies[-1].start()
    for copy in copies:
        copy.wait()


def per_device(
    wide_size, narrow_size,
    ref_local, displacement, velocity, acceleration, history, critical, active, partners, move_src, move_dst,
):
    vmem, smem, anywhere = (pl.BlockSpec(memory_space=m) for m in (pltpu.VMEM, pltpu.SMEM, pl.ANY))
    total = CLUSTERS + 4
    hist_shape = (total, SLOTS, POINTS, POINTS)
    operands = [
        ref_local, displacement, velocity, acceleration, critical, active, partners, move_src, move_dst,
        jnp.asarray(pairing(), BF16), history.reshape(CLUSTERS, SLOTS, POINTS, POINTS),
    ]
    operands = [pltpu.with_memory_space_constraint(x, pltpu.HBM) for x in operands]
    hist_rows, state_rows, state_in, sources = pl.pallas_call(
        functools.partial(step_kernel, wide_size, narrow_size),
        out_shape=(
            pltpu.VMEM(hist_shape, F32),
            pltpu.VMEM((CLUSTERS, 16, POINTS), F32),
            pltpu.VMEM((4, 16, POINTS), F32),
            pltpu.SMEM((CLUSTERS,), jnp.int32),
        ),
        in_specs=[anywhere] * len(operands),
        out_specs=(vmem, vmem, vmem, smem),
        scratch_shapes=[
            pltpu.VMEM((CLUSTERS, SLOTS, POINTS, POINTS), F32),
            *[pltpu.VMEM(ref_local.shape, F32)] * 4,
            pltpu.SMEM(critical.shape, F32),
            pltpu.SMEM(active.shape, jnp.int32),
            pltpu.SMEM(partners.shape, jnp.int32),
            pltpu.SMEM(move_src.shape, jnp.int32),
            pltpu.SMEM(move_dst.shape, jnp.int32),
            pltpu.VMEM((3, 96, 48), BF16),
            pltpu.SMEM(((CW + 2) * (CN + 2),), jnp.int32),
            pltpu.VMEM((CLUSTERS, 16, POINTS), F32),
            pltpu.VMEM((TILES + 1, 16, POINTS), F32),
            pltpu.VMEM((TILES - CLUSTERS, 16, POINTS), F32),
            pltpu.VMEM((TILES + 1, 48, POINTS), BF16),
            pltpu.VMEM((CLUSTERS, 3 * POINTS, 96), BF16),
            pltpu.VMEM((SLOTS // 2, 3 * POINTS, 2 * POINTS), F32),
            pltpu.VMEM((POINTS, POINTS), F32),
            pltpu.SMEM((2, 16, POINTS), F32),
            pltpu.VMEM((4, SLOTS, POINTS, POINTS), F32),
            pltpu.VMEM((4, PACK_ROWS, POINTS), F32),
            pltpu.VMEM((4, PACK_ROWS, POINTS), F32),
            pltpu.VMEM((4, 16, POINTS), F32),
            pltpu.SemaphoreType.DMA((10,)),
            pltpu.SemaphoreType.DMA((2,)),
            pltpu.SemaphoreType.DMA((CLUSTERS,)),
            pltpu.SemaphoreType.DMA((8,)),
            pltpu.SemaphoreType.DMA((8,)),
            *[pltpu.SemaphoreType.DMA((4,))] * 6,
        ],
        compiler_params=pltpu.CompilerParams(
            collective_id=0, has_side_effects=True, vmem_limit_bytes=20 << 20
        ),
        name="step",
    )(*operands)
    hist_rows = pltpu.with_memory_space_constraint(hist_rows, pltpu.VMEM)
    state_rows = pltpu.with_memory_space_constraint(state_rows, pltpu.VMEM)
    state_in = pltpu.with_memory_space_constraint(state_in, pltpu.VMEM)
    sources = pltpu.with_memory_space_constraint(sources, pltpu.SMEM)
    state = jax.ShapeDtypeStruct(ref_local.shape, F32)
    outs = pl.pallas_call(
        place_kernel,
        out_shape=(state,) * 4 + (jax.ShapeDtypeStruct((CLUSTERS, SLOTS, POINTS, POINTS), F32),),
        in_specs=[anywhere, vmem, vmem, smem],
        out_specs=(anywhere,) * 5,
        scratch_shapes=[
            pltpu.VMEM((4,) + ref_local.shape, F32),
            pltpu.SemaphoreType.DMA((4,)),
            pltpu.SemaphoreType.DMA((CLUSTERS,)),
        ],
        compiler_params=pltpu.CompilerParams(vmem_limit_bytes=8 << 20),
        name="place",
    )(hist_rows, state_rows, state_in, sources)
    return outs[:4] + (outs[4].reshape(history.shape),)


def solution(mesh):
    field = P(None, "wide", "narrow", None)
    blocks = P("wide", "narrow", None)
    hist = P("wide", "narrow", None, None, None)
    moves = P("wide", "narrow", None, None)
    return jax.shard_map(
        functools.partial(per_device, mesh.shape["wide"], mesh.shape["narrow"]),
        mesh=mesh,
        in_specs=(field,) * 4 + (hist,) + (blocks,) * 3 + (moves,) * 2,
        out_specs=(field,) * 4 + (hist,),
        check_vma=False,
    )
```

```python
import functools

import jax
import jax.numpy as jnp
import numpy as np
from jax import lax
from jax.experimental import pallas as pl
from jax.experimental.pallas import tpu as pltpu
from jax.sharding import PartitionSpec as P

STIFFNESS = 8.0
DAMPING = 0.8
TIME_STEP = 0.1
CELL_SPAN = 4.0
FALLOFF = float(-np.log2(np.e) / 9.0)
FAR = 1024.0
APART = 1.0e6
TINY = 1.0e-12

F32 = jnp.float32
BF16 = jnp.bfloat16
MESH = pl.DeviceIdType.MESH
CW = CN = 4
CLUSTERS = CW * CN
SLOTS = 6
POINTS = 128
TILES = CLUSTERS + 22
SIDES = ((-1, 0), (1, 0), (0, -1), (0, 1), (-1, -1), (-1, 1), (1, -1), (1, 1))
SIDE_AT = (16, 21, 26, 30, 34, 35, 36, 37)
SIDE_COUNT = (5, 5, 4, 4, 1, 1, 1, 1)
TAGS_AT = (20, 25)

ROW_R, ROW_U, ROW_V, ROW_Y, ROW_SQ, ROW_ONE = 0, 3, 8, 11, (6, 7, 14), 15
PACK_ROWS = 16 + 8 * SLOTS + 8
PARTS = ((0, 0), (1, 0), (0, 1), (1, 1), (2, 0), (0, 2))


def pairing():
    s = np.zeros((3, 96, 48), np.float32)
    for block, (q, p) in enumerate(PARTS):
        for d in range(3):
            s[0, block * 16 + ROW_R + d, p * 16 + ROW_R + d] = -2
            s[1, block * 16 + ROW_U + d, p * 16 + ROW_Y + d] = -2
            s[1, block * 16 + ROW_R + d, p * 16 + ROW_U + d] = -2
            s[2, block * 16 + ROW_Y + d, p * 16 + ROW_V + d] = -1
            s[2, block * 16 + ROW_V + d, p * 16 + ROW_Y + d] = -1
    for g in range(3):
        for part in range(3):
            s[g, PARTS.index((part, 0)) * 16 + ROW_SQ[g], ROW_ONE] = 1
            s[g, PARTS.index((0, part)) * 16 + ROW_ONE, part * 16 + ROW_SQ[g]] = 1
    return s


def around(i, size):
    i = jnp.where(i < 0, i + size, i)
    return jnp.where(i >= size, i - size, i)


def dot(a, b):
    return lax.dot_general(a, b, (((1,), (0,)), ((), ())), preferred_element_type=F32)


def dot_t(a, b):
    return lax.dot_general(a, b, (((1,), (1,)), ((), ())), preferred_element_type=F32)


def tile_index(i, j):
    if 0 <= i < CW and 0 <= j < CN:
        return i * CN + j
    if 0 <= j < CN:
        return (16 if i < 0 else 21) + j
    if 0 <= i < CW:
        return (26 if j < 0 else 30) + i
    return 34 + 2 * (i > 0) + (j > 0)


def step_kernel(
    wide_size, narrow_size,
    ref_hbm, disp_hbm, vel_hbm, acc_hbm, critical_hbm, active_hbm, partners_hbm, src_hbm, dst_hbm, pairs_hbm, history,
    hist_rows, state_rows, state_in, sources,
    held, ref_local, displacement, velocity, acceleration, critical, active, partners, move_src, move_dst, pairs, where_is,
    plain, table, leaving, split, left, forms, forms_in, apart, tags, raw, pack, packed, sent_state,
    small_sem, tag_sem, load_sem, halo_send, halo_recv, hist_send, hist_recv, pack_send, pack_recv, state_send, state_recv,
):
    me_w, me_n = lax.axis_index("wide"), lax.axis_index("narrow")
    small = [
        pltpu.make_async_copy(source, target, small_sem.at[n])
        for n, (source, target) in enumerate((
            (ref_hbm, ref_local), (disp_hbm, displacement), (vel_hbm, velocity), (acc_hbm, acceleration),
            (dst_hbm, move_dst), (pairs_hbm, pairs), (critical_hbm, critical), (active_hbm, active), (partners_hbm, partners),
            (src_hbm, move_src),
        ))
    ]
    for copy in small:
        copy.start()
    loads = [pltpu.make_async_copy(history.at[c], held.at[c], load_sem.at[c]) for c in range(CLUSTERS)]
    for copy in loads:
        copy.start()

    def device(dw, dn):
        return (around(me_w + dw, wide_size), around(me_n + dn, narrow_size))

    barrier = pltpu.get_barrier_semaphore()
    for dw, dn in SIDES:
        pl.semaphore_signal(barrier, inc=1, device_id=device(dw, dn), device_id_type=MESH)

    sub = lax.broadcasted_iota(jnp.int32, (POINTS, POINTS), 0)
    lane = lax.broadcasted_iota(jnp.int32, (POINTS, POINTS), 1)
    apart[...] = jnp.where(sub == lane, APART, 0.0).astype(F32)
    eye = jnp.where(sub == lane, 1.0, 0.0).astype(BF16)
    row = lax.broadcasted_iota(jnp.int32, (16, POINTS), 0)
    far = jnp.where((row == ROW_R) | (row == ROW_Y), FAR, 0.0)
    far = jnp.where(row == ROW_SQ[0], FAR * FAR, far)
    table[TILES] = jnp.where(row == ROW_ONE, 1.0, far)
    for i in range(CW + 2):
        for j in range(CN + 2):
            edges = [
                edge for out, edge in (
                    (i == 0, me_w == 0), (i == CW + 1, me_w == wide_size - 1),
                    (j == 0, me_n == 0), (j == CN + 1, me_n == narrow_size - 1),
                ) if out
            ]
            spot = tile_index(i - 1, j - 1)
            for edge in edges:
                spot = jnp.where(edge, TILES, spot)
            where_is[i * (CN + 2) + j] = spot

    for copy in small[:5]:
        copy.wait()
    column = lax.broadcasted_iota(jnp.int32, (CN, POINTS), 0)
    anchor_n = column.astype(F32) * CELL_SPAN - CELL_SPAN * CN / 2
    hop_n = jnp.where(column == 0, CELL_SPAN * CN, jnp.where(column == CN - 1, -CELL_SPAN * CN, 0.0))

    def advanced(a):
        base, u, half, v = [], [], [], []
        for d in range(3):
            speed, push = velocity[d, a], acceleration[d, a]
            base.append(ref_local[d, a])
            u.append(displacement[d, a] + TIME_STEP * speed + 0.5 * TIME_STEP * TIME_STEP * push)
            half.append(speed + 0.5 * TIME_STEP * push)
            v.append(half[d] * (DAMPING / STIFFNESS))
        return base, u, half, v

    def tile_rows(a, up_w, up_n, base, u, v):
        r = [base[0] + (CELL_SPAN * (a - CW / 2) + up_w), base[1] + (anchor_n + up_n), base[2] - CELL_SPAN]
        y = [r[d] + u[d] for d in range(3)]
        squares = [
            r[0] * r[0] + r[1] * r[1] + r[2] * r[2],
            u[0] * (r[0] + y[0]) + u[1] * (r[1] + y[1]) + u[2] * (r[2] + y[2]),
            v[0] * y[0] + v[1] * y[1] + v[2] * y[2],
        ]
        return r + u + squares[:2] + v + y + squares[2:] + [jnp.ones_like(u[0])]

    for a in range(CW):
        base, u, half, v = advanced(a)
        for f, row in enumerate(tile_rows(a, 0.0, hop_n, base, u, v)):
            leaving[SIDE_AT[2] - CLUSTERS + a, f:f + 1] = row[0:1]
            leaving[SIDE_AT[3] - CLUSTERS + a, f:f + 1] = row[CN - 1:CN]
        if a in (0, CW - 1):
            side, hop_w = (0, CELL_SPAN * CW) if a == 0 else (1, -CELL_SPAN * CW)
            at = SIDE_AT[side] - CLUSTERS
            for f, row in enumerate(tile_rows(a, hop_w, 0.0, base, u, v)):
                leaving[at:at + CN, f] = row
            at = SIDE_AT[4 + 2 * side] - CLUSTERS
            for f, row in enumerate(tile_rows(a, hop_w, hop_n, base, u, v)):
                leaving[at, f:f + 1] = row[0:1]
                leaving[at + 1, f:f + 1] = row[CN - 1:CN]
    for side in range(2):
        for m in range(2):
            tag = jnp.full((8, POINTS), move_dst[0, 0, 1 - side, m], jnp.int32).astype(F32)
            leaving[TAGS_AT[side] - CLUSTERS, 8 * m:8 * m + 8] = tag

    pl.semaphore_wait(barrier, len(SIDES))
    halos = []
    for n, (dw, dn) in enumerate(SIDES):
        landing = SIDE_AT[SIDES.index((-dw, -dn))]
        halos.append(pltpu.make_async_remote_copy(
            src_ref=leaving.at[pl.ds(SIDE_AT[n] - CLUSTERS, SIDE_COUNT[n])],
            dst_ref=table.at[pl.ds(landing, SIDE_COUNT[n])],
            send_sem=halo_send.at[n], recv_sem=halo_recv.at[n],
            device_id=device(dw, dn), device_id_type=MESH,
        ))
    for copy in halos:
        copy.start()

    for a in range(CW):
        base, u, half, v = advanced(a)
        here = pl.ds(a * CN, CN)
        for f, row in enumerate(base + u + half):
            plain[here, f] = row
        for f in range(9, 16):
            plain[here, f] = jnp.zeros((CN, POINTS), F32)
        for f, row in enumerate(tile_rows(a, 0.0, 0.0, base, u, v)):
            table[here, f] = row

    def split_parts(tile):
        high = tile.astype(BF16)
        rest = tile - high.astype(F32)
        middle = rest.astype(BF16)
        return high, middle, (rest - middle.astype(F32)).astype(BF16)

    def split_tile(t, carry):
        for n, part in enumerate(split_parts(table[t])):
            split[t, n * 16:n * 16 + 16] = part
        return carry

    def toward(e):
        return device(1 - 2 * lax.rem(e, 2), 0)

    def hist_copy(e):
        return pltpu.make_async_remote_copy(
            src_ref=raw.at[e], dst_ref=hist_rows.at[CLUSTERS + e], send_sem=hist_send.at[e], recv_sem=hist_recv.at[e],
            device_id=toward(e), device_id_type=MESH,
        )

    def pack_copy(e):
        return pltpu.make_async_remote_copy(
            src_ref=pack.at[e], dst_ref=packed.at[e], send_sem=pack_send.at[e], recv_sem=pack_recv.at[e],
            device_id=toward(e), device_id_type=MESH,
        )

    def state_copy(e):
        return pltpu.make_async_remote_copy(
            src_ref=sent_state.at[e], dst_ref=state_in.at[e],
            send_sem=state_send.at[e], recv_sem=state_recv.at[e],
            device_id=toward(e), device_id_type=MESH,
        )

    def leaver(e):
        return jnp.maximum(move_src[0, 0, lax.rem(e, 2), e // 2], 0)

    for copy in small[5:]:
        copy.wait()
    lax.fori_loop(0, CLUSTERS, split_tile, 0, unroll=4)
    split_tile(TILES, 0)

    def left_side(c, carry):
        for g in range(3):
            rows = dot(pairs[g], split[c]).astype(BF16)
            left[c, g * POINTS:(g + 1) * POINTS, :] = dot_t(eye, rows).astype(BF16)
        return carry

    lax.fori_loop(0, CLUSTERS, left_side, 0, unroll=4)

    for copy in loads:
        copy.wait()

    def send_hist(e, carry):
        c = leaver(e)
        for k in range(SLOTS):
            raw[e, k] = held[c, k]
        hist_copy(e).start()
        return carry

    lax.fori_loop(0, 4, send_hist, 0)

    def place_of(c):
        a = lax.shift_right_logical(c, 2)
        return a, c - CN * a

    def partner(c, k):
        a, b = place_of(c)
        o = partners[a, b, k]
        third = lax.shift_right_logical(o * 11, 5)
        spot = where_is[(CN + 2) * (a + third) + b + o - 3 * third]
        return jnp.where(active[a, b, k] > 0, spot, TILES)

    def inverse_limit(c, k, spot):
        a, b = place_of(c)
        return jnp.where(spot == TILES, 0.0, 1.0) / jnp.full((1, POINTS), critical[a, b, k], F32)

    def right_side(tile):
        return jnp.concatenate([tile[q * 16:q * 16 + 16] for q, _ in PARTS], 0)

    def prepare(c, buffer, pair):
        theirs = [right_side(split[partner(c, k)]) for k in (2 * pair, 2 * pair + 1)]
        forms[buffer, pair] = dot(left[c], jnp.concatenate(theirs, 1))

    def pull(c, buffer, k):
        pair, at = k // 2, pl.ds((k % 2) * POINTS, POINTS)
        spot = partner(c, k)
        rest_sq = forms[buffer, pair, 0:POINTS, at]
        if k == 0:
            rest_sq = rest_sq + apart[...]
        now_sq = jnp.maximum(rest_sq + forms[buffer, pair, POINTS:2 * POINTS, at], TINY)
        rate = forms[buffer, pair, 2 * POINTS:3 * POINTS, at]
        now_inv = lax.rsqrt(now_sq)
        stretch = now_sq * now_inv * lax.rsqrt(rest_sq) - 1.0
        scaled = stretch * inverse_limit(c, k, spot)
        if k == 0:
            scaled = scaled - apart[...]
        hist = jnp.maximum(held[c, k], scaled)
        hist_rows[c, k] = hist
        weight = jnp.exp2(rest_sq * FALLOFF) * jnp.minimum(jnp.maximum(2.0 - hist, 0.0), 1.0)
        factor = weight * (stretch + rate * now_inv) * now_inv
        high = factor.astype(BF16)
        low = (factor - high.astype(F32)).astype(BF16)
        tile = split[spot]
        return dot_t(jnp.concatenate([high, low], 1), jnp.concatenate([tile, tile], 1))

    def cluster(c, buffer, after, after_buffer):
        sums = None
        for pair in range(SLOTS // 2):
            prepare(after, after_buffer, pair)
            for k in (2 * pair, 2 * pair + 1):
                term = pull(c, buffer, k)
                sums = term if sums is None else sums + term
        sums = jnp.transpose(sums)
        sums = sums[0:16] + sums[16:32] + sums[32:48]
        here = table[c]
        own = plain[c]
        acc = STIFFNESS * (sums[ROW_Y:ROW_Y + 3] - here[ROW_Y:ROW_Y + 3] * sums[ROW_ONE:ROW_ONE + 1])
        state_rows[c, 0:6] = own[0:6]
        state_rows[c, 6:9] = own[6:9] + 0.5 * TIME_STEP * acc
        state_rows[c, 9:12] = acc
        state_rows[c, 12:16] = own[12:16]

    tag_copies = [
        pltpu.make_async_copy(table.at[TAGS_AT[side]], tags.at[side], tag_sem.at[side]) for side in range(2)
    ]

    def send_pack(e, carry):
        c = leaver(e)
        pack[e, 0:16] = table[c]
        for k in range(SLOTS):
            spot = partner(c, k)
            pack[e, 16 + 8 * k:24 + 8 * k] = table[spot, 0:8]
            pack[e, 16 + 8 * SLOTS + k:17 + 8 * SLOTS + k] = inverse_limit(c, k, spot)
        pack[e, 16 + 9 * SLOTS:PACK_ROWS] = jnp.zeros((8 - SLOTS, POINTS), F32)
        pack_copy(e).start()
        return carry

    def nth(i):
        inner = 5 + lax.rem(i, 2) + 4 * (i // 2)
        side = 4 + 4 * ((i - 8) // 2) + 3 * lax.rem(i, 2)
        return jnp.where(i < 4, inner, jnp.where(i < 8, i - 4, jnp.where(i < 12, side, i)))

    for pair in range(SLOTS // 2):
        prepare(nth(0), 0, pair)

    def two(i, carry):
        @pl.when(i == 1)
        def _():
            for copy in halos:
                copy.wait()
            for copy in tag_copies:
                copy.start()
            lax.fori_loop(CLUSTERS, TILES, split_tile, 0, unroll=2)
            lax.fori_loop(0, 4, send_pack, 0)

        first, second = nth(2 * i), nth(2 * i + 1)
        cluster(first, 0, second, 1)
        cluster(second, 1, nth(jnp.minimum(2 * i + 2, CLUSTERS - 1)), 0)
        return carry

    lax.fori_loop(0, CLUSTERS // 2, two, 0)

    def send_state(e, carry):
        sent_state[e] = state_rows[leaver(e)]
        state_copy(e).start()
        return carry

    lax.fori_loop(0, 4, send_state, 0)

    tail = jnp.where(lax.broadcasted_iota(jnp.int32, (8, POINTS), 0) == ROW_ONE - 8, 1.0, 0.0)

    def expect(e, carry):
        pack_copy(e).wait()
        own = jnp.concatenate(split_parts(packed[e, 0:16]), 0)
        mine = jnp.concatenate([dot_t(eye, dot(pairs[g], own).astype(BF16)).astype(BF16) for g in range(2)], 0)
        for pair in range(SLOTS // 2):
            theirs = []
            for k in (2 * pair, 2 * pair + 1):
                tile = jnp.concatenate([packed[e, 16 + 8 * k:24 + 8 * k], tail], 0)
                theirs.append(right_side(jnp.concatenate(split_parts(tile), 0)))
            forms_in[e, pair] = dot(mine, jnp.concatenate(theirs, 1))
        return carry

    lax.fori_loop(0, 4, expect, 0)

    for copy in tag_copies:
        copy.wait()
    for o in range(CLUSTERS):
        source = o
        for e in range(4):
            source = jnp.where(tags[e % 2, 8 * (e // 2), 0] == float(o), CLUSTERS + e, source)
        sources[o] = source

    def arrive(e, carry):
        hist_copy(e).wait()
        for k in range(SLOTS):
            pair, at = k // 2, pl.ds((k % 2) * POINTS, POINTS)
            rest_sq = forms_in[e, pair, 0:POINTS, at]
            if k == 0:
                rest_sq = rest_sq + apart[...]
            now_sq = jnp.maximum(rest_sq + forms_in[e, pair, POINTS:2 * POINTS, at], TINY)
            stretch = now_sq * lax.rsqrt(now_sq) * lax.rsqrt(rest_sq) - 1.0
            scaled = stretch * packed[e, 16 + 8 * SLOTS + k:17 + 8 * SLOTS + k]
            if k == 0:
                scaled = scaled - apart[...]
            hist_rows[CLUSTERS + e, k] = jnp.maximum(hist_rows[CLUSTERS + e, k], scaled)
        return carry

    lax.fori_loop(0, 4, arrive, 0)

    for e in range(4):
        state_copy(e).wait()


def place_kernel(hist_rows, state_rows, state_in, sources, ref_out, disp_out, vel_out, acc_out, hist_out, states, state_sem, sem):
    copies = []
    for o in range(CLUSTERS):
        copies.append(pltpu.make_async_copy(hist_rows.at[sources[o]], hist_out.at[o], sem.at[o]))
        copies[-1].start()
    for o in range(CLUSTERS):
        source = sources[o]
        rows = jnp.where(source < CLUSTERS, state_rows[o], state_in[jnp.maximum(source - CLUSTERS, 0)])
        for f in range(4):
            for d in range(3):
                states[f, d, o // CN, o % CN:o % CN + 1] = rows[3 * f + d:3 * f + d + 1]
    for f, ref in enumerate((ref_out, disp_out, vel_out, acc_out)):
        copies.append(pltpu.make_async_copy(states.at[f], ref, state_sem.at[f]))
        copies[-1].start()
    for copy in copies:
        copy.wait()


def per_device(
    wide_size, narrow_size,
    ref_local, displacement, velocity, acceleration, history, critical, active, partners, move_src, move_dst,
):
    vmem, smem, anywhere = (pl.BlockSpec(memory_space=m) for m in (pltpu.VMEM, pltpu.SMEM, pl.ANY))
    total = CLUSTERS + 4
    hist_shape = (total, SLOTS, POINTS, POINTS)
    operands = [
        ref_local, displacement, velocity, acceleration, critical, active, partners, move_src, move_dst,
        jnp.asarray(pairing(), BF16), history.reshape(CLUSTERS, SLOTS, POINTS, POINTS),
    ]
    operands = [pltpu.with_memory_space_constraint(x, pltpu.HBM) for x in operands]
    hist_rows, state_rows, state_in, sources = pl.pallas_call(
        functools.partial(step_kernel, wide_size, narrow_size),
        out_shape=(
            pltpu.VMEM(hist_shape, F32),
            pltpu.VMEM((CLUSTERS, 16, POINTS), F32),
            pltpu.VMEM((4, 16, POINTS), F32),
            pltpu.SMEM((CLUSTERS,), jnp.int32),
        ),
        in_specs=[anywhere] * len(operands),
        out_specs=(vmem, vmem, vmem, smem),
        scratch_shapes=[
            pltpu.VMEM((CLUSTERS, SLOTS, POINTS, POINTS), F32),
            *[pltpu.VMEM(ref_local.shape, F32)] * 4,
            pltpu.SMEM(critical.shape, F32),
            pltpu.SMEM(active.shape, jnp.int32),
            pltpu.SMEM(partners.shape, jnp.int32),
            pltpu.SMEM(move_src.shape, jnp.int32),
            pltpu.SMEM(move_dst.shape, jnp.int32),
            pltpu.VMEM((3, 96, 48), BF16),
            pltpu.SMEM(((CW + 2) * (CN + 2),), jnp.int32),
            pltpu.VMEM((CLUSTERS, 16, POINTS), F32),
            pltpu.VMEM((TILES + 1, 16, POINTS), F32),
            pltpu.VMEM((TILES - CLUSTERS, 16, POINTS), F32),
            pltpu.VMEM((TILES + 1, 48, POINTS), BF16),
            pltpu.VMEM((CLUSTERS, 3 * POINTS, 96), BF16),
            pltpu.VMEM((2, SLOTS // 2, 3 * POINTS, 2 * POINTS), F32),
            pltpu.VMEM((4, SLOTS // 2, 2 * POINTS, 2 * POINTS), F32),
            pltpu.VMEM((POINTS, POINTS), F32),
            pltpu.SMEM((2, 16, POINTS), F32),
            pltpu.VMEM((4, SLOTS, POINTS, POINTS), F32),
            pltpu.VMEM((4, PACK_ROWS, POINTS), F32),
            pltpu.VMEM((4, PACK_ROWS, POINTS), F32),
            pltpu.VMEM((4, 16, POINTS), F32),
            pltpu.SemaphoreType.DMA((10,)),
            pltpu.SemaphoreType.DMA((2,)),
            pltpu.SemaphoreType.DMA((CLUSTERS,)),
            pltpu.SemaphoreType.DMA((8,)),
            pltpu.SemaphoreType.DMA((8,)),
            *[pltpu.SemaphoreType.DMA((4,))] * 6,
        ],
        compiler_params=pltpu.CompilerParams(
            collective_id=0, has_side_effects=True, vmem_limit_bytes=26 << 20
        ),
        name="step",
    )(*operands)
    hist_rows = pltpu.with_memory_space_constraint(hist_rows, pltpu.VMEM)
    state_rows = pltpu.with_memory_space_constraint(state_rows, pltpu.VMEM)
    state_in = pltpu.with_memory_space_constraint(state_in, pltpu.VMEM)
    sources = pltpu.with_memory_space_constraint(sources, pltpu.SMEM)
    state = jax.ShapeDtypeStruct(ref_local.shape, F32)
    outs = pl.pallas_call(
        place_kernel,
        out_shape=(state,) * 4 + (jax.ShapeDtypeStruct((CLUSTERS, SLOTS, POINTS, POINTS), F32),),
        in_specs=[anywhere, vmem, vmem, smem],
        out_specs=(anywhere,) * 5,
        scratch_shapes=[
            pltpu.VMEM((4,) + ref_local.shape, F32),
            pltpu.SemaphoreType.DMA((4,)),
            pltpu.SemaphoreType.DMA((CLUSTERS,)),
        ],
        compiler_params=pltpu.CompilerParams(vmem_limit_bytes=8 << 20),
        name="place",
    )(hist_rows, state_rows, state_in, sources)
    return outs[:4] + (outs[4].reshape(history.shape),)


def solution(mesh):
    field = P(None, "wide", "narrow", None)
    blocks = P("wide", "narrow", None)
    hist = P("wide", "narrow", None, None, None)
    moves = P("wide", "narrow", None, None)
    return jax.shard_map(
        functools.partial(per_device, mesh.shape["wide"], mesh.shape["narrow"]),
        mesh=mesh,
        in_specs=(field,) * 4 + (hist,) + (blocks,) * 3 + (moves,) * 2,
        out_specs=(field,) * 4 + (hist,),
        check_vma=False,
    )
```

```python
import functools

import jax
import jax.numpy as jnp
import numpy as np
from jax import lax
from jax.experimental import pallas as pl
from jax.experimental.pallas import tpu as pltpu
from jax.sharding import PartitionSpec as P

STIFFNESS = 8.0
DAMPING = 0.8
TIME_STEP = 0.1
CELL_SPAN = 4.0
FALLOFF = float(-np.log2(np.e) / 9.0)
FAR = 1024.0
APART = 1.0e6
TINY = 1.0e-12

F32 = jnp.float32
BF16 = jnp.bfloat16
MESH = pl.DeviceIdType.MESH
CW = CN = 4
CLUSTERS = CW * CN
SLOTS = 6
POINTS = 128
TILES = CLUSTERS + 22
SIDES = ((-1, 0), (1, 0), (0, -1), (0, 1), (-1, -1), (-1, 1), (1, -1), (1, 1))
SIDE_AT = (16, 21, 26, 30, 34, 35, 36, 37)
SIDE_COUNT = (5, 5, 4, 4, 1, 1, 1, 1)
TAGS_AT = (20, 25)

ROW_R, ROW_U, ROW_V, ROW_Y, ROW_SQ, ROW_ONE = 0, 3, 8, 11, (6, 7, 14), 15
PACK_ROWS = 16 + 8 * SLOTS + 8
PARTS = ((0, 0), (1, 0), (0, 1), (1, 1), (2, 0), (0, 2))


def pairing():
    s = np.zeros((3, 128, 48), np.float32)
    for block, (q, p) in enumerate(PARTS):
        for d in range(3):
            s[0, block * 16 + ROW_R + d, p * 16 + ROW_R + d] = -2
            s[1, block * 16 + ROW_U + d, p * 16 + ROW_Y + d] = -2
            s[1, block * 16 + ROW_R + d, p * 16 + ROW_U + d] = -2
            s[2, block * 16 + ROW_Y + d, p * 16 + ROW_V + d] = -1
            s[2, block * 16 + ROW_V + d, p * 16 + ROW_Y + d] = -1
    for g in range(3):
        for part in range(3):
            s[g, PARTS.index((part, 0)) * 16 + ROW_SQ[g], ROW_ONE] = 1
            s[g, PARTS.index((0, part)) * 16 + ROW_ONE, part * 16 + ROW_SQ[g]] = 1
    return s.reshape(3 * 128, 48).T


def around(i, size):
    i = jnp.where(i < 0, i + size, i)
    return jnp.where(i >= size, i - size, i)


def dot(a, b):
    return lax.dot_general(a, b, (((1,), (0,)), ((), ())), preferred_element_type=F32)


def dot_t(a, b):
    return lax.dot_general(a, b, (((1,), (1,)), ((), ())), preferred_element_type=F32)


def tile_index(i, j):
    if 0 <= i < CW and 0 <= j < CN:
        return i * CN + j
    if 0 <= j < CN:
        return (16 if i < 0 else 21) + j
    if 0 <= i < CW:
        return (26 if j < 0 else 30) + i
    return 34 + 2 * (i > 0) + (j > 0)


def step_kernel(
    wide_size, narrow_size,
    ref_hbm, disp_hbm, vel_hbm, acc_hbm, critical_hbm, active_hbm, partners_hbm, src_hbm, dst_hbm, pairs_hbm, history,
    hist_rows, state_rows, state_in, sources,
    held, ref_local, displacement, velocity, acceleration, critical, active, partners, move_src, move_dst, pairs, where_is,
    plain, table, leaving, split, left, forms, forms_in, apart, tags, raw, pack, packed, sent_state,
    small_sem, tag_sem, load_sem, halo_send, halo_recv, hist_send, hist_recv, pack_send, pack_recv, state_send, state_recv,
):
    me_w, me_n = lax.axis_index("wide"), lax.axis_index("narrow")
    small = [
        pltpu.make_async_copy(source, target, small_sem.at[n])
        for n, (source, target) in enumerate((
            (ref_hbm, ref_local), (disp_hbm, displacement), (vel_hbm, velocity), (acc_hbm, acceleration),
            (dst_hbm, move_dst), (pairs_hbm, pairs), (critical_hbm, critical), (active_hbm, active), (partners_hbm, partners),
            (src_hbm, move_src),
        ))
    ]
    for copy in small:
        copy.start()
    loads = [pltpu.make_async_copy(history.at[c], held.at[c], load_sem.at[c]) for c in range(CLUSTERS)]
    for copy in loads:
        copy.start()

    def device(dw, dn):
        return (around(me_w + dw, wide_size), around(me_n + dn, narrow_size))

    barrier = pltpu.get_barrier_semaphore()
    for dw, dn in SIDES:
        pl.semaphore_signal(barrier, inc=1, device_id=device(dw, dn), device_id_type=MESH)

    sub = lax.broadcasted_iota(jnp.int32, (POINTS, POINTS), 0)
    lane = lax.broadcasted_iota(jnp.int32, (POINTS, POINTS), 1)
    apart[...] = jnp.where(sub == lane, APART, 0.0).astype(F32)
    row = lax.broadcasted_iota(jnp.int32, (16, POINTS), 0)
    far = jnp.where((row == ROW_R) | (row == ROW_Y), FAR, 0.0)
    far = jnp.where(row == ROW_SQ[0], FAR * FAR, far)
    table[TILES] = jnp.where(row == ROW_ONE, 1.0, far)
    for i in range(CW + 2):
        for j in range(CN + 2):
            edges = [
                edge for out, edge in (
                    (i == 0, me_w == 0), (i == CW + 1, me_w == wide_size - 1),
                    (j == 0, me_n == 0), (j == CN + 1, me_n == narrow_size - 1),
                ) if out
            ]
            spot = tile_index(i - 1, j - 1)
            for edge in edges:
                spot = jnp.where(edge, TILES, spot)
            where_is[i * (CN + 2) + j] = spot

    for copy in small[:5]:
        copy.wait()
    column = lax.broadcasted_iota(jnp.int32, (CN, POINTS), 0)
    anchor_n = column.astype(F32) * CELL_SPAN - CELL_SPAN * CN / 2
    hop_n = jnp.where(column == 0, CELL_SPAN * CN, jnp.where(column == CN - 1, -CELL_SPAN * CN, 0.0))

    def advanced(a):
        base, u, half, v = [], [], [], []
        for d in range(3):
            speed, push = velocity[d, a], acceleration[d, a]
            base.append(ref_local[d, a])
            u.append(displacement[d, a] + TIME_STEP * speed + 0.5 * TIME_STEP * TIME_STEP * push)
            half.append(speed + 0.5 * TIME_STEP * push)
            v.append(half[d] * (DAMPING / STIFFNESS))
        return base, u, half, v

    def tile_rows(a, up_w, up_n, base, u, v):
        r = [base[0] + (CELL_SPAN * (a - CW / 2) + up_w), base[1] + (anchor_n + up_n), base[2] - CELL_SPAN]
        y = [r[d] + u[d] for d in range(3)]
        squares = [
            r[0] * r[0] + r[1] * r[1] + r[2] * r[2],
            u[0] * (r[0] + y[0]) + u[1] * (r[1] + y[1]) + u[2] * (r[2] + y[2]),
            v[0] * y[0] + v[1] * y[1] + v[2] * y[2],
        ]
        return r + u + squares[:2] + v + y + squares[2:] + [jnp.ones_like(u[0])]

    for a in range(CW):
        base, u, half, v = advanced(a)
        for f, row in enumerate(tile_rows(a, 0.0, hop_n, base, u, v)):
            leaving[SIDE_AT[2] - CLUSTERS + a, f:f + 1] = row[0:1]
            leaving[SIDE_AT[3] - CLUSTERS + a, f:f + 1] = row[CN - 1:CN]
        if a in (0, CW - 1):
            side, hop_w = (0, CELL_SPAN * CW) if a == 0 else (1, -CELL_SPAN * CW)
            at = SIDE_AT[side] - CLUSTERS
            for f, row in enumerate(tile_rows(a, hop_w, 0.0, base, u, v)):
                leaving[at:at + CN, f] = row
            at = SIDE_AT[4 + 2 * side] - CLUSTERS
            for f, row in enumerate(tile_rows(a, hop_w, hop_n, base, u, v)):
                leaving[at, f:f + 1] = row[0:1]
                leaving[at + 1, f:f + 1] = row[CN - 1:CN]
    for side in range(2):
        for m in range(2):
            tag = jnp.full((8, POINTS), move_dst[0, 0, 1 - side, m], jnp.int32).astype(F32)
            leaving[TAGS_AT[side] - CLUSTERS, 8 * m:8 * m + 8] = tag

    pl.semaphore_wait(barrier, len(SIDES))
    halos = []
    for n, (dw, dn) in enumerate(SIDES):
        landing = SIDE_AT[SIDES.index((-dw, -dn))]
        halos.append(pltpu.make_async_remote_copy(
            src_ref=leaving.at[pl.ds(SIDE_AT[n] - CLUSTERS, SIDE_COUNT[n])],
            dst_ref=table.at[pl.ds(landing, SIDE_COUNT[n])],
            send_sem=halo_send.at[n], recv_sem=halo_recv.at[n],
            device_id=device(dw, dn), device_id_type=MESH,
        ))
    for copy in halos:
        copy.start()

    for a in range(CW):
        base, u, half, v = advanced(a)
        here = pl.ds(a * CN, CN)
        for f, row in enumerate(base + u + half):
            plain[here, f] = row
        for f in range(9, 16):
            plain[here, f] = jnp.zeros((CN, POINTS), F32)
        for f, row in enumerate(tile_rows(a, 0.0, 0.0, base, u, v)):
            table[here, f] = row

    def split_parts(tile):
        high = tile.astype(BF16)
        rest = tile - high.astype(F32)
        middle = rest.astype(BF16)
        return high, middle, (rest - middle.astype(F32)).astype(BF16)

    def split_tile(t, carry):
        for n, part in enumerate(split_parts(table[t])):
            split[t, n * 16:n * 16 + 16] = part
        return carry

    def toward(e):
        return device(1 - 2 * lax.rem(e, 2), 0)

    def hist_copy(e):
        return pltpu.make_async_remote_copy(
            src_ref=raw.at[e], dst_ref=hist_rows.at[CLUSTERS + e], send_sem=hist_send.at[e], recv_sem=hist_recv.at[e],
            device_id=toward(e), device_id_type=MESH,
        )

    def pack_copy(e):
        return pltpu.make_async_remote_copy(
            src_ref=pack.at[e], dst_ref=packed.at[e], send_sem=pack_send.at[e], recv_sem=pack_recv.at[e],
            device_id=toward(e), device_id_type=MESH,
        )

    def state_copy(e):
        return pltpu.make_async_remote_copy(
            src_ref=sent_state.at[e], dst_ref=state_in.at[e],
            send_sem=state_send.at[e], recv_sem=state_recv.at[e],
            device_id=toward(e), device_id_type=MESH,
        )

    def leaver(e):
        return jnp.maximum(move_src[0, 0, lax.rem(e, 2), e // 2], 0)

    for copy in small[5:]:
        copy.wait()
    lax.fori_loop(0, CLUSTERS, split_tile, 0, unroll=4)
    split_tile(TILES, 0)

    def left_rows(parts, count):
        turned = jnp.transpose(parts.astype(F32)).astype(BF16)
        wide = dot(turned, pairs[:, 0:count * POINTS]).astype(BF16)
        return jnp.concatenate([wide[:, g * POINTS:(g + 1) * POINTS] for g in range(count)], 0)

    def left_side(c, carry):
        left[c] = left_rows(split[c], 3)
        return carry

    lax.fori_loop(0, CLUSTERS, left_side, 0, unroll=4)

    for copy in loads:
        copy.wait()

    def send_hist(e, carry):
        c = leaver(e)
        for k in range(SLOTS):
            raw[e, k] = held[c, k]
        hist_copy(e).start()
        return carry

    lax.fori_loop(0, 2, send_hist, 0)

    def place_of(c):
        a = lax.shift_right_logical(c, 2)
        return a, c - CN * a

    def partner(c, k):
        a, b = place_of(c)
        o = partners[a, b, k]
        third = lax.shift_right_logical(o * 11, 5)
        spot = where_is[(CN + 2) * (a + third) + b + o - 3 * third]
        return jnp.where(active[a, b, k] > 0, spot, TILES)

    def inverse_limit(c, k, spot):
        a, b = place_of(c)
        return jnp.where(spot == TILES, 0.0, 1.0) / jnp.full((1, POINTS), critical[a, b, k], F32)

    def right_side(tile):
        return jnp.concatenate([tile[q * 16:q * 16 + 16] for q, _ in PARTS], 0)

    def prepare(c, buffer, pair):
        theirs = [right_side(split[partner(c, k)]) for k in (2 * pair, 2 * pair + 1)]
        forms[buffer, pair] = dot(left[c, :, 0:96], jnp.concatenate(theirs, 1))

    def pull(c, buffer, k):
        pair, at = k // 2, pl.ds((k % 2) * POINTS, POINTS)
        spot = partner(c, k)
        rest_sq = forms[buffer, pair, 0:POINTS, at]
        if k == 0:
            rest_sq = rest_sq + apart[...]
        now_sq = jnp.maximum(rest_sq + forms[buffer, pair, POINTS:2 * POINTS, at], TINY)
        rate = forms[buffer, pair, 2 * POINTS:3 * POINTS, at]
        now_inv = lax.rsqrt(now_sq)
        stretch = now_sq * now_inv * lax.rsqrt(rest_sq) - 1.0
        scaled = stretch * inverse_limit(c, k, spot)
        if k == 0:
            scaled = scaled - apart[...]
        hist = jnp.maximum(held[c, k], scaled)
        hist_rows[c, k] = hist
        weight = jnp.exp2(rest_sq * FALLOFF) * jnp.minimum(jnp.maximum(2.0 - hist, 0.0), 1.0)
        factor = weight * (stretch + rate * now_inv) * now_inv
        high = factor.astype(BF16)
        low = (factor - high.astype(F32)).astype(BF16)
        tile = split[spot]
        return dot_t(jnp.concatenate([high, low], 1), jnp.concatenate([tile, tile], 1))

    def cluster(c, buffer, after, after_buffer):
        sums = None
        for pair in range(SLOTS // 2):
            prepare(after, after_buffer, pair)
            for k in (2 * pair, 2 * pair + 1):
                term = pull(c, buffer, k)
                sums = term if sums is None else sums + term
        sums = jnp.transpose(sums)
        sums = sums[0:16] + sums[16:32] + sums[32:48]
        here = table[c]
        own = plain[c]
        acc = STIFFNESS * (sums[ROW_Y:ROW_Y + 3] - here[ROW_Y:ROW_Y + 3] * sums[ROW_ONE:ROW_ONE + 1])
        state_rows[c, 0:6] = own[0:6]
        state_rows[c, 6:9] = own[6:9] + 0.5 * TIME_STEP * acc
        state_rows[c, 9:12] = acc
        state_rows[c, 12:16] = own[12:16]

    tag_copies = [
        pltpu.make_async_copy(table.at[TAGS_AT[side]], tags.at[side], tag_sem.at[side]) for side in range(2)
    ]

    def send_pack(e, carry):
        c = leaver(e)
        pack[e, 0:16] = table[c]
        for k in range(SLOTS):
            spot = partner(c, k)
            pack[e, 16 + 8 * k:24 + 8 * k] = table[spot, 0:8]
            pack[e, 16 + 8 * SLOTS + k:17 + 8 * SLOTS + k] = inverse_limit(c, k, spot)
        pack[e, 16 + 9 * SLOTS:PACK_ROWS] = jnp.zeros((8 - SLOTS, POINTS), F32)
        pack_copy(e).start()
        return carry

    def nth(i):
        inner = 5 + lax.rem(i, 2) + 4 * (i // 2)
        side = 4 + 4 * ((i - 8) // 2) + 3 * lax.rem(i, 2)
        return jnp.where(i < 4, inner, jnp.where(i < 8, i - 4, jnp.where(i < 12, side, i)))

    for pair in range(SLOTS // 2):
        prepare(nth(0), 0, pair)

    def two(i, carry):
        @pl.when(i == 1)
        def _():
            for copy in halos:
                copy.wait()
            for copy in tag_copies:
                copy.start()
            lax.fori_loop(CLUSTERS, TILES, split_tile, 0, unroll=2)
            lax.fori_loop(0, 4, send_pack, 0)
            lax.fori_loop(2, 4, send_hist, 0)

        first, second = nth(2 * i), nth(2 * i + 1)
        cluster(first, 0, second, 1)
        cluster(second, 1, nth(jnp.minimum(2 * i + 2, CLUSTERS - 1)), 0)
        return carry

    lax.fori_loop(0, CLUSTERS // 2, two, 0)

    def send_state(e, carry):
        sent_state[e] = state_rows[leaver(e)]
        state_copy(e).start()
        return carry

    lax.fori_loop(0, 4, send_state, 0)

    tail = jnp.where(lax.broadcasted_iota(jnp.int32, (8, POINTS), 0) == ROW_ONE - 8, 1.0, 0.0)

    def expect(e, carry):
        pack_copy(e).wait()
        own = jnp.concatenate(split_parts(packed[e, 0:16]), 0)
        mine = left_rows(own, 2)[:, 0:96]
        for pair in range(SLOTS // 2):
            theirs = []
            for k in (2 * pair, 2 * pair + 1):
                tile = jnp.concatenate([packed[e, 16 + 8 * k:24 + 8 * k], tail], 0)
                theirs.append(right_side(jnp.concatenate(split_parts(tile), 0)))
            forms_in[e, pair] = dot(mine, jnp.concatenate(theirs, 1))
        return carry

    lax.fori_loop(0, 4, expect, 0, unroll=2)

    for copy in tag_copies:
        copy.wait()
    for o in range(CLUSTERS):
        source = o
        for e in range(4):
            source = jnp.where(tags[e % 2, 8 * (e // 2), 0] == float(o), CLUSTERS + e, source)
        sources[o] = source

    def arrive(e, carry):
        hist_copy(e).wait()
        for k in range(SLOTS):
            pair, at = k // 2, pl.ds((k % 2) * POINTS, POINTS)
            rest_sq = forms_in[e, pair, 0:POINTS, at]
            if k == 0:
                rest_sq = rest_sq + apart[...]
            now_sq = jnp.maximum(rest_sq + forms_in[e, pair, POINTS:2 * POINTS, at], TINY)
            stretch = now_sq * lax.rsqrt(now_sq) * lax.rsqrt(rest_sq) - 1.0
            scaled = stretch * packed[e, 16 + 8 * SLOTS + k:17 + 8 * SLOTS + k]
            if k == 0:
                scaled = scaled - apart[...]
            hist_rows[CLUSTERS + e, k] = jnp.maximum(hist_rows[CLUSTERS + e, k], scaled)
        return carry

    lax.fori_loop(0, 4, arrive, 0)

    for e in range(4):
        state_copy(e).wait()


def place_kernel(hist_rows, state_rows, state_in, sources, ref_out, disp_out, vel_out, acc_out, hist_out, states, state_sem, sem):
    copies = []
    for o in range(CLUSTERS):
        copies.append(pltpu.make_async_copy(hist_rows.at[sources[o]], hist_out.at[o], sem.at[o]))
        copies[-1].start()
    for o in range(CLUSTERS):
        source = sources[o]
        rows = jnp.where(source < CLUSTERS, state_rows[o], state_in[jnp.maximum(source - CLUSTERS, 0)])
        for f in range(4):
            for d in range(3):
                states[f, d, o // CN, o % CN:o % CN + 1] = rows[3 * f + d:3 * f + d + 1]
    for f, ref in enumerate((ref_out, disp_out, vel_out, acc_out)):
        copies.append(pltpu.make_async_copy(states.at[f], ref, state_sem.at[f]))
        copies[-1].start()
    for copy in copies:
        copy.wait()


def per_device(
    wide_size, narrow_size,
    ref_local, displacement, velocity, acceleration, history, critical, active, partners, move_src, move_dst,
):
    vmem, smem, anywhere = (pl.BlockSpec(memory_space=m) for m in (pltpu.VMEM, pltpu.SMEM, pl.ANY))
    total = CLUSTERS + 4
    hist_shape = (total, SLOTS, POINTS, POINTS)
    operands = [
        ref_local, displacement, velocity, acceleration, critical, active, partners, move_src, move_dst,
        jnp.asarray(pairing(), BF16), history.reshape(CLUSTERS, SLOTS, POINTS, POINTS),
    ]
    operands = [pltpu.with_memory_space_constraint(x, pltpu.HBM) for x in operands]
    hist_rows, state_rows, state_in, sources = pl.pallas_call(
        functools.partial(step_kernel, wide_size, narrow_size),
        out_shape=(
            pltpu.VMEM(hist_shape, F32),
            pltpu.VMEM((CLUSTERS, 16, POINTS), F32),
            pltpu.VMEM((4, 16, POINTS), F32),
            pltpu.SMEM((CLUSTERS,), jnp.int32),
        ),
        in_specs=[anywhere] * len(operands),
        out_specs=(vmem, vmem, vmem, smem),
        scratch_shapes=[
            pltpu.VMEM((CLUSTERS, SLOTS, POINTS, POINTS), F32),
            *[pltpu.VMEM(ref_local.shape, F32)] * 4,
            pltpu.SMEM(critical.shape, F32),
            pltpu.SMEM(active.shape, jnp.int32),
            pltpu.SMEM(partners.shape, jnp.int32),
            pltpu.SMEM(move_src.shape, jnp.int32),
            pltpu.SMEM(move_dst.shape, jnp.int32),
            pltpu.VMEM((48, 3 * POINTS), BF16),
            pltpu.SMEM(((CW + 2) * (CN + 2),), jnp.int32),
            pltpu.VMEM((CLUSTERS, 16, POINTS), F32),
            pltpu.VMEM((TILES + 1, 16, POINTS), F32),
            pltpu.VMEM((TILES - CLUSTERS, 16, POINTS), F32),
            pltpu.VMEM((TILES + 1, 48, POINTS), BF16),
            pltpu.VMEM((CLUSTERS, 3 * POINTS, 128), BF16),
            pltpu.VMEM((2, SLOTS // 2, 3 * POINTS, 2 * POINTS), F32),
            pltpu.VMEM((4, SLOTS // 2, 2 * POINTS, 2 * POINTS), F32),
            pltpu.VMEM((POINTS, POINTS), F32),
            pltpu.SMEM((2, 16, POINTS), F32),
            pltpu.VMEM((4, SLOTS, POINTS, POINTS), F32),
            pltpu.VMEM((4, PACK_ROWS, POINTS), F32),
            pltpu.VMEM((4, PACK_ROWS, POINTS), F32),
            pltpu.VMEM((4, 16, POINTS), F32),
            pltpu.SemaphoreType.DMA((10,)),
            pltpu.SemaphoreType.DMA((2,)),
            pltpu.SemaphoreType.DMA((CLUSTERS,)),
            pltpu.SemaphoreType.DMA((8,)),
            pltpu.SemaphoreType.DMA((8,)),
            *[pltpu.SemaphoreType.DMA((4,))] * 6,
        ],
        compiler_params=pltpu.CompilerParams(
            collective_id=0, has_side_effects=True, vmem_limit_bytes=26 << 20
        ),
        name="step",
    )(*operands)
    hist_rows = pltpu.with_memory_space_constraint(hist_rows, pltpu.VMEM)
    state_rows = pltpu.with_memory_space_constraint(state_rows, pltpu.VMEM)
    state_in = pltpu.with_memory_space_constraint(state_in, pltpu.VMEM)
    sources = pltpu.with_memory_space_constraint(sources, pltpu.SMEM)
    state = jax.ShapeDtypeStruct(ref_local.shape, F32)
    outs = pl.pallas_call(
        place_kernel,
        out_shape=(state,) * 4 + (jax.ShapeDtypeStruct((CLUSTERS, SLOTS, POINTS, POINTS), F32),),
        in_specs=[anywhere, vmem, vmem, smem],
        out_specs=(anywhere,) * 5,
        scratch_shapes=[
            pltpu.VMEM((4,) + ref_local.shape, F32),
            pltpu.SemaphoreType.DMA((4,)),
            pltpu.SemaphoreType.DMA((CLUSTERS,)),
        ],
        compiler_params=pltpu.CompilerParams(vmem_limit_bytes=8 << 20),
        name="place",
    )(hist_rows, state_rows, state_in, sources)
    return outs[:4] + (outs[4].reshape(history.shape),)


def solution(mesh):
    field = P(None, "wide", "narrow", None)
    blocks = P("wide", "narrow", None)
    hist = P("wide", "narrow", None, None, None)
    moves = P("wide", "narrow", None, None)
    return jax.shard_map(
        functools.partial(per_device, mesh.shape["wide"], mesh.shape["narrow"]),
        mesh=mesh,
        in_specs=(field,) * 4 + (hist,) + (blocks,) * 3 + (moves,) * 2,
        out_specs=(field,) * 4 + (hist,),
        check_vma=False,
    )
```

```python
import functools

import jax
import jax.numpy as jnp
import numpy as np
from jax import lax
from jax.experimental import pallas as pl
from jax.experimental.pallas import tpu as pltpu
from jax.sharding import PartitionSpec as P

STIFFNESS = 8.0
DAMPING = 0.8
TIME_STEP = 0.1
CELL_SPAN = 4.0
FALLOFF = float(-np.log2(np.e) / 9.0)
FAR = 1024.0
APART = 1.0e6
TINY = 1.0e-12

F32 = jnp.float32
BF16 = jnp.bfloat16
MESH = pl.DeviceIdType.MESH
CW = CN = 4
CLUSTERS = CW * CN
SLOTS = 6
POINTS = 128
TILES = CLUSTERS + 22
SIDES = ((-1, 0), (1, 0), (0, -1), (0, 1), (-1, -1), (-1, 1), (1, -1), (1, 1))
SIDE_AT = (16, 21, 26, 30, 34, 35, 36, 37)
SIDE_COUNT = (5, 5, 4, 4, 1, 1, 1, 1)
TAGS_AT = (20, 25)

ROW_R, ROW_U, ROW_V, ROW_Y, ROW_SQ, ROW_ONE = 0, 3, 8, 11, (6, 7, 14), 15
PACK_ROWS = 16 + 8 * SLOTS + 8
PARTS = ((0, 0), (1, 0), (0, 1), (1, 1), (2, 0), (0, 2))


def pairing():
    s = np.zeros((3, 128, 48), np.float32)
    for block, (q, p) in enumerate(PARTS):
        for d in range(3):
            s[0, block * 16 + ROW_R + d, p * 16 + ROW_R + d] = -2
            s[1, block * 16 + ROW_U + d, p * 16 + ROW_Y + d] = -2
            s[1, block * 16 + ROW_R + d, p * 16 + ROW_U + d] = -2
            s[2, block * 16 + ROW_Y + d, p * 16 + ROW_V + d] = -1
            s[2, block * 16 + ROW_V + d, p * 16 + ROW_Y + d] = -1
    for g in range(3):
        for part in range(3):
            s[g, PARTS.index((part, 0)) * 16 + ROW_SQ[g], ROW_ONE] = 1
            s[g, PARTS.index((0, part)) * 16 + ROW_ONE, part * 16 + ROW_SQ[g]] = 1
    return s.reshape(3 * 128, 48).T


def around(i, size):
    i = jnp.where(i < 0, i + size, i)
    return jnp.where(i >= size, i - size, i)


def dot(a, b):
    return lax.dot_general(a, b, (((1,), (0,)), ((), ())), preferred_element_type=F32)


def dot_t(a, b):
    return lax.dot_general(a, b, (((1,), (1,)), ((), ())), preferred_element_type=F32)


def tile_index(i, j):
    if 0 <= i < CW and 0 <= j < CN:
        return i * CN + j
    if 0 <= j < CN:
        return (16 if i < 0 else 21) + j
    if 0 <= i < CW:
        return (26 if j < 0 else 30) + i
    return 34 + 2 * (i > 0) + (j > 0)


def step_kernel(
    wide_size, narrow_size,
    ref_hbm, disp_hbm, vel_hbm, acc_hbm, critical_hbm, active_hbm, partners_hbm, src_hbm, dst_hbm, pairs_hbm, history,
    hist_rows, state_rows, state_in, sources,
    held_0, held_1, held_2, held_3, held_4, held_5, ref_local, displacement, velocity, acceleration, critical, active, partners, move_src, move_dst, pairs, where_is,
    plain, table, leaving, split, left, forms, forms_in, apart, tags, raw, pack, packed, sent_state,
    small_sem, tag_sem, load_sem, halo_send, halo_recv, hist_send, hist_recv, pack_send, pack_recv, state_send, state_recv,
):
    held = (held_0, held_1, held_2, held_3, held_4, held_5)
    me_w, me_n = lax.axis_index("wide"), lax.axis_index("narrow")
    small = [
        pltpu.make_async_copy(source, target, small_sem.at[n])
        for n, (source, target) in enumerate((
            (ref_hbm, ref_local), (disp_hbm, displacement), (vel_hbm, velocity), (acc_hbm, acceleration),
            (dst_hbm, move_dst), (pairs_hbm, pairs), (critical_hbm, critical), (active_hbm, active), (partners_hbm, partners),
            (src_hbm, move_src),
        ))
    ]
    for copy in small:
        copy.start()
    loads = [pltpu.make_async_copy(history.at[:, k], held[k], load_sem.at[k]) for k in range(SLOTS)]
    for copy in loads:
        copy.start()

    def device(dw, dn):
        return (around(me_w + dw, wide_size), around(me_n + dn, narrow_size))

    barrier = pltpu.get_barrier_semaphore()
    for dw, dn in SIDES:
        pl.semaphore_signal(barrier, inc=1, device_id=device(dw, dn), device_id_type=MESH)

    sub = lax.broadcasted_iota(jnp.int32, (POINTS, POINTS), 0)
    lane = lax.broadcasted_iota(jnp.int32, (POINTS, POINTS), 1)
    apart[...] = jnp.where(sub == lane, APART, 0.0).astype(F32)
    row = lax.broadcasted_iota(jnp.int32, (16, POINTS), 0)
    far = jnp.where((row == ROW_R) | (row == ROW_Y), FAR, 0.0)
    far = jnp.where(row == ROW_SQ[0], FAR * FAR, far)
    table[TILES] = jnp.where(row == ROW_ONE, 1.0, far)
    for i in range(CW + 2):
        for j in range(CN + 2):
            edges = [
                edge for out, edge in (
                    (i == 0, me_w == 0), (i == CW + 1, me_w == wide_size - 1),
                    (j == 0, me_n == 0), (j == CN + 1, me_n == narrow_size - 1),
                ) if out
            ]
            spot = tile_index(i - 1, j - 1)
            for edge in edges:
                spot = jnp.where(edge, TILES, spot)
            where_is[i * (CN + 2) + j] = spot

    for copy in small[:5]:
        copy.wait()
    column = lax.broadcasted_iota(jnp.int32, (CN, POINTS), 0)
    anchor_n = column.astype(F32) * CELL_SPAN - CELL_SPAN * CN / 2
    hop_n = jnp.where(column == 0, CELL_SPAN * CN, jnp.where(column == CN - 1, -CELL_SPAN * CN, 0.0))

    def advanced(a):
        base, u, half, v = [], [], [], []
        for d in range(3):
            speed, push = velocity[d, a], acceleration[d, a]
            base.append(ref_local[d, a])
            u.append(displacement[d, a] + TIME_STEP * speed + 0.5 * TIME_STEP * TIME_STEP * push)
            half.append(speed + 0.5 * TIME_STEP * push)
            v.append(half[d] * (DAMPING / STIFFNESS))
        return base, u, half, v

    def tile_rows(a, up_w, up_n, base, u, v):
        r = [base[0] + (CELL_SPAN * (a - CW / 2) + up_w), base[1] + (anchor_n + up_n), base[2] - CELL_SPAN]
        y = [r[d] + u[d] for d in range(3)]
        squares = [
            r[0] * r[0] + r[1] * r[1] + r[2] * r[2],
            u[0] * (r[0] + y[0]) + u[1] * (r[1] + y[1]) + u[2] * (r[2] + y[2]),
            v[0] * y[0] + v[1] * y[1] + v[2] * y[2],
        ]
        return r + u + squares[:2] + v + y + squares[2:] + [jnp.ones_like(u[0])]

    for a in range(CW):
        base, u, half, v = advanced(a)
        for f, row in enumerate(tile_rows(a, 0.0, hop_n, base, u, v)):
            leaving[SIDE_AT[2] - CLUSTERS + a, f:f + 1] = row[0:1]
            leaving[SIDE_AT[3] - CLUSTERS + a, f:f + 1] = row[CN - 1:CN]
        if a in (0, CW - 1):
            side, hop_w = (0, CELL_SPAN * CW) if a == 0 else (1, -CELL_SPAN * CW)
            at = SIDE_AT[side] - CLUSTERS
            for f, row in enumerate(tile_rows(a, hop_w, 0.0, base, u, v)):
                leaving[at:at + CN, f] = row
            at = SIDE_AT[4 + 2 * side] - CLUSTERS
            for f, row in enumerate(tile_rows(a, hop_w, hop_n, base, u, v)):
                leaving[at, f:f + 1] = row[0:1]
                leaving[at + 1, f:f + 1] = row[CN - 1:CN]
    for side in range(2):
        for m in range(2):
            tag = jnp.full((8, POINTS), move_dst[0, 0, 1 - side, m], jnp.int32).astype(F32)
            leaving[TAGS_AT[side] - CLUSTERS, 8 * m:8 * m + 8] = tag

    pl.semaphore_wait(barrier, len(SIDES))
    halos = []
    for n, (dw, dn) in enumerate(SIDES):
        landing = SIDE_AT[SIDES.index((-dw, -dn))]
        halos.append(pltpu.make_async_remote_copy(
            src_ref=leaving.at[pl.ds(SIDE_AT[n] - CLUSTERS, SIDE_COUNT[n])],
            dst_ref=table.at[pl.ds(landing, SIDE_COUNT[n])],
            send_sem=halo_send.at[n], recv_sem=halo_recv.at[n],
            device_id=device(dw, dn), device_id_type=MESH,
        ))
    for copy in halos:
        copy.start()

    def split_parts(tile):
        high = tile.astype(BF16)
        rest = tile - high.astype(F32)
        middle = rest.astype(BF16)
        return high, middle, (rest - middle.astype(F32)).astype(BF16)

    def split_tile(t, carry):
        for n, part in enumerate(split_parts(table[t])):
            split[t, n * 16:n * 16 + 16] = part
        return carry

    def toward(e):
        return device(1 - 2 * lax.rem(e, 2), 0)

    def hist_copy(e, k):
        return pltpu.make_async_remote_copy(
            src_ref=raw.at[e, k], dst_ref=hist_rows.at[CLUSTERS + e, k],
            send_sem=hist_send.at[e, k], recv_sem=hist_recv.at[e, k],
            device_id=toward(e), device_id_type=MESH,
        )

    def pack_copy(e):
        return pltpu.make_async_remote_copy(
            src_ref=pack.at[e], dst_ref=packed.at[e], send_sem=pack_send.at[e], recv_sem=pack_recv.at[e],
            device_id=toward(e), device_id_type=MESH,
        )

    def state_copy(e):
        return pltpu.make_async_remote_copy(
            src_ref=sent_state.at[e], dst_ref=state_in.at[e],
            send_sem=state_send.at[e], recv_sem=state_recv.at[e],
            device_id=toward(e), device_id_type=MESH,
        )

    def leaver(e):
        return jnp.maximum(move_src[0, 0, lax.rem(e, 2), e // 2], 0)

    for copy in small[5:]:
        copy.wait()

    def send_hist(e, k):
        raw[e, k] = held[k][leaver(e)]
        hist_copy(e, k).start()

    def send_first(k):
        loads[k].wait()
        for e in range(2):
            send_hist(e, k)

    send_first(0)
    send_first(1)
    for a in range(CW):
        base, u, half, v = advanced(a)
        here = pl.ds(a * CN, CN)
        for f, row in enumerate(base + u + half):
            plain[here, f] = row
        for f in range(9, 16):
            plain[here, f] = jnp.zeros((CN, POINTS), F32)
        for f, row in enumerate(tile_rows(a, 0.0, 0.0, base, u, v)):
            table[here, f] = row

    lax.fori_loop(0, CLUSTERS, split_tile, 0, unroll=4)
    split_tile(TILES, 0)
    send_first(2)
    send_first(3)

    def left_rows(parts, count):
        turned = jnp.transpose(parts.astype(F32)).astype(BF16)
        wide = dot(turned, pairs[:, 0:count * POINTS]).astype(BF16)
        return jnp.concatenate([wide[:, g * POINTS:(g + 1) * POINTS] for g in range(count)], 0)

    def left_side(c, carry):
        left[c] = left_rows(split[c], 3)
        return carry

    lax.fori_loop(0, CLUSTERS, left_side, 0, unroll=4)
    send_first(4)
    send_first(5)

    def place_of(c):
        a = lax.shift_right_logical(c, 2)
        return a, c - CN * a

    def partner(c, k):
        a, b = place_of(c)
        o = partners[a, b, k]
        third = lax.shift_right_logical(o * 11, 5)
        spot = where_is[(CN + 2) * (a + third) + b + o - 3 * third]
        return jnp.where(active[a, b, k] > 0, spot, TILES)

    def inverse_limit(c, k, spot):
        a, b = place_of(c)
        return jnp.where(spot == TILES, 0.0, 1.0) / jnp.full((1, POINTS), critical[a, b, k], F32)

    def right_side(tile):
        return jnp.concatenate([tile[q * 16:q * 16 + 16] for q, _ in PARTS], 0)

    def prepare(c, buffer, pair):
        theirs = [right_side(split[partner(c, k)]) for k in (2 * pair, 2 * pair + 1)]
        forms[buffer, pair] = dot(left[c, :, 0:96], jnp.concatenate(theirs, 1))

    def pull(c, buffer, k):
        pair, at = k // 2, pl.ds((k % 2) * POINTS, POINTS)
        spot = partner(c, k)
        rest_sq = forms[buffer, pair, 0:POINTS, at]
        if k == 0:
            rest_sq = rest_sq + apart[...]
        now_sq = jnp.maximum(rest_sq + forms[buffer, pair, POINTS:2 * POINTS, at], TINY)
        rate = forms[buffer, pair, 2 * POINTS:3 * POINTS, at]
        now_inv = lax.rsqrt(now_sq)
        stretch = now_sq * now_inv * lax.rsqrt(rest_sq) - 1.0
        scaled = stretch * inverse_limit(c, k, spot)
        if k == 0:
            scaled = scaled - apart[...]
        hist = jnp.maximum(held[k][c], scaled)
        hist_rows[c, k] = hist
        weight = jnp.exp2(rest_sq * FALLOFF) * jnp.minimum(jnp.maximum(2.0 - hist, 0.0), 1.0)
        factor = weight * (stretch + rate * now_inv) * now_inv
        high = factor.astype(BF16)
        low = (factor - high.astype(F32)).astype(BF16)
        tile = split[spot]
        return dot_t(jnp.concatenate([high, low], 1), jnp.concatenate([tile, tile], 1))

    def cluster(c, buffer, after, after_buffer):
        sums = None
        for pair in range(SLOTS // 2):
            prepare(after, after_buffer, pair)
            for k in (2 * pair, 2 * pair + 1):
                term = pull(c, buffer, k)
                sums = term if sums is None else sums + term
        sums = jnp.transpose(sums)
        sums = sums[0:16] + sums[16:32] + sums[32:48]
        here = table[c]
        own = plain[c]
        acc = STIFFNESS * (sums[ROW_Y:ROW_Y + 3] - here[ROW_Y:ROW_Y + 3] * sums[ROW_ONE:ROW_ONE + 1])
        state_rows[c, 0:6] = own[0:6]
        state_rows[c, 6:9] = own[6:9] + 0.5 * TIME_STEP * acc
        state_rows[c, 9:12] = acc
        state_rows[c, 12:16] = own[12:16]

    tag_copies = [
        pltpu.make_async_copy(table.at[TAGS_AT[side]], tags.at[side], tag_sem.at[side]) for side in range(2)
    ]

    def send_pack(e, carry):
        c = leaver(e)
        pack[e, 0:16] = table[c]
        for k in range(SLOTS):
            spot = partner(c, k)
            pack[e, 16 + 8 * k:24 + 8 * k] = table[spot, 0:8]
            pack[e, 16 + 8 * SLOTS + k:17 + 8 * SLOTS + k] = inverse_limit(c, k, spot)
        pack[e, 16 + 9 * SLOTS:PACK_ROWS] = jnp.zeros((8 - SLOTS, POINTS), F32)
        pack_copy(e).start()
        return carry

    def nth(i):
        inner = 5 + lax.rem(i, 2) + 4 * (i // 2)
        side = 4 + 4 * ((i - 8) // 2) + 3 * lax.rem(i, 2)
        return jnp.where(i < 4, inner, jnp.where(i < 8, i - 4, jnp.where(i < 12, side, i)))

    for pair in range(SLOTS // 2):
        prepare(nth(0), 0, pair)

    def two(i, carry):
        @pl.when(i == 1)
        def _():
            for copy in halos:
                copy.wait()
            for copy in tag_copies:
                copy.start()
            lax.fori_loop(CLUSTERS, TILES, split_tile, 0, unroll=2)
            lax.fori_loop(0, 4, send_pack, 0)

            def send_second(e, carry):
                for k in range(SLOTS):
                    send_hist(e, k)
                return carry

            lax.fori_loop(2, 4, send_second, 0)

        first, second = nth(2 * i), nth(2 * i + 1)
        cluster(first, 0, second, 1)
        cluster(second, 1, nth(jnp.minimum(2 * i + 2, CLUSTERS - 1)), 0)
        return carry

    lax.fori_loop(0, CLUSTERS // 2, two, 0)

    def send_state(e, carry):
        sent_state[e] = state_rows[leaver(e)]
        state_copy(e).start()
        return carry

    lax.fori_loop(0, 4, send_state, 0)

    tail = jnp.where(lax.broadcasted_iota(jnp.int32, (8, POINTS), 0) == ROW_ONE - 8, 1.0, 0.0)

    def expect(e, carry):
        pack_copy(e).wait()
        own = jnp.concatenate(split_parts(packed[e, 0:16]), 0)
        mine = left_rows(own, 2)[:, 0:96]
        for pair in range(SLOTS // 2):
            theirs = []
            for k in (2 * pair, 2 * pair + 1):
                tile = jnp.concatenate([packed[e, 16 + 8 * k:24 + 8 * k], tail], 0)
                theirs.append(right_side(jnp.concatenate(split_parts(tile), 0)))
            forms_in[e, pair] = dot(mine, jnp.concatenate(theirs, 1))
        return carry

    lax.fori_loop(0, 4, expect, 0, unroll=2)

    for copy in tag_copies:
        copy.wait()
    for o in range(CLUSTERS):
        source = o
        for e in range(4):
            source = jnp.where(tags[e % 2, 8 * (e // 2), 0] == float(o), CLUSTERS + e, source)
        sources[o] = source

    def arrive(e, carry):
        for k in range(SLOTS):
            hist_copy(e, k).wait()
            pair, at = k // 2, pl.ds((k % 2) * POINTS, POINTS)
            rest_sq = forms_in[e, pair, 0:POINTS, at]
            if k == 0:
                rest_sq = rest_sq + apart[...]
            now_sq = jnp.maximum(rest_sq + forms_in[e, pair, POINTS:2 * POINTS, at], TINY)
            stretch = now_sq * lax.rsqrt(now_sq) * lax.rsqrt(rest_sq) - 1.0
            scaled = stretch * packed[e, 16 + 8 * SLOTS + k:17 + 8 * SLOTS + k]
            if k == 0:
                scaled = scaled - apart[...]
            hist_rows[CLUSTERS + e, k] = jnp.maximum(hist_rows[CLUSTERS + e, k], scaled)
        return carry

    lax.fori_loop(0, 4, arrive, 0)

    for e in range(4):
        state_copy(e).wait()


def place_kernel(hist_rows, state_rows, state_in, sources, ref_out, disp_out, vel_out, acc_out, hist_out, states, state_sem, sem):
    copies = []
    for o in range(CLUSTERS):
        copies.append(pltpu.make_async_copy(hist_rows.at[sources[o]], hist_out.at[o], sem.at[o]))
        copies[-1].start()
    for o in range(CLUSTERS):
        source = sources[o]
        rows = jnp.where(source < CLUSTERS, state_rows[o], state_in[jnp.maximum(source - CLUSTERS, 0)])
        for f in range(4):
            for d in range(3):
                states[f, d, o // CN, o % CN:o % CN + 1] = rows[3 * f + d:3 * f + d + 1]
    for f, ref in enumerate((ref_out, disp_out, vel_out, acc_out)):
        copies.append(pltpu.make_async_copy(states.at[f], ref, state_sem.at[f]))
        copies[-1].start()
    for copy in copies:
        copy.wait()


def per_device(
    wide_size, narrow_size,
    ref_local, displacement, velocity, acceleration, history, critical, active, partners, move_src, move_dst,
):
    vmem, smem, anywhere = (pl.BlockSpec(memory_space=m) for m in (pltpu.VMEM, pltpu.SMEM, pl.ANY))
    total = CLUSTERS + 4
    hist_shape = (total, SLOTS, POINTS, POINTS)
    operands = [
        ref_local, displacement, velocity, acceleration, critical, active, partners, move_src, move_dst,
        jnp.asarray(pairing(), BF16), history.reshape(CLUSTERS, SLOTS, POINTS, POINTS),
    ]
    operands = [pltpu.with_memory_space_constraint(x, pltpu.HBM) for x in operands]
    hist_rows, state_rows, state_in, sources = pl.pallas_call(
        functools.partial(step_kernel, wide_size, narrow_size),
        out_shape=(
            pltpu.VMEM(hist_shape, F32),
            pltpu.VMEM((CLUSTERS, 16, POINTS), F32),
            pltpu.VMEM((4, 16, POINTS), F32),
            pltpu.SMEM((CLUSTERS,), jnp.int32),
        ),
        in_specs=[anywhere] * len(operands),
        out_specs=(vmem, vmem, vmem, smem),
        scratch_shapes=[
            *[pltpu.VMEM((CLUSTERS, POINTS, POINTS), F32)] * SLOTS,
            *[pltpu.VMEM(ref_local.shape, F32)] * 4,
            pltpu.SMEM(critical.shape, F32),
            pltpu.SMEM(active.shape, jnp.int32),
            pltpu.SMEM(partners.shape, jnp.int32),
            pltpu.SMEM(move_src.shape, jnp.int32),
            pltpu.SMEM(move_dst.shape, jnp.int32),
            pltpu.VMEM((48, 3 * POINTS), BF16),
            pltpu.SMEM(((CW + 2) * (CN + 2),), jnp.int32),
            pltpu.VMEM((CLUSTERS, 16, POINTS), F32),
            pltpu.VMEM((TILES + 1, 16, POINTS), F32),
            pltpu.VMEM((TILES - CLUSTERS, 16, POINTS), F32),
            pltpu.VMEM((TILES + 1, 48, POINTS), BF16),
            pltpu.VMEM((CLUSTERS, 3 * POINTS, 128), BF16),
            pltpu.VMEM((2, SLOTS // 2, 3 * POINTS, 2 * POINTS), F32),
            pltpu.VMEM((4, SLOTS // 2, 2 * POINTS, 2 * POINTS), F32),
            pltpu.VMEM((POINTS, POINTS), F32),
            pltpu.SMEM((2, 16, POINTS), F32),
            pltpu.VMEM((4, SLOTS, POINTS, POINTS), F32),
            pltpu.VMEM((4, PACK_ROWS, POINTS), F32),
            pltpu.VMEM((4, PACK_ROWS, POINTS), F32),
            pltpu.VMEM((4, 16, POINTS), F32),
            pltpu.SemaphoreType.DMA((10,)),
            pltpu.SemaphoreType.DMA((2,)),
            pltpu.SemaphoreType.DMA((SLOTS,)),
            pltpu.SemaphoreType.DMA((8,)),
            pltpu.SemaphoreType.DMA((8,)),
            *[pltpu.SemaphoreType.DMA((4, SLOTS))] * 2,
            *[pltpu.SemaphoreType.DMA((4,))] * 4,
        ],
        compiler_params=pltpu.CompilerParams(
            collective_id=0, has_side_effects=True, vmem_limit_bytes=26 << 20
        ),
        name="step",
    )(*operands)
    hist_rows = pltpu.with_memory_space_constraint(hist_rows, pltpu.VMEM)
    state_rows = pltpu.with_memory_space_constraint(state_rows, pltpu.VMEM)
    state_in = pltpu.with_memory_space_constraint(state_in, pltpu.VMEM)
    sources = pltpu.with_memory_space_constraint(sources, pltpu.SMEM)
    state = jax.ShapeDtypeStruct(ref_local.shape, F32)
    outs = pl.pallas_call(
        place_kernel,
        out_shape=(state,) * 4 + (jax.ShapeDtypeStruct((CLUSTERS, SLOTS, POINTS, POINTS), F32),),
        in_specs=[anywhere, vmem, vmem, smem],
        out_specs=(anywhere,) * 5,
        scratch_shapes=[
            pltpu.VMEM((4,) + ref_local.shape, F32),
            pltpu.SemaphoreType.DMA((4,)),
            pltpu.SemaphoreType.DMA((CLUSTERS,)),
        ],
        compiler_params=pltpu.CompilerParams(vmem_limit_bytes=8 << 20),
        name="place",
    )(hist_rows, state_rows, state_in, sources)
    return outs[:4] + (outs[4].reshape(history.shape),)


def solution(mesh):
    field = P(None, "wide", "narrow", None)
    blocks = P("wide", "narrow", None)
    hist = P("wide", "narrow", None, None, None)
    moves = P("wide", "narrow", None, None)
    return jax.shard_map(
        functools.partial(per_device, mesh.shape["wide"], mesh.shape["narrow"]),
        mesh=mesh,
        in_specs=(field,) * 4 + (hist,) + (blocks,) * 3 + (moves,) * 2,
        out_specs=(field,) * 4 + (hist,),
        check_vma=False,
    )
```

```python
import functools

import jax
import jax.numpy as jnp
import numpy as np
from jax import lax
from jax.experimental import pallas as pl
from jax.experimental.pallas import tpu as pltpu
from jax.sharding import PartitionSpec as P

STIFFNESS = 8.0
DAMPING = 0.8
TIME_STEP = 0.1
CELL_SPAN = 4.0
FALLOFF = float(-np.log2(np.e) / 9.0)
FAR = 1024.0
APART = 1.0e6
TINY = 1.0e-12

F32 = jnp.float32
BF16 = jnp.bfloat16
MESH = pl.DeviceIdType.MESH
CW = CN = 4
CLUSTERS = CW * CN
SLOTS = 6
POINTS = 128
TILES = CLUSTERS + 22
SIDES = ((-1, 0), (1, 0), (0, -1), (0, 1), (-1, -1), (-1, 1), (1, -1), (1, 1))
SIDE_AT = (16, 21, 26, 30, 34, 35, 36, 37)
SIDE_COUNT = (5, 5, 4, 4, 1, 1, 1, 1)
TAGS_AT = (20, 25)

ROW_R, ROW_U, ROW_V, ROW_Y, ROW_SQ, ROW_ONE = 0, 3, 8, 11, (6, 7, 14), 15
PACK_ROWS = 16 + 8 * SLOTS + 8
PARTS = ((0, 0), (1, 0), (0, 1), (1, 1), (2, 0), (0, 2))


def pairing():
    s = np.zeros((3, 128, 48), np.float32)
    for block, (q, p) in enumerate(PARTS):
        for d in range(3):
            s[0, block * 16 + ROW_R + d, p * 16 + ROW_R + d] = -2
            s[1, block * 16 + ROW_U + d, p * 16 + ROW_Y + d] = -2
            s[1, block * 16 + ROW_R + d, p * 16 + ROW_U + d] = -2
            s[2, block * 16 + ROW_Y + d, p * 16 + ROW_V + d] = -1
            s[2, block * 16 + ROW_V + d, p * 16 + ROW_Y + d] = -1
    for g in range(3):
        for part in range(3):
            s[g, PARTS.index((part, 0)) * 16 + ROW_SQ[g], ROW_ONE] = 1
            s[g, PARTS.index((0, part)) * 16 + ROW_ONE, part * 16 + ROW_SQ[g]] = 1
    return s.reshape(3 * 128, 48).T


def dot(a, b):
    return lax.dot_general(a, b, (((1,), (0,)), ((), ())), preferred_element_type=F32)


def dot_t(a, b):
    return lax.dot_general(a, b, (((1,), (1,)), ((), ())), preferred_element_type=F32)


def tile_index(i, j):
    if 0 <= i < CW and 0 <= j < CN:
        return i * CN + j
    if 0 <= j < CN:
        return (16 if i < 0 else 21) + j
    if 0 <= i < CW:
        return (26 if j < 0 else 30) + i
    return 34 + 2 * (i > 0) + (j > 0)


def step_kernel(
    wide_size, narrow_size,
    ref_hbm, disp_hbm, vel_hbm, acc_hbm, critical_hbm, active_hbm, partners_hbm, src_hbm, dst_hbm, pairs_hbm, history,
    hist_rows, state_rows, state_in, sources,
    held_0, held_1, held_2, held_3, held_4, held_5, ref_local, displacement, velocity, acceleration, critical, active, partners, move_src, move_dst, pairs, where_is,
    plain, table, leaving, split, left, forms, forms_in, apart, tags, raw, pack, packed, sent_state,
    small_sem, tag_sem, load_sem, halo_send, halo_recv, hist_send, hist_recv, pack_send, pack_recv, state_send, state_recv,
):
    held = (held_0, held_1, held_2, held_3, held_4, held_5)
    me_w, me_n = lax.axis_index("wide"), lax.axis_index("narrow")
    small = [
        pltpu.make_async_copy(source, target, small_sem.at[n])
        for n, (source, target) in enumerate((
            (ref_hbm, ref_local), (disp_hbm, displacement), (vel_hbm, velocity), (acc_hbm, acceleration),
            (dst_hbm, move_dst), (pairs_hbm, pairs), (critical_hbm, critical), (active_hbm, active), (partners_hbm, partners),
            (src_hbm, move_src),
        ))
    ]
    for copy in small:
        copy.start()
    loads = [pltpu.make_async_copy(history.at[:, k], held[k], load_sem.at[k]) for k in range(SLOTS)]
    for copy in loads:
        copy.start()

    def device(dw, dn):
        return (me_w + dw, me_n + dn)

    at_edge = {-1: (me_w == 0, me_n == 0), 1: (me_w == wide_size - 1, me_n == narrow_size - 1)}

    def beyond(dw, dn):
        out = False
        if dw:
            out = out | at_edge[dw][0]
        if dn:
            out = out | at_edge[dn][1]
        return out

    barrier = pltpu.get_barrier_semaphore()
    greeted = 0
    for dw, dn in SIDES:
        greeted = greeted + jnp.where(beyond(dw, dn), 0, 1)

        @pl.when(jnp.logical_not(beyond(dw, dn)))
        def _():
            pl.semaphore_signal(barrier, inc=1, device_id=device(dw, dn), device_id_type=MESH)

    sub = lax.broadcasted_iota(jnp.int32, (POINTS, POINTS), 0)
    lane = lax.broadcasted_iota(jnp.int32, (POINTS, POINTS), 1)
    apart[...] = jnp.where(sub == lane, APART, 0.0).astype(F32)
    row = lax.broadcasted_iota(jnp.int32, (16, POINTS), 0)
    far = jnp.where((row == ROW_R) | (row == ROW_Y), FAR, 0.0)
    far = jnp.where(row == ROW_SQ[0], FAR * FAR, far)
    table[TILES] = jnp.where(row == ROW_ONE, 1.0, far)
    for i in range(CW + 2):
        for j in range(CN + 2):
            out = beyond((i == CW + 1) - (i == 0), (j == CN + 1) - (j == 0))
            where_is[i * (CN + 2) + j] = jnp.where(out, TILES, tile_index(i - 1, j - 1))

    for copy in small[:5]:
        copy.wait()
    column = lax.broadcasted_iota(jnp.int32, (CN, POINTS), 0)
    anchor_n = column.astype(F32) * CELL_SPAN - CELL_SPAN * CN / 2
    hop_n = jnp.where(column == 0, CELL_SPAN * CN, jnp.where(column == CN - 1, -CELL_SPAN * CN, 0.0))

    def advanced(a):
        base, u, half, v = [], [], [], []
        for d in range(3):
            speed, push = velocity[d, a], acceleration[d, a]
            base.append(ref_local[d, a])
            u.append(displacement[d, a] + TIME_STEP * speed + 0.5 * TIME_STEP * TIME_STEP * push)
            half.append(speed + 0.5 * TIME_STEP * push)
            v.append(half[d] * (DAMPING / STIFFNESS))
        return base, u, half, v

    def tile_rows(a, up_w, up_n, base, u, v):
        r = [base[0] + (CELL_SPAN * (a - CW / 2) + up_w), base[1] + (anchor_n + up_n), base[2] - CELL_SPAN]
        y = [r[d] + u[d] for d in range(3)]
        squares = [
            r[0] * r[0] + r[1] * r[1] + r[2] * r[2],
            u[0] * (r[0] + y[0]) + u[1] * (r[1] + y[1]) + u[2] * (r[2] + y[2]),
            v[0] * y[0] + v[1] * y[1] + v[2] * y[2],
        ]
        return r + u + squares[:2] + v + y + squares[2:] + [jnp.ones_like(u[0])]

    for a in range(CW):
        base, u, half, v = advanced(a)
        for f, row in enumerate(tile_rows(a, 0.0, hop_n, base, u, v)):
            leaving[SIDE_AT[2] - CLUSTERS + a, f:f + 1] = row[0:1]
            leaving[SIDE_AT[3] - CLUSTERS + a, f:f + 1] = row[CN - 1:CN]
        if a in (0, CW - 1):
            side, hop_w = (0, CELL_SPAN * CW) if a == 0 else (1, -CELL_SPAN * CW)
            at = SIDE_AT[side] - CLUSTERS
            for f, row in enumerate(tile_rows(a, hop_w, 0.0, base, u, v)):
                leaving[at:at + CN, f] = row
            at = SIDE_AT[4 + 2 * side] - CLUSTERS
            for f, row in enumerate(tile_rows(a, hop_w, hop_n, base, u, v)):
                leaving[at, f:f + 1] = row[0:1]
                leaving[at + 1, f:f + 1] = row[CN - 1:CN]
    for side in range(2):
        for m in range(2):
            tag = jnp.full((8, POINTS), move_dst[0, 0, 1 - side, m], jnp.int32).astype(F32)
            leaving[TAGS_AT[side] - CLUSTERS, 8 * m:8 * m + 8] = tag

    pl.semaphore_wait(barrier, greeted)
    halos = []
    for n, (dw, dn) in enumerate(SIDES):
        landing = SIDE_AT[SIDES.index((-dw, -dn))]
        halos.append(pltpu.make_async_remote_copy(
            src_ref=leaving.at[pl.ds(SIDE_AT[n] - CLUSTERS, SIDE_COUNT[n])],
            dst_ref=table.at[pl.ds(landing, SIDE_COUNT[n])],
            send_sem=halo_send.at[n], recv_sem=halo_recv.at[n],
            device_id=device(dw, dn), device_id_type=MESH,
        ))
    for side, copy in zip(SIDES, halos):
        pl.when(jnp.logical_not(beyond(*side)))(copy.start)
    for n in range(2):
        @pl.when(beyond(*SIDES[n]))
        def _():
            table[TAGS_AT[n]] = jnp.full((16, POINTS), -1.0, F32)


    def split_parts(tile):
        high = tile.astype(BF16)
        rest = tile - high.astype(F32)
        middle = rest.astype(BF16)
        return high, middle, (rest - middle.astype(F32)).astype(BF16)

    def split_tile(t, carry):
        for n, part in enumerate(split_parts(table[t])):
            split[t, n * 16:n * 16 + 16] = part
        return carry

    def toward(e):
        return device(1 - 2 * lax.rem(e, 2), 0)

    def goes(e):
        return jnp.logical_not(jnp.where(lax.rem(e, 2) == 0, at_edge[1][0], at_edge[-1][0]))

    def comes(e):
        return jnp.logical_not(jnp.where(lax.rem(e, 2) == 0, at_edge[-1][0], at_edge[1][0]))

    def hist_copy(e, k):
        return pltpu.make_async_remote_copy(
            src_ref=raw.at[e, k], dst_ref=hist_rows.at[CLUSTERS + e, k],
            send_sem=hist_send.at[e, k], recv_sem=hist_recv.at[e, k],
            device_id=toward(e), device_id_type=MESH,
        )

    def pack_copy(e):
        return pltpu.make_async_remote_copy(
            src_ref=pack.at[e], dst_ref=packed.at[e], send_sem=pack_send.at[e], recv_sem=pack_recv.at[e],
            device_id=toward(e), device_id_type=MESH,
        )

    def state_copy(e):
        return pltpu.make_async_remote_copy(
            src_ref=sent_state.at[e], dst_ref=state_in.at[e],
            send_sem=state_send.at[e], recv_sem=state_recv.at[e],
            device_id=toward(e), device_id_type=MESH,
        )

    def leaver(e):
        return jnp.maximum(move_src[0, 0, lax.rem(e, 2), e // 2], 0)

    for copy in small[5:]:
        copy.wait()

    def send_hist(e, k):
        raw[e, k] = held[k][leaver(e)]
        hist_copy(e, k).start()

    def send_first(k):
        loads[k].wait()
        for e in range(2):
            pl.when(goes(e))(functools.partial(send_hist, e, k))

    send_first(0)
    send_first(1)
    for a in range(CW):
        base, u, half, v = advanced(a)
        here = pl.ds(a * CN, CN)
        for f, row in enumerate(base + u + half):
            plain[here, f] = row
        for f in range(9, 16):
            plain[here, f] = jnp.zeros((CN, POINTS), F32)
        for f, row in enumerate(tile_rows(a, 0.0, 0.0, base, u, v)):
            table[here, f] = row

    lax.fori_loop(0, CLUSTERS, split_tile, 0, unroll=4)
    split_tile(TILES, 0)
    send_first(2)
    send_first(3)

    def left_rows(parts, count):
        turned = jnp.transpose(parts.astype(F32)).astype(BF16)
        wide = dot(turned, pairs[:, 0:count * POINTS]).astype(BF16)
        return jnp.concatenate([wide[:, g * POINTS:(g + 1) * POINTS] for g in range(count)], 0)

    def left_side(c, carry):
        left[c] = left_rows(split[c], 3)
        return carry

    lax.fori_loop(0, CLUSTERS, left_side, 0, unroll=4)
    send_first(4)
    send_first(5)

    def place_of(c):
        a = lax.shift_right_logical(c, 2)
        return a, c - CN * a

    def partner(c, k):
        a, b = place_of(c)
        o = partners[a, b, k]
        third = lax.shift_right_logical(o * 11, 5)
        spot = where_is[(CN + 2) * (a + third) + b + o - 3 * third]
        return jnp.where(active[a, b, k] > 0, spot, TILES)

    def inverse_limit(c, k, spot):
        a, b = place_of(c)
        return jnp.where(spot == TILES, 0.0, 1.0) / jnp.full((1, POINTS), critical[a, b, k], F32)

    def right_side(tile):
        return jnp.concatenate([tile[q * 16:q * 16 + 16] for q, _ in PARTS], 0)

    def prepare(c, buffer, pair):
        theirs = [right_side(split[partner(c, k)]) for k in (2 * pair, 2 * pair + 1)]
        forms[buffer, pair] = dot(left[c, :, 0:96], jnp.concatenate(theirs, 1))

    def pull(c, buffer, k):
        pair, at = k // 2, pl.ds((k % 2) * POINTS, POINTS)
        spot = partner(c, k)
        rest_sq = forms[buffer, pair, 0:POINTS, at]
        if k == 0:
            rest_sq = rest_sq + apart[...]
        now_sq = jnp.maximum(rest_sq + forms[buffer, pair, POINTS:2 * POINTS, at], TINY)
        rate = forms[buffer, pair, 2 * POINTS:3 * POINTS, at]
        now_inv = lax.rsqrt(now_sq)
        stretch = now_sq * now_inv * lax.rsqrt(rest_sq) - 1.0
        scaled = stretch * inverse_limit(c, k, spot)
        if k == 0:
            scaled = scaled - apart[...]
        hist = jnp.maximum(held[k][c], scaled)
        hist_rows[c, k] = hist
        weight = jnp.exp2(rest_sq * FALLOFF) * jnp.minimum(jnp.maximum(2.0 - hist, 0.0), 1.0)
        factor = weight * (stretch + rate * now_inv) * now_inv
        high = factor.astype(BF16)
        low = (factor - high.astype(F32)).astype(BF16)
        tile = split[spot]
        return dot_t(jnp.concatenate([high, low], 1), jnp.concatenate([tile, tile], 1))

    def cluster(c, buffer, after, after_buffer):
        sums = None
        for pair in range(SLOTS // 2):
            prepare(after, after_buffer, pair)
            for k in (2 * pair, 2 * pair + 1):
                term = pull(c, buffer, k)
                sums = term if sums is None else sums + term
        sums = jnp.transpose(sums)
        sums = sums[0:16] + sums[16:32] + sums[32:48]
        here = table[c]
        own = plain[c]
        acc = STIFFNESS * (sums[ROW_Y:ROW_Y + 3] - here[ROW_Y:ROW_Y + 3] * sums[ROW_ONE:ROW_ONE + 1])
        state_rows[c, 0:6] = own[0:6]
        state_rows[c, 6:9] = own[6:9] + 0.5 * TIME_STEP * acc
        state_rows[c, 9:12] = acc
        state_rows[c, 12:16] = own[12:16]

    tag_copies = [
        pltpu.make_async_copy(table.at[TAGS_AT[side]], tags.at[side], tag_sem.at[side]) for side in range(2)
    ]

    def send_pack(e, carry):
        c = leaver(e)
        pack[e, 0:16] = table[c]
        for k in range(SLOTS):
            spot = partner(c, k)
            pack[e, 16 + 8 * k:24 + 8 * k] = table[spot, 0:8]
            pack[e, 16 + 8 * SLOTS + k:17 + 8 * SLOTS + k] = inverse_limit(c, k, spot)
        pack[e, 16 + 9 * SLOTS:PACK_ROWS] = jnp.zeros((8 - SLOTS, POINTS), F32)
        pl.when(goes(e))(pack_copy(e).start)
        return carry

    def nth(i):
        inner = 5 + lax.rem(i, 2) + 4 * (i // 2)
        side = 4 + 4 * ((i - 8) // 2) + 3 * lax.rem(i, 2)
        return jnp.where(i < 4, inner, jnp.where(i < 8, i - 4, jnp.where(i < 12, side, i)))

    for pair in range(SLOTS // 2):
        prepare(nth(0), 0, pair)

    def two(i, carry):
        @pl.when(i == 1)
        def _():
            for (dw, dn), copy in zip(SIDES, halos):
                pl.when(jnp.logical_not(beyond(dw, dn)))(copy.wait_send)
                pl.when(jnp.logical_not(beyond(-dw, -dn)))(copy.wait_recv)
            for copy in tag_copies:
                copy.start()
            lax.fori_loop(CLUSTERS, TILES, split_tile, 0, unroll=2)
            lax.fori_loop(0, 4, send_pack, 0)

            def send_second(e, carry):
                @pl.when(goes(e))
                def _():
                    for k in range(SLOTS):
                        send_hist(e, k)
                return carry

            lax.fori_loop(2, 4, send_second, 0)

        first, second = nth(2 * i), nth(2 * i + 1)
        cluster(first, 0, second, 1)
        cluster(second, 1, nth(jnp.minimum(2 * i + 2, CLUSTERS - 1)), 0)
        return carry

    lax.fori_loop(0, CLUSTERS // 2, two, 0)

    def send_state(e, carry):
        sent_state[e] = state_rows[leaver(e)]
        pl.when(goes(e))(state_copy(e).start)
        return carry

    lax.fori_loop(0, 4, send_state, 0)

    tail = jnp.where(lax.broadcasted_iota(jnp.int32, (8, POINTS), 0) == ROW_ONE - 8, 1.0, 0.0)

    def expect(e, carry):
        pl.when(comes(e))(pack_copy(e).wait_recv)
        own = jnp.concatenate(split_parts(packed[e, 0:16]), 0)
        mine = left_rows(own, 2)[:, 0:96]
        for pair in range(SLOTS // 2):
            theirs = []
            for k in (2 * pair, 2 * pair + 1):
                tile = jnp.concatenate([packed[e, 16 + 8 * k:24 + 8 * k], tail], 0)
                theirs.append(right_side(jnp.concatenate(split_parts(tile), 0)))
            forms_in[e, pair] = dot(mine, jnp.concatenate(theirs, 1))
        return carry

    lax.fori_loop(0, 4, expect, 0, unroll=2)

    for copy in tag_copies:
        copy.wait()
    for o in range(CLUSTERS):
        source = o
        for e in range(4):
            source = jnp.where(tags[e % 2, 8 * (e // 2), 0] == float(o), CLUSTERS + e, source)
        sources[o] = source

    def arrive(e, carry):
        for k in range(SLOTS):
            pl.when(comes(e))(hist_copy(e, k).wait_recv)
            pair, at = k // 2, pl.ds((k % 2) * POINTS, POINTS)
            rest_sq = forms_in[e, pair, 0:POINTS, at]
            if k == 0:
                rest_sq = rest_sq + apart[...]
            now_sq = jnp.maximum(rest_sq + forms_in[e, pair, POINTS:2 * POINTS, at], TINY)
            stretch = now_sq * lax.rsqrt(now_sq) * lax.rsqrt(rest_sq) - 1.0
            scaled = stretch * packed[e, 16 + 8 * SLOTS + k:17 + 8 * SLOTS + k]
            if k == 0:
                scaled = scaled - apart[...]
            hist_rows[CLUSTERS + e, k] = jnp.maximum(hist_rows[CLUSTERS + e, k], scaled)
        return carry

    lax.fori_loop(0, 4, arrive, 0)

    def finish(e, carry):
        pl.when(comes(e))(state_copy(e).wait_recv)

        @pl.when(goes(e))
        def _():
            for k in range(SLOTS):
                hist_copy(e, k).wait_send()
            pack_copy(e).wait_send()
            state_copy(e).wait_send()
        return carry

    lax.fori_loop(0, 4, finish, 0)


def place_kernel(hist_rows, state_rows, state_in, sources, ref_out, disp_out, vel_out, acc_out, hist_out, states, state_sem, sem):
    copies = []
    for o in range(CLUSTERS):
        copies.append(pltpu.make_async_copy(hist_rows.at[sources[o]], hist_out.at[o], sem.at[o]))
        copies[-1].start()
    for o in range(CLUSTERS):
        source = sources[o]
        rows = jnp.where(source < CLUSTERS, state_rows[o], state_in[jnp.maximum(source - CLUSTERS, 0)])
        for f in range(4):
            for d in range(3):
                states[f, d, o // CN, o % CN:o % CN + 1] = rows[3 * f + d:3 * f + d + 1]
    for f, ref in enumerate((ref_out, disp_out, vel_out, acc_out)):
        copies.append(pltpu.make_async_copy(states.at[f], ref, state_sem.at[f]))
        copies[-1].start()
    for copy in copies:
        copy.wait()


def per_device(
    wide_size, narrow_size,
    ref_local, displacement, velocity, acceleration, history, critical, active, partners, move_src, move_dst,
):
    vmem, smem, anywhere = (pl.BlockSpec(memory_space=m) for m in (pltpu.VMEM, pltpu.SMEM, pl.ANY))
    total = CLUSTERS + 4
    hist_shape = (total, SLOTS, POINTS, POINTS)
    operands = [
        ref_local, displacement, velocity, acceleration, critical, active, partners, move_src, move_dst,
        jnp.asarray(pairing(), BF16), history.reshape(CLUSTERS, SLOTS, POINTS, POINTS),
    ]
    operands = [pltpu.with_memory_space_constraint(x, pltpu.HBM) for x in operands]
    hist_rows, state_rows, state_in, sources = pl.pallas_call(
        functools.partial(step_kernel, wide_size, narrow_size),
        out_shape=(
            pltpu.VMEM(hist_shape, F32),
            pltpu.VMEM((CLUSTERS, 16, POINTS), F32),
            pltpu.VMEM((4, 16, POINTS), F32),
            pltpu.SMEM((CLUSTERS,), jnp.int32),
        ),
        in_specs=[anywhere] * len(operands),
        out_specs=(vmem, vmem, vmem, smem),
        scratch_shapes=[
            *[pltpu.VMEM((CLUSTERS, POINTS, POINTS), F32)] * SLOTS,
            *[pltpu.VMEM(ref_local.shape, F32)] * 4,
            pltpu.SMEM(critical.shape, F32),
            pltpu.SMEM(active.shape, jnp.int32),
            pltpu.SMEM(partners.shape, jnp.int32),
            pltpu.SMEM(move_src.shape, jnp.int32),
            pltpu.SMEM(move_dst.shape, jnp.int32),
            pltpu.VMEM((48, 3 * POINTS), BF16),
            pltpu.SMEM(((CW + 2) * (CN + 2),), jnp.int32),
            pltpu.VMEM((CLUSTERS, 16, POINTS), F32),
            pltpu.VMEM((TILES + 1, 16, POINTS), F32),
            pltpu.VMEM((TILES - CLUSTERS, 16, POINTS), F32),
            pltpu.VMEM((TILES + 1, 48, POINTS), BF16),
            pltpu.VMEM((CLUSTERS, 3 * POINTS, 128), BF16),
            pltpu.VMEM((2, SLOTS // 2, 3 * POINTS, 2 * POINTS), F32),
            pltpu.VMEM((4, SLOTS // 2, 2 * POINTS, 2 * POINTS), F32),
            pltpu.VMEM((POINTS, POINTS), F32),
            pltpu.SMEM((2, 16, POINTS), F32),
            pltpu.VMEM((4, SLOTS, POINTS, POINTS), F32),
            pltpu.VMEM((4, PACK_ROWS, POINTS), F32),
            pltpu.VMEM((4, PACK_ROWS, POINTS), F32),
            pltpu.VMEM((4, 16, POINTS), F32),
            pltpu.SemaphoreType.DMA((10,)),
            pltpu.SemaphoreType.DMA((2,)),
            pltpu.SemaphoreType.DMA((SLOTS,)),
            pltpu.SemaphoreType.DMA((8,)),
            pltpu.SemaphoreType.DMA((8,)),
            *[pltpu.SemaphoreType.DMA((4, SLOTS))] * 2,
            *[pltpu.SemaphoreType.DMA((4,))] * 4,
        ],
        compiler_params=pltpu.CompilerParams(
            collective_id=0, has_side_effects=True, vmem_limit_bytes=26 << 20
        ),
        name="step",
    )(*operands)
    hist_rows = pltpu.with_memory_space_constraint(hist_rows, pltpu.VMEM)
    state_rows = pltpu.with_memory_space_constraint(state_rows, pltpu.VMEM)
    state_in = pltpu.with_memory_space_constraint(state_in, pltpu.VMEM)
    sources = pltpu.with_memory_space_constraint(sources, pltpu.SMEM)
    state = jax.ShapeDtypeStruct(ref_local.shape, F32)
    outs = pl.pallas_call(
        place_kernel,
        out_shape=(state,) * 4 + (jax.ShapeDtypeStruct((CLUSTERS, SLOTS, POINTS, POINTS), F32),),
        in_specs=[anywhere, vmem, vmem, smem],
        out_specs=(anywhere,) * 5,
        scratch_shapes=[
            pltpu.VMEM((4,) + ref_local.shape, F32),
            pltpu.SemaphoreType.DMA((4,)),
            pltpu.SemaphoreType.DMA((CLUSTERS,)),
        ],
        compiler_params=pltpu.CompilerParams(vmem_limit_bytes=8 << 20),
        name="place",
    )(hist_rows, state_rows, state_in, sources)
    return outs[:4] + (outs[4].reshape(history.shape),)


def solution(mesh):
    field = P(None, "wide", "narrow", None)
    blocks = P("wide", "narrow", None)
    hist = P("wide", "narrow", None, None, None)
    moves = P("wide", "narrow", None, None)
    return jax.shard_map(
        functools.partial(per_device, mesh.shape["wide"], mesh.shape["narrow"]),
        mesh=mesh,
        in_specs=(field,) * 4 + (hist,) + (blocks,) * 3 + (moves,) * 2,
        out_specs=(field,) * 4 + (hist,),
        check_vma=False,
    )
```

```python
import functools

import jax
import jax.numpy as jnp
import numpy as np
from jax import lax
from jax.experimental import pallas as pl
from jax.experimental.pallas import tpu as pltpu
from jax.sharding import PartitionSpec as P

STIFFNESS = 8.0
DAMPING = 0.8
TIME_STEP = 0.1
CELL_SPAN = 4.0
FALLOFF = float(-np.log2(np.e) / 9.0)
FAR = 1024.0
APART = 1.0e6
TINY = 1.0e-12

F32 = jnp.float32
BF16 = jnp.bfloat16
MESH = pl.DeviceIdType.MESH
CW = CN = 4
CLUSTERS = CW * CN
SLOTS = 6
POINTS = 128
TILES = CLUSTERS + 22
SIDES = ((-1, 0), (1, 0), (0, -1), (0, 1), (-1, -1), (-1, 1), (1, -1), (1, 1))
SIDE_AT = (16, 21, 26, 30, 34, 35, 36, 37)
SIDE_COUNT = (5, 5, 4, 4, 1, 1, 1, 1)
TAGS_AT = (20, 25)

ROW_R, ROW_U, ROW_V, ROW_Y, ROW_SQ, ROW_ONE = 0, 3, 8, 11, (6, 7, 14), 15
PACK_ROWS = 16 + 8 * SLOTS + 8
PARTS = ((0, 0), (1, 0), (0, 1), (1, 1), (2, 0), (0, 2))


def pairing():
    s = np.zeros((3, 128, 48), np.float32)
    for block, (q, p) in enumerate(PARTS):
        for d in range(3):
            s[0, block * 16 + ROW_R + d, p * 16 + ROW_R + d] = -2
            s[1, block * 16 + ROW_U + d, p * 16 + ROW_Y + d] = -2
            s[1, block * 16 + ROW_R + d, p * 16 + ROW_U + d] = -2
            s[2, block * 16 + ROW_Y + d, p * 16 + ROW_V + d] = -1
            s[2, block * 16 + ROW_V + d, p * 16 + ROW_Y + d] = -1
    for g in range(3):
        for part in range(3):
            s[g, PARTS.index((part, 0)) * 16 + ROW_SQ[g], ROW_ONE] = 1
            s[g, PARTS.index((0, part)) * 16 + ROW_ONE, part * 16 + ROW_SQ[g]] = 1
    return s.reshape(3 * 128, 48).T


def dot(a, b):
    return lax.dot_general(a, b, (((1,), (0,)), ((), ())), preferred_element_type=F32)


def dot_t(a, b):
    return lax.dot_general(a, b, (((1,), (1,)), ((), ())), preferred_element_type=F32)


def tile_index(i, j):
    if 0 <= i < CW and 0 <= j < CN:
        return i * CN + j
    if 0 <= j < CN:
        return (16 if i < 0 else 21) + j
    if 0 <= i < CW:
        return (26 if j < 0 else 30) + i
    return 34 + 2 * (i > 0) + (j > 0)


def step_kernel(
    wide_size, narrow_size,
    ref_hbm, disp_hbm, vel_hbm, acc_hbm, critical_hbm, active_hbm, partners_hbm, src_hbm, dst_hbm, pairs_hbm, history,
    hist_rows, state_rows, state_in, sources,
    held_0, held_1, held_2, held_3, held_4, held_5, ref_local, displacement, velocity, acceleration, critical, active, partners, move_src, move_dst, pairs, where_is,
    plain, table, leaving, split, left, forms, forms_in, apart, tags, raw, pack, packed, sent_state,
    small_sem, tag_sem, load_sem, halo_send, halo_recv, hist_send, hist_recv, pack_send, pack_recv, state_send, state_recv,
):
    held = (held_0, held_1, held_2, held_3, held_4, held_5)
    me_w, me_n = lax.axis_index("wide"), lax.axis_index("narrow")
    def device(dw, dn):
        return (me_w + dw, me_n + dn)

    at_edge = {-1: (me_w == 0, me_n == 0), 1: (me_w == wide_size - 1, me_n == narrow_size - 1)}

    def beyond(dw, dn):
        out = False
        if dw:
            out = out | at_edge[dw][0]
        if dn:
            out = out | at_edge[dn][1]
        return out

    barrier = pltpu.get_barrier_semaphore()
    greeted = 0
    for dw, dn in SIDES[::-1]:
        greeted = greeted + jnp.where(beyond(dw, dn), 0, 1)

        @pl.when(jnp.logical_not(beyond(dw, dn)))
        def _():
            pl.semaphore_signal(barrier, inc=1, device_id=device(dw, dn), device_id_type=MESH)

    small = [
        pltpu.make_async_copy(source, target, small_sem.at[n])
        for n, (source, target) in enumerate((
            (ref_hbm, ref_local), (disp_hbm, displacement), (vel_hbm, velocity), (acc_hbm, acceleration),
            (dst_hbm, move_dst), (pairs_hbm, pairs), (critical_hbm, critical), (active_hbm, active), (partners_hbm, partners),
            (src_hbm, move_src),
        ))
    ]
    for copy in small:
        copy.start()
    loads = [pltpu.make_async_copy(history.at[:, k], held[k], load_sem.at[k]) for k in range(SLOTS)]
    for copy in loads:
        copy.start()

    sub = lax.broadcasted_iota(jnp.int32, (POINTS, POINTS), 0)
    lane = lax.broadcasted_iota(jnp.int32, (POINTS, POINTS), 1)
    apart[...] = jnp.where(sub == lane, APART, 0.0).astype(F32)
    row = lax.broadcasted_iota(jnp.int32, (16, POINTS), 0)
    far = jnp.where((row == ROW_R) | (row == ROW_Y), FAR, 0.0)
    far = jnp.where(row == ROW_SQ[0], FAR * FAR, far)
    table[TILES] = jnp.where(row == ROW_ONE, 1.0, far)
    for i in range(CW + 2):
        for j in range(CN + 2):
            out = beyond((i == CW + 1) - (i == 0), (j == CN + 1) - (j == 0))
            where_is[i * (CN + 2) + j] = jnp.where(out, TILES, tile_index(i - 1, j - 1))

    for copy in small[:5]:
        copy.wait()
    column = lax.broadcasted_iota(jnp.int32, (CN, POINTS), 0)
    anchor_n = column.astype(F32) * CELL_SPAN - CELL_SPAN * CN / 2
    hop_n = jnp.where(column == 0, CELL_SPAN * CN, jnp.where(column == CN - 1, -CELL_SPAN * CN, 0.0))

    def advanced(a):
        base, u, half, v = [], [], [], []
        for d in range(3):
            speed, push = velocity[d, a], acceleration[d, a]
            base.append(ref_local[d, a])
            u.append(displacement[d, a] + TIME_STEP * speed + 0.5 * TIME_STEP * TIME_STEP * push)
            half.append(speed + 0.5 * TIME_STEP * push)
            v.append(half[d] * (DAMPING / STIFFNESS))
        return base, u, half, v

    def tile_rows(a, up_w, up_n, base, u, v):
        r = [base[0] + (CELL_SPAN * (a - CW / 2) + up_w), base[1] + (anchor_n + up_n), base[2] - CELL_SPAN]
        y = [r[d] + u[d] for d in range(3)]
        squares = [
            r[0] * r[0] + r[1] * r[1] + r[2] * r[2],
            u[0] * (r[0] + y[0]) + u[1] * (r[1] + y[1]) + u[2] * (r[2] + y[2]),
            v[0] * y[0] + v[1] * y[1] + v[2] * y[2],
        ]
        return r + u + squares[:2] + v + y + squares[2:] + [jnp.ones_like(u[0])]

    for a in range(CW):
        base, u, half, v = advanced(a)
        for f, row in enumerate(tile_rows(a, 0.0, hop_n, base, u, v)):
            leaving[SIDE_AT[2] - CLUSTERS + a, f:f + 1] = row[0:1]
            leaving[SIDE_AT[3] - CLUSTERS + a, f:f + 1] = row[CN - 1:CN]
        if a in (0, CW - 1):
            side, hop_w = (0, CELL_SPAN * CW) if a == 0 else (1, -CELL_SPAN * CW)
            at = SIDE_AT[side] - CLUSTERS
            for f, row in enumerate(tile_rows(a, hop_w, 0.0, base, u, v)):
                leaving[at:at + CN, f] = row
            at = SIDE_AT[4 + 2 * side] - CLUSTERS
            for f, row in enumerate(tile_rows(a, hop_w, hop_n, base, u, v)):
                leaving[at, f:f + 1] = row[0:1]
                leaving[at + 1, f:f + 1] = row[CN - 1:CN]
    for side in range(2):
        for m in range(2):
            tag = jnp.full((8, POINTS), move_dst[0, 0, 1 - side, m], jnp.int32).astype(F32)
            leaving[TAGS_AT[side] - CLUSTERS, 8 * m:8 * m + 8] = tag

    pl.semaphore_wait(barrier, greeted)
    halos = []
    for n, (dw, dn) in enumerate(SIDES):
        landing = SIDE_AT[SIDES.index((-dw, -dn))]
        halos.append(pltpu.make_async_remote_copy(
            src_ref=leaving.at[pl.ds(SIDE_AT[n] - CLUSTERS, SIDE_COUNT[n])],
            dst_ref=table.at[pl.ds(landing, SIDE_COUNT[n])],
            send_sem=halo_send.at[n], recv_sem=halo_recv.at[n],
            device_id=device(dw, dn), device_id_type=MESH,
        ))
    for side, copy in reversed(list(zip(SIDES, halos))):
        pl.when(jnp.logical_not(beyond(*side)))(copy.start)
    for n in range(2):
        @pl.when(beyond(*SIDES[n]))
        def _():
            table[TAGS_AT[n]] = jnp.full((16, POINTS), -1.0, F32)


    def split_parts(tile):
        high = tile.astype(BF16)
        rest = tile - high.astype(F32)
        middle = rest.astype(BF16)
        return high, middle, (rest - middle.astype(F32)).astype(BF16)

    def split_tile(t, carry):
        for n, part in enumerate(split_parts(table[t])):
            split[t, n * 16:n * 16 + 16] = part
        return carry

    def toward(e):
        return device(1 - 2 * lax.rem(e, 2), 0)

    def goes(e):
        return jnp.logical_not(jnp.where(lax.rem(e, 2) == 0, at_edge[1][0], at_edge[-1][0]))

    def comes(e):
        return jnp.logical_not(jnp.where(lax.rem(e, 2) == 0, at_edge[-1][0], at_edge[1][0]))

    def hist_copy(e, k):
        return pltpu.make_async_remote_copy(
            src_ref=raw.at[e, k], dst_ref=hist_rows.at[CLUSTERS + e, k],
            send_sem=hist_send.at[e, k], recv_sem=hist_recv.at[e, k],
            device_id=toward(e), device_id_type=MESH,
        )

    def pack_copy(e):
        return pltpu.make_async_remote_copy(
            src_ref=pack.at[e], dst_ref=packed.at[e], send_sem=pack_send.at[e], recv_sem=pack_recv.at[e],
            device_id=toward(e), device_id_type=MESH,
        )

    def state_copy(e):
        return pltpu.make_async_remote_copy(
            src_ref=sent_state.at[e], dst_ref=state_in.at[e],
            send_sem=state_send.at[e], recv_sem=state_recv.at[e],
            device_id=toward(e), device_id_type=MESH,
        )

    def leaver(e):
        return jnp.maximum(move_src[0, 0, lax.rem(e, 2), e // 2], 0)

    for copy in small[5:]:
        copy.wait()

    def send_hist(e, k):
        raw[e, k] = held[k][leaver(e)]
        hist_copy(e, k).start()

    def send_first(k):
        loads[k].wait()
        for e in range(2):
            pl.when(goes(e))(functools.partial(send_hist, e, k))

    send_first(0)
    send_first(1)
    for a in range(CW):
        base, u, half, v = advanced(a)
        here = pl.ds(a * CN, CN)
        for f, row in enumerate(base + u + half):
            plain[here, f] = row
        for f in range(9, 16):
            plain[here, f] = jnp.zeros((CN, POINTS), F32)
        for f, row in enumerate(tile_rows(a, 0.0, 0.0, base, u, v)):
            table[here, f] = row

    lax.fori_loop(0, CLUSTERS, split_tile, 0, unroll=4)
    split_tile(TILES, 0)
    send_first(2)
    send_first(3)

    def left_rows(parts, count):
        turned = jnp.transpose(parts.astype(F32)).astype(BF16)
        wide = dot(turned, pairs[:, 0:count * POINTS]).astype(BF16)
        return jnp.concatenate([wide[:, g * POINTS:(g + 1) * POINTS] for g in range(count)], 0)

    def left_side(c, carry):
        left[c] = left_rows(split[c], 3)
        return carry

    lax.fori_loop(0, CLUSTERS, left_side, 0, unroll=4)
    send_first(4)
    send_first(5)

    def place_of(c):
        a = lax.shift_right_logical(c, 2)
        return a, c - CN * a

    def partner(c, k):
        a, b = place_of(c)
        o = partners[a, b, k]
        third = lax.shift_right_logical(o * 11, 5)
        spot = where_is[(CN + 2) * (a + third) + b + o - 3 * third]
        return jnp.where(active[a, b, k] > 0, spot, TILES)

    def inverse_limit(c, k, spot):
        a, b = place_of(c)
        return jnp.where(spot == TILES, 0.0, 1.0) / jnp.full((1, POINTS), critical[a, b, k], F32)

    def right_side(tile):
        return jnp.concatenate([tile[q * 16:q * 16 + 16] for q, _ in PARTS], 0)

    def prepare(c, buffer, pair):
        theirs = [right_side(split[partner(c, k)]) for k in (2 * pair, 2 * pair + 1)]
        forms[buffer, pair] = dot(left[c, :, 0:96], jnp.concatenate(theirs, 1))

    def pull(c, buffer, k):
        pair, at = k // 2, pl.ds((k % 2) * POINTS, POINTS)
        spot = partner(c, k)
        rest_sq = forms[buffer, pair, 0:POINTS, at]
        if k == 0:
            rest_sq = rest_sq + apart[...]
        now_sq = jnp.maximum(rest_sq + forms[buffer, pair, POINTS:2 * POINTS, at], TINY)
        rate = forms[buffer, pair, 2 * POINTS:3 * POINTS, at]
        now_inv = lax.rsqrt(now_sq)
        stretch = now_sq * now_inv * lax.rsqrt(rest_sq) - 1.0
        scaled = stretch * inverse_limit(c, k, spot)
        if k == 0:
            scaled = scaled - apart[...]
        hist = jnp.maximum(held[k][c], scaled)
        hist_rows[c, k] = hist
        weight = jnp.exp2(rest_sq * FALLOFF) * jnp.minimum(jnp.maximum(2.0 - hist, 0.0), 1.0)
        factor = weight * (stretch + rate * now_inv) * now_inv
        high = factor.astype(BF16)
        low = (factor - high.astype(F32)).astype(BF16)
        tile = split[spot]
        return dot_t(jnp.concatenate([high, low], 1), jnp.concatenate([tile, tile], 1))

    def cluster(c, buffer, after, after_buffer):
        sums = None
        for pair in range(SLOTS // 2):
            prepare(after, after_buffer, pair)
            for k in (2 * pair, 2 * pair + 1):
                term = pull(c, buffer, k)
                sums = term if sums is None else sums + term
        sums = jnp.transpose(sums)
        sums = sums[0:16] + sums[16:32] + sums[32:48]
        here = table[c]
        own = plain[c]
        acc = STIFFNESS * (sums[ROW_Y:ROW_Y + 3] - here[ROW_Y:ROW_Y + 3] * sums[ROW_ONE:ROW_ONE + 1])
        state_rows[c, 0:6] = own[0:6]
        state_rows[c, 6:9] = own[6:9] + 0.5 * TIME_STEP * acc
        state_rows[c, 9:12] = acc
        state_rows[c, 12:16] = own[12:16]

    tag_copies = [
        pltpu.make_async_copy(table.at[TAGS_AT[side]], tags.at[side], tag_sem.at[side]) for side in range(2)
    ]

    def send_pack(e, carry):
        c = leaver(e)
        pack[e, 0:16] = table[c]
        for k in range(SLOTS):
            spot = partner(c, k)
            pack[e, 16 + 8 * k:24 + 8 * k] = table[spot, 0:8]
            pack[e, 16 + 8 * SLOTS + k:17 + 8 * SLOTS + k] = inverse_limit(c, k, spot)
        pack[e, 16 + 9 * SLOTS:PACK_ROWS] = jnp.zeros((8 - SLOTS, POINTS), F32)
        pl.when(goes(e))(pack_copy(e).start)
        return carry

    def nth(i):
        inner = 5 + lax.rem(i, 2) + 4 * (i // 2)
        row = 1 + lax.rem(i, 2) + 12 * ((i - 4) // 2)
        column = 4 + 4 * lax.rem(i, 2) + 3 * ((i - 8) // 2)
        corner = 3 * lax.rem(i, 2) + 12 * ((i - 12) // 2)
        return jnp.where(i < 4, inner, jnp.where(i < 8, row, jnp.where(i < 12, column, corner)))

    for pair in range(SLOTS // 2):
        prepare(nth(0), 0, pair)

    def landed(sides):
        for n in sides:
            (dw, dn), copy = SIDES[n], halos[n]
            pl.when(jnp.logical_not(beyond(dw, dn)))(copy.wait_send)
            pl.when(jnp.logical_not(beyond(-dw, -dn)))(copy.wait_recv)

    def send_second(slots):
        def go(e, carry):
            @pl.when(goes(e))
            def _():
                for k in slots:
                    send_hist(e, k)
            return carry

        lax.fori_loop(2, 4, go, 0)

    def two(i, carry):
        @pl.when(i == 1)
        def _():
            send_second(range(0, 3))
            landed(range(0, 4))
            for copy in tag_copies:
                copy.start()
            lax.fori_loop(CLUSTERS, SIDE_AT[4], split_tile, 0, unroll=2)

        @pl.when(i == 4)
        def _():
            landed(range(4, 8))
            lax.fori_loop(0, 4, send_pack, 0)
            send_second(range(3, SLOTS))
            lax.fori_loop(SIDE_AT[4], TILES, split_tile, 0, unroll=2)

        first, second = nth(2 * i), nth(2 * i + 1)
        cluster(first, 0, second, 1)
        cluster(second, 1, nth(jnp.minimum(2 * i + 2, CLUSTERS - 1)), 0)
        return carry

    lax.fori_loop(0, CLUSTERS // 2, two, 0)

    def send_state(e, carry):
        sent_state[e] = state_rows[leaver(e)]
        pl.when(goes(e))(state_copy(e).start)
        return carry

    lax.fori_loop(0, 4, send_state, 0)

    tail = jnp.where(lax.broadcasted_iota(jnp.int32, (8, POINTS), 0) == ROW_ONE - 8, 1.0, 0.0)

    def expect(e, carry):
        pl.when(comes(e))(pack_copy(e).wait_recv)
        own = jnp.concatenate(split_parts(packed[e, 0:16]), 0)
        mine = left_rows(own, 2)[:, 0:96]
        for pair in range(SLOTS // 2):
            theirs = []
            for k in (2 * pair, 2 * pair + 1):
                tile = jnp.concatenate([packed[e, 16 + 8 * k:24 + 8 * k], tail], 0)
                theirs.append(right_side(jnp.concatenate(split_parts(tile), 0)))
            forms_in[e, pair] = dot(mine, jnp.concatenate(theirs, 1))
        return carry

    lax.fori_loop(0, 4, expect, 0, unroll=4)

    for copy in tag_copies:
        copy.wait()
    for o in range(CLUSTERS):
        source = o
        for e in range(4):
            source = jnp.where(tags[e % 2, 8 * (e // 2), 0] == float(o), CLUSTERS + e, source)
        sources[o] = source

    def arrive(e, carry):
        for k in range(SLOTS):
            pl.when(comes(e))(hist_copy(e, k).wait_recv)
            pair, at = k // 2, pl.ds((k % 2) * POINTS, POINTS)
            rest_sq = forms_in[e, pair, 0:POINTS, at]
            if k == 0:
                rest_sq = rest_sq + apart[...]
            now_sq = jnp.maximum(rest_sq + forms_in[e, pair, POINTS:2 * POINTS, at], TINY)
            stretch = now_sq * lax.rsqrt(now_sq) * lax.rsqrt(rest_sq) - 1.0
            scaled = stretch * packed[e, 16 + 8 * SLOTS + k:17 + 8 * SLOTS + k]
            if k == 0:
                scaled = scaled - apart[...]
            hist_rows[CLUSTERS + e, k] = jnp.maximum(hist_rows[CLUSTERS + e, k], scaled)
        return carry

    lax.fori_loop(0, 4, arrive, 0)

    def finish(e, carry):
        pl.when(comes(e))(state_copy(e).wait_recv)

        @pl.when(goes(e))
        def _():
            for k in range(SLOTS):
                hist_copy(e, k).wait_send()
            pack_copy(e).wait_send()
            state_copy(e).wait_send()
        return carry

    lax.fori_loop(0, 4, finish, 0)


def place_kernel(hist_rows, state_rows, state_in, sources, ref_out, disp_out, vel_out, acc_out, hist_out, states, state_sem, sem):
    copies = []
    for o in range(CLUSTERS):
        copies.append(pltpu.make_async_copy(hist_rows.at[sources[o]], hist_out.at[o], sem.at[o]))
        copies[-1].start()
    for o in range(CLUSTERS):
        source = sources[o]
        rows = jnp.where(source < CLUSTERS, state_rows[o], state_in[jnp.maximum(source - CLUSTERS, 0)])
        for f in range(4):
            for d in range(3):
                states[f, d, o // CN, o % CN:o % CN + 1] = rows[3 * f + d:3 * f + d + 1]
    for f, ref in enumerate((ref_out, disp_out, vel_out, acc_out)):
        copies.append(pltpu.make_async_copy(states.at[f], ref, state_sem.at[f]))
        copies[-1].start()
    for copy in copies:
        copy.wait()


def per_device(
    wide_size, narrow_size,
    ref_local, displacement, velocity, acceleration, history, critical, active, partners, move_src, move_dst,
):
    vmem, smem, anywhere = (pl.BlockSpec(memory_space=m) for m in (pltpu.VMEM, pltpu.SMEM, pl.ANY))
    total = CLUSTERS + 4
    hist_shape = (total, SLOTS, POINTS, POINTS)
    operands = [
        ref_local, displacement, velocity, acceleration, critical, active, partners, move_src, move_dst,
        jnp.asarray(pairing(), BF16), history.reshape(CLUSTERS, SLOTS, POINTS, POINTS),
    ]
    operands = [pltpu.with_memory_space_constraint(x, pltpu.HBM) for x in operands]
    hist_rows, state_rows, state_in, sources = pl.pallas_call(
        functools.partial(step_kernel, wide_size, narrow_size),
        out_shape=(
            pltpu.VMEM(hist_shape, F32),
            pltpu.VMEM((CLUSTERS, 16, POINTS), F32),
            pltpu.VMEM((4, 16, POINTS), F32),
            pltpu.SMEM((CLUSTERS,), jnp.int32),
        ),
        in_specs=[anywhere] * len(operands),
        out_specs=(vmem, vmem, vmem, smem),
        scratch_shapes=[
            *[pltpu.VMEM((CLUSTERS, POINTS, POINTS), F32)] * SLOTS,
            *[pltpu.VMEM(ref_local.shape, F32)] * 4,
            pltpu.SMEM(critical.shape, F32),
            pltpu.SMEM(active.shape, jnp.int32),
            pltpu.SMEM(partners.shape, jnp.int32),
            pltpu.SMEM(move_src.shape, jnp.int32),
            pltpu.SMEM(move_dst.shape, jnp.int32),
            pltpu.VMEM((48, 3 * POINTS), BF16),
            pltpu.SMEM(((CW + 2) * (CN + 2),), jnp.int32),
            pltpu.VMEM((CLUSTERS, 16, POINTS), F32),
            pltpu.VMEM((TILES + 1, 16, POINTS), F32),
            pltpu.VMEM((TILES - CLUSTERS, 16, POINTS), F32),
            pltpu.VMEM((TILES + 1, 48, POINTS), BF16),
            pltpu.VMEM((CLUSTERS, 3 * POINTS, 128), BF16),
            pltpu.VMEM((2, SLOTS // 2, 3 * POINTS, 2 * POINTS), F32),
            pltpu.VMEM((4, SLOTS // 2, 2 * POINTS, 2 * POINTS), F32),
            pltpu.VMEM((POINTS, POINTS), F32),
            pltpu.SMEM((2, 16, POINTS), F32),
            pltpu.VMEM((4, SLOTS, POINTS, POINTS), F32),
            pltpu.VMEM((4, PACK_ROWS, POINTS), F32),
            pltpu.VMEM((4, PACK_ROWS, POINTS), F32),
            pltpu.VMEM((4, 16, POINTS), F32),
            pltpu.SemaphoreType.DMA((10,)),
            pltpu.SemaphoreType.DMA((2,)),
            pltpu.SemaphoreType.DMA((SLOTS,)),
            pltpu.SemaphoreType.DMA((8,)),
            pltpu.SemaphoreType.DMA((8,)),
            *[pltpu.SemaphoreType.DMA((4, SLOTS))] * 2,
            *[pltpu.SemaphoreType.DMA((4,))] * 4,
        ],
        compiler_params=pltpu.CompilerParams(
            collective_id=0, has_side_effects=True, vmem_limit_bytes=26 << 20
        ),
        name="step",
    )(*operands)
    hist_rows = pltpu.with_memory_space_constraint(hist_rows, pltpu.VMEM)
    state_rows = pltpu.with_memory_space_constraint(state_rows, pltpu.VMEM)
    state_in = pltpu.with_memory_space_constraint(state_in, pltpu.VMEM)
    sources = pltpu.with_memory_space_constraint(sources, pltpu.SMEM)
    state = jax.ShapeDtypeStruct(ref_local.shape, F32)
    outs = pl.pallas_call(
        place_kernel,
        out_shape=(state,) * 4 + (jax.ShapeDtypeStruct((CLUSTERS, SLOTS, POINTS, POINTS), F32),),
        in_specs=[anywhere, vmem, vmem, smem],
        out_specs=(anywhere,) * 5,
        scratch_shapes=[
            pltpu.VMEM((4,) + ref_local.shape, F32),
            pltpu.SemaphoreType.DMA((4,)),
            pltpu.SemaphoreType.DMA((CLUSTERS,)),
        ],
        compiler_params=pltpu.CompilerParams(vmem_limit_bytes=8 << 20),
        name="place",
    )(hist_rows, state_rows, state_in, sources)
    return outs[:4] + (outs[4].reshape(history.shape),)


def solution(mesh):
    field = P(None, "wide", "narrow", None)
    blocks = P("wide", "narrow", None)
    hist = P("wide", "narrow", None, None, None)
    moves = P("wide", "narrow", None, None)
    return jax.shard_map(
        functools.partial(per_device, mesh.shape["wide"], mesh.shape["narrow"]),
        mesh=mesh,
        in_specs=(field,) * 4 + (hist,) + (blocks,) * 3 + (moves,) * 2,
        out_specs=(field,) * 4 + (hist,),
        check_vma=False,
    )
```

```python
import functools

import jax
import jax.numpy as jnp
import numpy as np
from jax import lax
from jax.experimental import pallas as pl
from jax.experimental.pallas import tpu as pltpu
from jax.sharding import PartitionSpec as P

STIFFNESS = 8.0
DAMPING = 0.8
TIME_STEP = 0.1
CELL_SPAN = 4.0
FALLOFF = float(-np.log2(np.e) / 9.0)
FAR = 1024.0
APART = 1.0e6
TINY = 1.0e-12

F32 = jnp.float32
BF16 = jnp.bfloat16
MESH = pl.DeviceIdType.MESH
CW = CN = 4
CLUSTERS = CW * CN
SLOTS = 6
POINTS = 128
TILES = CLUSTERS + 22
SIDES = ((-1, 0), (1, 0), (0, -1), (0, 1), (-1, -1), (-1, 1), (1, -1), (1, 1))
SIDE_AT = (16, 21, 26, 30, 34, 35, 36, 37)
SIDE_COUNT = (5, 5, 4, 4, 1, 1, 1, 1)
TAGS_AT = (20, 25)

ROW_R, ROW_U, ROW_V, ROW_Y, ROW_SQ, ROW_ONE = 0, 3, 8, 11, (6, 7, 14), 15
PACK_ROWS = 16 + 8 * SLOTS + 8
PARTS = ((0, 0), (1, 0), (0, 1), (1, 1), (2, 0), (0, 2))


def pairing():
    s = np.zeros((3, 128, 48), np.float32)
    for block, (q, p) in enumerate(PARTS):
        for d in range(3):
            s[0, block * 16 + ROW_R + d, p * 16 + ROW_R + d] = -2
            s[1, block * 16 + ROW_U + d, p * 16 + ROW_Y + d] = -2
            s[1, block * 16 + ROW_R + d, p * 16 + ROW_U + d] = -2
            s[2, block * 16 + ROW_Y + d, p * 16 + ROW_V + d] = -1
            s[2, block * 16 + ROW_V + d, p * 16 + ROW_Y + d] = -1
    for g in range(3):
        for part in range(3):
            s[g, PARTS.index((part, 0)) * 16 + ROW_SQ[g], ROW_ONE] = 1
            s[g, PARTS.index((0, part)) * 16 + ROW_ONE, part * 16 + ROW_SQ[g]] = 1
    return s.reshape(3 * 128, 48).T


def dot(a, b):
    return lax.dot_general(a, b, (((1,), (0,)), ((), ())), preferred_element_type=F32)


def dot_t(a, b):
    return lax.dot_general(a, b, (((1,), (1,)), ((), ())), preferred_element_type=F32)


def tile_index(i, j):
    if 0 <= i < CW and 0 <= j < CN:
        return i * CN + j
    if 0 <= j < CN:
        return (16 if i < 0 else 21) + j
    if 0 <= i < CW:
        return (26 if j < 0 else 30) + i
    return 34 + 2 * (i > 0) + (j > 0)


def step_kernel(
    wide_size, narrow_size,
    ref_hbm, disp_hbm, vel_hbm, acc_hbm, critical_hbm, active_hbm, partners_hbm, src_hbm, dst_hbm, pairs_hbm, history,
    hist_rows, state_rows, state_in, sources,
    held_0, held_1, held_2, held_3, held_4, held_5, ref_local, displacement, velocity, acceleration, critical, active, partners, move_src, move_dst, pairs, where_is,
    plain, table, leaving, split, left, forms, forms_in, apart, tags, raw, pack, packed, sent_state,
    small_sem, tag_sem, load_sem, halo_send, halo_recv, hist_send, hist_recv, pack_send, pack_recv, state_send, state_recv,
):
    held = (held_0, held_1, held_2, held_3, held_4, held_5)
    me_w, me_n = lax.axis_index("wide"), lax.axis_index("narrow")
    def device(dw, dn):
        return (me_w + dw, me_n + dn)

    at_edge = {-1: (me_w == 0, me_n == 0), 1: (me_w == wide_size - 1, me_n == narrow_size - 1)}

    def beyond(dw, dn):
        out = False
        if dw:
            out = out | at_edge[dw][0]
        if dn:
            out = out | at_edge[dn][1]
        return out

    barrier = pltpu.get_barrier_semaphore()
    greeted = 0
    for dw, dn in SIDES[::-1]:
        greeted = greeted + jnp.where(beyond(dw, dn), 0, 1)

        @pl.when(jnp.logical_not(beyond(dw, dn)))
        def _():
            pl.semaphore_signal(barrier, inc=1, device_id=device(dw, dn), device_id_type=MESH)

    small = [
        pltpu.make_async_copy(source, target, small_sem.at[n])
        for n, (source, target) in enumerate((
            (ref_hbm, ref_local), (disp_hbm, displacement), (vel_hbm, velocity), (acc_hbm, acceleration),
            (dst_hbm, move_dst), (pairs_hbm, pairs), (critical_hbm, critical), (active_hbm, active), (partners_hbm, partners),
            (src_hbm, move_src),
        ))
    ]
    for copy in small:
        copy.start()
    loads = [pltpu.make_async_copy(history.at[:, k], held[k], load_sem.at[k]) for k in range(SLOTS)]
    for copy in loads:
        copy.start()

    sub = lax.broadcasted_iota(jnp.int32, (POINTS, POINTS), 0)
    lane = lax.broadcasted_iota(jnp.int32, (POINTS, POINTS), 1)
    apart[...] = jnp.where(sub == lane, APART, 0.0).astype(F32)
    row = lax.broadcasted_iota(jnp.int32, (16, POINTS), 0)
    far = jnp.where((row == ROW_R) | (row == ROW_Y), FAR, 0.0)
    far = jnp.where(row == ROW_SQ[0], FAR * FAR, far)
    table[TILES] = jnp.where(row == ROW_ONE, 1.0, far)
    for i in range(CW + 2):
        for j in range(CN + 2):
            out = beyond((i == CW + 1) - (i == 0), (j == CN + 1) - (j == 0))
            where_is[i * (CN + 2) + j] = jnp.where(out, TILES, tile_index(i - 1, j - 1))

    for copy in small[:5]:
        copy.wait()
    column = lax.broadcasted_iota(jnp.int32, (CN, POINTS), 0)
    anchor_n = column.astype(F32) * CELL_SPAN - CELL_SPAN * CN / 2
    hop_n = jnp.where(column == 0, CELL_SPAN * CN, jnp.where(column == CN - 1, -CELL_SPAN * CN, 0.0))

    def advanced(a):
        base, u, half, v = [], [], [], []
        for d in range(3):
            speed, push = velocity[d, a], acceleration[d, a]
            base.append(ref_local[d, a])
            u.append(displacement[d, a] + TIME_STEP * speed + 0.5 * TIME_STEP * TIME_STEP * push)
            half.append(speed + 0.5 * TIME_STEP * push)
            v.append(half[d] * (DAMPING / STIFFNESS))
        return base, u, half, v

    def tile_rows(a, up_w, up_n, base, u, v):
        r = [base[0] + (CELL_SPAN * (a - CW / 2) + up_w), base[1] + (anchor_n + up_n), base[2] - CELL_SPAN]
        y = [r[d] + u[d] for d in range(3)]
        squares = [
            r[0] * r[0] + r[1] * r[1] + r[2] * r[2],
            u[0] * (r[0] + y[0]) + u[1] * (r[1] + y[1]) + u[2] * (r[2] + y[2]),
            v[0] * y[0] + v[1] * y[1] + v[2] * y[2],
        ]
        return r + u + squares[:2] + v + y + squares[2:] + [jnp.ones_like(u[0])]

    for a in range(CW):
        base, u, half, v = advanced(a)
        for f, row in enumerate(tile_rows(a, 0.0, hop_n, base, u, v)):
            leaving[SIDE_AT[2] - CLUSTERS + a, f:f + 1] = row[0:1]
            leaving[SIDE_AT[3] - CLUSTERS + a, f:f + 1] = row[CN - 1:CN]
        if a in (0, CW - 1):
            side, hop_w = (0, CELL_SPAN * CW) if a == 0 else (1, -CELL_SPAN * CW)
            at = SIDE_AT[side] - CLUSTERS
            for f, row in enumerate(tile_rows(a, hop_w, 0.0, base, u, v)):
                leaving[at:at + CN, f] = row
            at = SIDE_AT[4 + 2 * side] - CLUSTERS
            for f, row in enumerate(tile_rows(a, hop_w, hop_n, base, u, v)):
                leaving[at, f:f + 1] = row[0:1]
                leaving[at + 1, f:f + 1] = row[CN - 1:CN]
    for side in range(2):
        for m in range(2):
            tag = jnp.full((8, POINTS), move_dst[0, 0, 1 - side, m], jnp.int32).astype(F32)
            leaving[TAGS_AT[side] - CLUSTERS, 8 * m:8 * m + 8] = tag

    pl.semaphore_wait(barrier, greeted)
    halos = []
    for n, (dw, dn) in enumerate(SIDES):
        landing = SIDE_AT[SIDES.index((-dw, -dn))]
        halos.append(pltpu.make_async_remote_copy(
            src_ref=leaving.at[pl.ds(SIDE_AT[n] - CLUSTERS, SIDE_COUNT[n])],
            dst_ref=table.at[pl.ds(landing, SIDE_COUNT[n])],
            send_sem=halo_send.at[n], recv_sem=halo_recv.at[n],
            device_id=device(dw, dn), device_id_type=MESH,
        ))
    for n in (0, 1, 4, 5, 6, 7, 2, 3):
        pl.when(jnp.logical_not(beyond(*SIDES[n])))(halos[n].start)
    for n in range(2):
        @pl.when(beyond(*SIDES[n]))
        def _():
            table[TAGS_AT[n]] = jnp.full((16, POINTS), -1.0, F32)


    def split_parts(tile):
        high = tile.astype(BF16)
        rest = tile - high.astype(F32)
        middle = rest.astype(BF16)
        return high, middle, (rest - middle.astype(F32)).astype(BF16)

    def split_tile(t, carry):
        for n, part in enumerate(split_parts(table[t])):
            split[t, n * 16:n * 16 + 16] = part
        return carry

    def toward(e):
        return device(1 - 2 * lax.rem(e, 2), 0)

    def goes(e):
        return jnp.logical_not(jnp.where(lax.rem(e, 2) == 0, at_edge[1][0], at_edge[-1][0]))

    def comes(e):
        return jnp.logical_not(jnp.where(lax.rem(e, 2) == 0, at_edge[-1][0], at_edge[1][0]))

    def hist_copy(e, k):
        return pltpu.make_async_remote_copy(
            src_ref=raw.at[e, k], dst_ref=hist_rows.at[CLUSTERS + e, k],
            send_sem=hist_send.at[e, k], recv_sem=hist_recv.at[e, k],
            device_id=toward(e), device_id_type=MESH,
        )

    def pack_copy(e):
        return pltpu.make_async_remote_copy(
            src_ref=pack.at[e], dst_ref=packed.at[e], send_sem=pack_send.at[e], recv_sem=pack_recv.at[e],
            device_id=toward(e), device_id_type=MESH,
        )

    def state_copy(e):
        return pltpu.make_async_remote_copy(
            src_ref=sent_state.at[e], dst_ref=state_in.at[e],
            send_sem=state_send.at[e], recv_sem=state_recv.at[e],
            device_id=toward(e), device_id_type=MESH,
        )

    def leaver(e):
        return jnp.maximum(move_src[0, 0, lax.rem(e, 2), e // 2], 0)

    for copy in small[5:]:
        copy.wait()

    def send_hist(e, k):
        raw[e, k] = held[k][leaver(e)]
        hist_copy(e, k).start()

    def send_first(k):
        loads[k].wait()
        for e in range(2):
            pl.when(goes(e))(functools.partial(send_hist, e, k))

    send_first(0)
    send_first(1)
    for a in range(CW):
        base, u, half, v = advanced(a)
        here = pl.ds(a * CN, CN)
        for f, row in enumerate(base + u + half):
            plain[here, f] = row
        for f in range(9, 16):
            plain[here, f] = jnp.zeros((CN, POINTS), F32)
        for f, row in enumerate(tile_rows(a, 0.0, 0.0, base, u, v)):
            table[here, f] = row

    lax.fori_loop(0, CLUSTERS, split_tile, 0, unroll=4)
    split_tile(TILES, 0)
    send_first(2)
    send_first(3)

    def left_rows(parts, count):
        turned = jnp.transpose(parts.astype(F32)).astype(BF16)
        wide = dot(turned, pairs[:, 0:count * POINTS]).astype(BF16)
        return jnp.concatenate([wide[:, g * POINTS:(g + 1) * POINTS] for g in range(count)], 0)

    def left_side(c, carry):
        left[c] = left_rows(split[c], 3)
        return carry

    lax.fori_loop(0, CLUSTERS, left_side, 0, unroll=4)
    send_first(4)
    send_first(5)

    def place_of(c):
        a = lax.shift_right_logical(c, 2)
        return a, c - CN * a

    def partner(c, k):
        a, b = place_of(c)
        o = partners[a, b, k]
        third = lax.shift_right_logical(o * 11, 5)
        spot = where_is[(CN + 2) * (a + third) + b + o - 3 * third]
        return jnp.where(active[a, b, k] > 0, spot, TILES)

    def inverse_limit(c, k, spot):
        a, b = place_of(c)
        return jnp.where(spot == TILES, 0.0, 1.0) / jnp.full((1, POINTS), critical[a, b, k], F32)

    def right_side(tile):
        return jnp.concatenate([tile[q * 16:q * 16 + 16] for q, _ in PARTS], 0)

    def prepare(c, buffer, pair):
        theirs = [right_side(split[partner(c, k)]) for k in (2 * pair, 2 * pair + 1)]
        forms[buffer, pair] = dot(left[c, :, 0:96], jnp.concatenate(theirs, 1))

    def pull(c, buffer, k):
        pair, at = k // 2, pl.ds((k % 2) * POINTS, POINTS)
        spot = partner(c, k)
        rest_sq = forms[buffer, pair, 0:POINTS, at]
        if k == 0:
            rest_sq = rest_sq + apart[...]
        now_sq = jnp.maximum(rest_sq + forms[buffer, pair, POINTS:2 * POINTS, at], TINY)
        rate = forms[buffer, pair, 2 * POINTS:3 * POINTS, at]
        now_inv = lax.rsqrt(now_sq)
        stretch = now_sq * now_inv * lax.rsqrt(rest_sq) - 1.0
        scaled = stretch * inverse_limit(c, k, spot)
        if k == 0:
            scaled = scaled - apart[...]
        hist = jnp.maximum(held[k][c], scaled)
        hist_rows[c, k] = hist
        weight = jnp.exp2(rest_sq * FALLOFF) * jnp.minimum(jnp.maximum(2.0 - hist, 0.0), 1.0)
        factor = weight * (stretch + rate * now_inv) * now_inv
        high = factor.astype(BF16)
        low = (factor - high.astype(F32)).astype(BF16)
        tile = split[spot]
        return dot_t(jnp.concatenate([high, low], 1), jnp.concatenate([tile, tile], 1))

    def cluster(c, buffer, after, after_buffer):
        sums = None
        for pair in range(SLOTS // 2):
            prepare(after, after_buffer, pair)
            for k in (2 * pair, 2 * pair + 1):
                term = pull(c, buffer, k)
                sums = term if sums is None else sums + term
        sums = jnp.transpose(sums)
        sums = sums[0:16] + sums[16:32] + sums[32:48]
        here = table[c]
        own = plain[c]
        acc = STIFFNESS * (sums[ROW_Y:ROW_Y + 3] - here[ROW_Y:ROW_Y + 3] * sums[ROW_ONE:ROW_ONE + 1])
        state_rows[c, 0:6] = own[0:6]
        state_rows[c, 6:9] = own[6:9] + 0.5 * TIME_STEP * acc
        state_rows[c, 9:12] = acc
        state_rows[c, 12:16] = own[12:16]

    tag_copies = [
        pltpu.make_async_copy(table.at[TAGS_AT[side]], tags.at[side], tag_sem.at[side]) for side in range(2)
    ]

    def send_pack(e, carry):
        c = leaver(e)
        pack[e, 0:16] = table[c]
        for k in range(SLOTS):
            spot = partner(c, k)
            pack[e, 16 + 8 * k:24 + 8 * k] = table[spot, 0:8]
            pack[e, 16 + 8 * SLOTS + k:17 + 8 * SLOTS + k] = inverse_limit(c, k, spot)
        pack[e, 16 + 9 * SLOTS:PACK_ROWS] = jnp.zeros((8 - SLOTS, POINTS), F32)
        pl.when(goes(e))(pack_copy(e).start)
        return carry

    def nth(i):
        inner = 5 + lax.rem(i, 2) + 4 * (i // 2)
        column = 4 + 4 * lax.rem(i, 2) + 3 * ((i - 4) // 2)
        row = 1 + lax.rem(i, 2) + 12 * ((i - 8) // 2)
        corner = 3 * lax.rem(i, 2) + 12 * ((i - 12) // 2)
        return jnp.where(i < 4, inner, jnp.where(i < 8, column, jnp.where(i < 12, row, corner)))

    for pair in range(SLOTS // 2):
        prepare(nth(0), 0, pair)

    def landed(sides):
        for n in sides:
            (dw, dn), copy = SIDES[n], halos[n]
            pl.when(jnp.logical_not(beyond(dw, dn)))(copy.wait_send)
            pl.when(jnp.logical_not(beyond(-dw, -dn)))(copy.wait_recv)

    def send_second(slots):
        def go(e, carry):
            @pl.when(goes(e))
            def _():
                for k in slots:
                    send_hist(e, k)
            return carry

        lax.fori_loop(2, 4, go, 0)

    def two(i, carry):
        @pl.when(i == 1)
        def _():
            send_second(range(0, 3))
            landed(range(2, 4))
            lax.fori_loop(SIDE_AT[2], SIDE_AT[4], split_tile, 0, unroll=2)

        @pl.when(i == 3)
        def _():
            landed(range(0, 2))
            for copy in tag_copies:
                copy.start()
            lax.fori_loop(CLUSTERS, SIDE_AT[2], split_tile, 0, unroll=2)

        @pl.when(i == 4)
        def _():
            landed(range(4, 8))
            lax.fori_loop(0, 4, send_pack, 0)
            send_second(range(3, SLOTS))
            lax.fori_loop(SIDE_AT[4], TILES, split_tile, 0, unroll=2)

        first, second = nth(2 * i), nth(2 * i + 1)
        cluster(first, 0, second, 1)
        cluster(second, 1, nth(jnp.minimum(2 * i + 2, CLUSTERS - 1)), 0)
        return carry

    lax.fori_loop(0, CLUSTERS // 2, two, 0)

    def send_state(e, carry):
        sent_state[e] = state_rows[leaver(e)]
        pl.when(goes(e))(state_copy(e).start)
        return carry

    lax.fori_loop(0, 4, send_state, 0)

    tail = jnp.where(lax.broadcasted_iota(jnp.int32, (8, POINTS), 0) == ROW_ONE - 8, 1.0, 0.0)

    def expect(e, carry):
        pl.when(comes(e))(pack_copy(e).wait_recv)
        own = jnp.concatenate(split_parts(packed[e, 0:16]), 0)
        mine = left_rows(own, 2)[:, 0:96]
        for pair in range(SLOTS // 2):
            theirs = []
            for k in (2 * pair, 2 * pair + 1):
                tile = jnp.concatenate([packed[e, 16 + 8 * k:24 + 8 * k], tail], 0)
                theirs.append(right_side(jnp.concatenate(split_parts(tile), 0)))
            forms_in[e, pair] = dot(mine, jnp.concatenate(theirs, 1))
        return carry

    lax.fori_loop(0, 4, expect, 0, unroll=4)

    for copy in tag_copies:
        copy.wait()
    for o in range(CLUSTERS):
        source = o
        for e in range(4):
            source = jnp.where(tags[e % 2, 8 * (e // 2), 0] == float(o), CLUSTERS + e, source)
        sources[o] = source

    def arrive(e, carry):
        for k in range(SLOTS):
            pl.when(comes(e))(hist_copy(e, k).wait_recv)
            pair, at = k // 2, pl.ds((k % 2) * POINTS, POINTS)
            rest_sq = forms_in[e, pair, 0:POINTS, at]
            if k == 0:
                rest_sq = rest_sq + apart[...]
            now_sq = jnp.maximum(rest_sq + forms_in[e, pair, POINTS:2 * POINTS, at], TINY)
            stretch = now_sq * lax.rsqrt(now_sq) * lax.rsqrt(rest_sq) - 1.0
            scaled = stretch * packed[e, 16 + 8 * SLOTS + k:17 + 8 * SLOTS + k]
            if k == 0:
                scaled = scaled - apart[...]
            hist_rows[CLUSTERS + e, k] = jnp.maximum(hist_rows[CLUSTERS + e, k], scaled)
        return carry

    lax.fori_loop(0, 4, arrive, 0)

    def finish(e, carry):
        pl.when(comes(e))(state_copy(e).wait_recv)

        @pl.when(goes(e))
        def _():
            for k in range(SLOTS):
                hist_copy(e, k).wait_send()
            pack_copy(e).wait_send()
            state_copy(e).wait_send()
        return carry

    lax.fori_loop(0, 4, finish, 0)


def place_kernel(hist_rows, state_rows, state_in, sources, ref_out, disp_out, vel_out, acc_out, hist_out, states, state_sem, sem):
    copies = []
    for o in range(CLUSTERS):
        copies.append(pltpu.make_async_copy(hist_rows.at[sources[o]], hist_out.at[o], sem.at[o]))
        copies[-1].start()
    for o in range(CLUSTERS):
        source = sources[o]
        rows = jnp.where(source < CLUSTERS, state_rows[o], state_in[jnp.maximum(source - CLUSTERS, 0)])
        for f in range(4):
            for d in range(3):
                states[f, d, o // CN, o % CN:o % CN + 1] = rows[3 * f + d:3 * f + d + 1]
    for f, ref in enumerate((ref_out, disp_out, vel_out, acc_out)):
        copies.append(pltpu.make_async_copy(states.at[f], ref, state_sem.at[f]))
        copies[-1].start()
    for copy in copies:
        copy.wait()


def per_device(
    wide_size, narrow_size,
    ref_local, displacement, velocity, acceleration, history, critical, active, partners, move_src, move_dst,
):
    vmem, smem, anywhere = (pl.BlockSpec(memory_space=m) for m in (pltpu.VMEM, pltpu.SMEM, pl.ANY))
    total = CLUSTERS + 4
    hist_shape = (total, SLOTS, POINTS, POINTS)
    operands = [
        ref_local, displacement, velocity, acceleration, critical, active, partners, move_src, move_dst,
        jnp.asarray(pairing(), BF16), history.reshape(CLUSTERS, SLOTS, POINTS, POINTS),
    ]
    operands = [pltpu.with_memory_space_constraint(x, pltpu.HBM) for x in operands]
    hist_rows, state_rows, state_in, sources = pl.pallas_call(
        functools.partial(step_kernel, wide_size, narrow_size),
        out_shape=(
            pltpu.VMEM(hist_shape, F32),
            pltpu.VMEM((CLUSTERS, 16, POINTS), F32),
            pltpu.VMEM((4, 16, POINTS), F32),
            pltpu.SMEM((CLUSTERS,), jnp.int32),
        ),
        in_specs=[anywhere] * len(operands),
        out_specs=(vmem, vmem, vmem, smem),
        scratch_shapes=[
            *[pltpu.VMEM((CLUSTERS, POINTS, POINTS), F32)] * SLOTS,
            *[pltpu.VMEM(ref_local.shape, F32)] * 4,
            pltpu.SMEM(critical.shape, F32),
            pltpu.SMEM(active.shape, jnp.int32),
            pltpu.SMEM(partners.shape, jnp.int32),
            pltpu.SMEM(move_src.shape, jnp.int32),
            pltpu.SMEM(move_dst.shape, jnp.int32),
            pltpu.VMEM((48, 3 * POINTS), BF16),
            pltpu.SMEM(((CW + 2) * (CN + 2),), jnp.int32),
            pltpu.VMEM((CLUSTERS, 16, POINTS), F32),
            pltpu.VMEM((TILES + 1, 16, POINTS), F32),
            pltpu.VMEM((TILES - CLUSTERS, 16, POINTS), F32),
            pltpu.VMEM((TILES + 1, 48, POINTS), BF16),
            pltpu.VMEM((CLUSTERS, 3 * POINTS, 128), BF16),
            pltpu.VMEM((2, SLOTS // 2, 3 * POINTS, 2 * POINTS), F32),
            pltpu.VMEM((4, SLOTS // 2, 2 * POINTS, 2 * POINTS), F32),
            pltpu.VMEM((POINTS, POINTS), F32),
            pltpu.SMEM((2, 16, POINTS), F32),
            pltpu.VMEM((4, SLOTS, POINTS, POINTS), F32),
            pltpu.VMEM((4, PACK_ROWS, POINTS), F32),
            pltpu.VMEM((4, PACK_ROWS, POINTS), F32),
            pltpu.VMEM((4, 16, POINTS), F32),
            pltpu.SemaphoreType.DMA((10,)),
            pltpu.SemaphoreType.DMA((2,)),
            pltpu.SemaphoreType.DMA((SLOTS,)),
            pltpu.SemaphoreType.DMA((8,)),
            pltpu.SemaphoreType.DMA((8,)),
            *[pltpu.SemaphoreType.DMA((4, SLOTS))] * 2,
            *[pltpu.SemaphoreType.DMA((4,))] * 4,
        ],
        compiler_params=pltpu.CompilerParams(
            collective_id=0, has_side_effects=True, vmem_limit_bytes=26 << 20
        ),
        name="step",
    )(*operands)
    hist_rows = pltpu.with_memory_space_constraint(hist_rows, pltpu.VMEM)
    state_rows = pltpu.with_memory_space_constraint(state_rows, pltpu.VMEM)
    state_in = pltpu.with_memory_space_constraint(state_in, pltpu.VMEM)
    sources = pltpu.with_memory_space_constraint(sources, pltpu.SMEM)
    state = jax.ShapeDtypeStruct(ref_local.shape, F32)
    outs = pl.pallas_call(
        place_kernel,
        out_shape=(state,) * 4 + (jax.ShapeDtypeStruct((CLUSTERS, SLOTS, POINTS, POINTS), F32),),
        in_specs=[anywhere, vmem, vmem, smem],
        out_specs=(anywhere,) * 5,
        scratch_shapes=[
            pltpu.VMEM((4,) + ref_local.shape, F32),
            pltpu.SemaphoreType.DMA((4,)),
            pltpu.SemaphoreType.DMA((CLUSTERS,)),
        ],
        compiler_params=pltpu.CompilerParams(vmem_limit_bytes=8 << 20),
        name="place",
    )(hist_rows, state_rows, state_in, sources)
    return outs[:4] + (outs[4].reshape(history.shape),)


def solution(mesh):
    field = P(None, "wide", "narrow", None)
    blocks = P("wide", "narrow", None)
    hist = P("wide", "narrow", None, None, None)
    moves = P("wide", "narrow", None, None)
    return jax.shard_map(
        functools.partial(per_device, mesh.shape["wide"], mesh.shape["narrow"]),
        mesh=mesh,
        in_specs=(field,) * 4 + (hist,) + (blocks,) * 3 + (moves,) * 2,
        out_specs=(field,) * 4 + (hist,),
        check_vma=False,
    )
```

```python
import functools

import jax
import jax.numpy as jnp
import numpy as np
from jax import lax
from jax.experimental import pallas as pl
from jax.experimental.pallas import tpu as pltpu
from jax.sharding import PartitionSpec as P

STIFFNESS = 8.0
DAMPING = 0.8
TIME_STEP = 0.1
CELL_SPAN = 4.0
FALLOFF = float(-np.log2(np.e) / 9.0)
FAR = 1024.0
APART = 1.0e6
TINY = 1.0e-12

F32 = jnp.float32
BF16 = jnp.bfloat16
MESH = pl.DeviceIdType.MESH
CW = CN = 4
CLUSTERS = CW * CN
SLOTS = 6
POINTS = 128
TILES = CLUSTERS + 22
SIDES = ((-1, 0), (1, 0), (0, -1), (0, 1), (-1, -1), (-1, 1), (1, -1), (1, 1))
SIDE_AT = (16, 21, 26, 30, 34, 35, 36, 37)
SIDE_COUNT = (5, 5, 4, 4, 1, 1, 1, 1)
TAGS_AT = (20, 25)

ROW_R, ROW_U, ROW_V, ROW_Y, ROW_SQ, ROW_ONE = 0, 3, 8, 11, (6, 7, 14), 15
PACK_ROWS = 16 + 8 * SLOTS + 8
PARTS = ((0, 0), (1, 0), (0, 1), (1, 1), (2, 0), (0, 2))


def pairing():
    s = np.zeros((3, 128, 48), np.float32)
    for block, (q, p) in enumerate(PARTS):
        for d in range(3):
            s[0, block * 16 + ROW_R + d, p * 16 + ROW_R + d] = -2
            s[1, block * 16 + ROW_U + d, p * 16 + ROW_Y + d] = -2
            s[1, block * 16 + ROW_R + d, p * 16 + ROW_U + d] = -2
            s[2, block * 16 + ROW_Y + d, p * 16 + ROW_V + d] = -1
            s[2, block * 16 + ROW_V + d, p * 16 + ROW_Y + d] = -1
    for g in range(3):
        for part in range(3):
            s[g, PARTS.index((part, 0)) * 16 + ROW_SQ[g], ROW_ONE] = 1
            s[g, PARTS.index((0, part)) * 16 + ROW_ONE, part * 16 + ROW_SQ[g]] = 1
    return s.reshape(3 * 128, 48).T


def dot(a, b):
    return lax.dot_general(a, b, (((1,), (0,)), ((), ())), preferred_element_type=F32)


def dot_t(a, b):
    return lax.dot_general(a, b, (((1,), (1,)), ((), ())), preferred_element_type=F32)


def tile_index(i, j):
    if 0 <= i < CW and 0 <= j < CN:
        return i * CN + j
    if 0 <= j < CN:
        return (16 if i < 0 else 21) + j
    if 0 <= i < CW:
        return (26 if j < 0 else 30) + i
    return 34 + 2 * (i > 0) + (j > 0)


def step_kernel(
    wide_size, narrow_size,
    ref_hbm, disp_hbm, vel_hbm, acc_hbm, critical_hbm, active_hbm, partners_hbm, src_hbm, dst_hbm, pairs_hbm, history,
    hist_rows, state_rows, state_in, packed, forms_in, sources,
    held_0, held_1, held_2, held_3, held_4, held_5, ref_local, displacement, velocity, acceleration, critical, active, partners, move_src, move_dst, pairs, where_is,
    plain, table, leaving, split, left, forms, apart, tags, raw, pack, sent_state,
    small_sem, tag_sem, load_sem, halo_send, halo_recv, hist_send, hist_recv, pack_send, pack_recv, state_send, state_recv,
):
    held = (held_0, held_1, held_2, held_3, held_4, held_5)
    me_w, me_n = lax.axis_index("wide"), lax.axis_index("narrow")
    def device(dw, dn):
        return (me_w + dw, me_n + dn)

    at_edge = {-1: (me_w == 0, me_n == 0), 1: (me_w == wide_size - 1, me_n == narrow_size - 1)}

    def beyond(dw, dn):
        out = False
        if dw:
            out = out | at_edge[dw][0]
        if dn:
            out = out | at_edge[dn][1]
        return out

    barrier = pltpu.get_barrier_semaphore()
    greeted = 0
    for dw, dn in SIDES[::-1]:
        greeted = greeted + jnp.where(beyond(dw, dn), 0, 1)

        @pl.when(jnp.logical_not(beyond(dw, dn)))
        def _():
            pl.semaphore_signal(barrier, inc=1, device_id=device(dw, dn), device_id_type=MESH)

    small = [
        pltpu.make_async_copy(source, target, small_sem.at[n])
        for n, (source, target) in enumerate((
            (src_hbm, move_src), (ref_hbm, ref_local), (disp_hbm, displacement), (vel_hbm, velocity), (acc_hbm, acceleration),
            (dst_hbm, move_dst), (pairs_hbm, pairs), (critical_hbm, critical), (active_hbm, active), (partners_hbm, partners),
        ))
    ]
    for copy in small:
        copy.start()
    loads = [pltpu.make_async_copy(history.at[:, k], held[k], load_sem.at[k]) for k in range(SLOTS)]
    for copy in loads:
        copy.start()

    sub = lax.broadcasted_iota(jnp.int32, (POINTS, POINTS), 0)
    lane = lax.broadcasted_iota(jnp.int32, (POINTS, POINTS), 1)
    apart[...] = jnp.where(sub == lane, APART, 0.0).astype(F32)
    row = lax.broadcasted_iota(jnp.int32, (16, POINTS), 0)
    far = jnp.where((row == ROW_R) | (row == ROW_Y), FAR, 0.0)
    far = jnp.where(row == ROW_SQ[0], FAR * FAR, far)
    table[TILES] = jnp.where(row == ROW_ONE, 1.0, far)
    for i in range(CW + 2):
        for j in range(CN + 2):
            out = beyond((i == CW + 1) - (i == 0), (j == CN + 1) - (j == 0))
            where_is[i * (CN + 2) + j] = jnp.where(out, TILES, tile_index(i - 1, j - 1))

    def toward(e):
        return device(1 - 2 * lax.rem(e, 2), 0)

    def goes(e):
        return jnp.logical_not(jnp.where(lax.rem(e, 2) == 0, at_edge[1][0], at_edge[-1][0]))

    def comes(e):
        return jnp.logical_not(jnp.where(lax.rem(e, 2) == 0, at_edge[-1][0], at_edge[1][0]))

    def hist_copy(e, k, count):
        return pltpu.make_async_remote_copy(
            src_ref=raw.at[e, pl.ds(k, count)], dst_ref=hist_rows.at[CLUSTERS + e, pl.ds(k, count)],
            send_sem=hist_send.at[e, k], recv_sem=hist_recv.at[e, k],
            device_id=toward(e), device_id_type=MESH,
        )

    def pack_copy(e):
        return pltpu.make_async_remote_copy(
            src_ref=pack.at[e], dst_ref=packed.at[e], send_sem=pack_send.at[e], recv_sem=pack_recv.at[e],
            device_id=toward(e), device_id_type=MESH,
        )

    def state_copy(e):
        return pltpu.make_async_remote_copy(
            src_ref=sent_state.at[e], dst_ref=state_in.at[e],
            send_sem=state_send.at[e], recv_sem=state_recv.at[e],
            device_id=toward(e), device_id_type=MESH,
        )

    def leaver(e):
        return jnp.maximum(move_src[0, 0, lax.rem(e, 2), e // 2], 0)

    def send_hist(e, k, count):
        for n in range(k, k + count):
            raw[e, n] = held[n][leaver(e)]
        hist_copy(e, k, count).start()

    def send_first(k, count):
        for n in range(k, k + count):
            loads[n].wait()
        for e in range(2):
            pl.when(goes(e))(functools.partial(send_hist, e, k, count))

    small[0].wait()
    pl.semaphore_wait(barrier, greeted)
    send_first(0, 1)
    for copy in small[1:6]:
        copy.wait()
    column = lax.broadcasted_iota(jnp.int32, (CN, POINTS), 0)
    anchor_n = column.astype(F32) * CELL_SPAN - CELL_SPAN * CN / 2
    hop_n = jnp.where(column == 0, CELL_SPAN * CN, jnp.where(column == CN - 1, -CELL_SPAN * CN, 0.0))

    def advanced(a):
        base, u, half, v = [], [], [], []
        for d in range(3):
            speed, push = velocity[d, a], acceleration[d, a]
            base.append(ref_local[d, a])
            u.append(displacement[d, a] + TIME_STEP * speed + 0.5 * TIME_STEP * TIME_STEP * push)
            half.append(speed + 0.5 * TIME_STEP * push)
            v.append(half[d] * (DAMPING / STIFFNESS))
        return base, u, half, v

    def tile_rows(a, up_w, up_n, base, u, v):
        r = [base[0] + (CELL_SPAN * (a - CW / 2) + up_w), base[1] + (anchor_n + up_n), base[2] - CELL_SPAN]
        y = [r[d] + u[d] for d in range(3)]
        squares = [
            r[0] * r[0] + r[1] * r[1] + r[2] * r[2],
            u[0] * (r[0] + y[0]) + u[1] * (r[1] + y[1]) + u[2] * (r[2] + y[2]),
            v[0] * y[0] + v[1] * y[1] + v[2] * y[2],
        ]
        return r + u + squares[:2] + v + y + squares[2:] + [jnp.ones_like(u[0])]

    for a in range(CW):
        base, u, half, v = advanced(a)
        for f, row in enumerate(tile_rows(a, 0.0, hop_n, base, u, v)):
            leaving[SIDE_AT[2] - CLUSTERS + a, f:f + 1] = row[0:1]
            leaving[SIDE_AT[3] - CLUSTERS + a, f:f + 1] = row[CN - 1:CN]
        if a in (0, CW - 1):
            side, hop_w = (0, CELL_SPAN * CW) if a == 0 else (1, -CELL_SPAN * CW)
            at = SIDE_AT[side] - CLUSTERS
            for f, row in enumerate(tile_rows(a, hop_w, 0.0, base, u, v)):
                leaving[at:at + CN, f] = row
            at = SIDE_AT[4 + 2 * side] - CLUSTERS
            for f, row in enumerate(tile_rows(a, hop_w, hop_n, base, u, v)):
                leaving[at, f:f + 1] = row[0:1]
                leaving[at + 1, f:f + 1] = row[CN - 1:CN]
    for side in range(2):
        for m in range(2):
            tag = jnp.full((8, POINTS), move_dst[0, 0, 1 - side, m], jnp.int32).astype(F32)
            leaving[TAGS_AT[side] - CLUSTERS, 8 * m:8 * m + 8] = tag

    halos = []
    for n, (dw, dn) in enumerate(SIDES):
        landing = SIDE_AT[SIDES.index((-dw, -dn))]
        halos.append(pltpu.make_async_remote_copy(
            src_ref=leaving.at[pl.ds(SIDE_AT[n] - CLUSTERS, SIDE_COUNT[n])],
            dst_ref=table.at[pl.ds(landing, SIDE_COUNT[n])],
            send_sem=halo_send.at[n], recv_sem=halo_recv.at[n],
            device_id=device(dw, dn), device_id_type=MESH,
        ))
    for n in (0, 1, 4, 5, 6, 7, 2, 3):
        pl.when(jnp.logical_not(beyond(*SIDES[n])))(halos[n].start)
    for n in range(2):
        @pl.when(beyond(*SIDES[n]))
        def _():
            table[TAGS_AT[n]] = jnp.full((16, POINTS), -1.0, F32)


    def split_parts(tile):
        high = tile.astype(BF16)
        rest = tile - high.astype(F32)
        middle = rest.astype(BF16)
        return high, middle, (rest - middle.astype(F32)).astype(BF16)

    def split_tile(t, carry):
        for n, part in enumerate(split_parts(table[t])):
            split[t, n * 16:n * 16 + 16] = part
        return carry

    for copy in small[6:]:
        copy.wait()

    send_first(1, 1)
    for a in range(CW):
        base, u, half, v = advanced(a)
        here = pl.ds(a * CN, CN)
        for f, row in enumerate(base + u + half):
            plain[here, f] = row
        for f in range(9, 16):
            plain[here, f] = jnp.zeros((CN, POINTS), F32)
        for f, row in enumerate(tile_rows(a, 0.0, 0.0, base, u, v)):
            table[here, f] = row

    lax.fori_loop(0, CLUSTERS, split_tile, 0, unroll=4)
    split_tile(TILES, 0)
    send_first(2, 2)

    def left_rows(parts, count):
        turned = jnp.transpose(parts.astype(F32)).astype(BF16)
        wide = dot(turned, pairs[:, 0:count * POINTS]).astype(BF16)
        return jnp.concatenate([wide[:, g * POINTS:(g + 1) * POINTS] for g in range(count)], 0)

    def left_side(c, carry):
        left[c] = left_rows(split[c], 3)
        return carry

    lax.fori_loop(0, CLUSTERS, left_side, 0, unroll=4)
    send_first(4, 2)

    def place_of(c):
        a = lax.shift_right_logical(c, 2)
        return a, c - CN * a

    def partner(c, k):
        a, b = place_of(c)
        o = partners[a, b, k]
        third = lax.shift_right_logical(o * 11, 5)
        spot = where_is[(CN + 2) * (a + third) + b + o - 3 * third]
        return jnp.where(active[a, b, k] > 0, spot, TILES)

    def inverse_limit(c, k, spot):
        a, b = place_of(c)
        return jnp.where(spot == TILES, 0.0, 1.0) / jnp.full((1, POINTS), critical[a, b, k], F32)

    def right_side(tile):
        return jnp.concatenate([tile[q * 16:q * 16 + 16] for q, _ in PARTS], 0)

    def prepare(c, buffer, pair):
        theirs = [right_side(split[partner(c, k)]) for k in (2 * pair, 2 * pair + 1)]
        forms[buffer, pair] = dot(left[c, :, 0:96], jnp.concatenate(theirs, 1))

    def pull(c, buffer, k):
        pair, at = k // 2, pl.ds((k % 2) * POINTS, POINTS)
        spot = partner(c, k)
        rest_sq = forms[buffer, pair, 0:POINTS, at]
        if k == 0:
            rest_sq = rest_sq + apart[...]
        now_sq = jnp.maximum(rest_sq + forms[buffer, pair, POINTS:2 * POINTS, at], TINY)
        rate = forms[buffer, pair, 2 * POINTS:3 * POINTS, at]
        now_inv = lax.rsqrt(now_sq)
        stretch = now_sq * now_inv * lax.rsqrt(rest_sq) - 1.0
        scaled = stretch * inverse_limit(c, k, spot)
        if k == 0:
            scaled = scaled - apart[...]
        hist = jnp.maximum(held[k][c], scaled)
        hist_rows[c, k] = hist
        weight = jnp.exp2(rest_sq * FALLOFF) * jnp.minimum(jnp.maximum(2.0 - hist, 0.0), 1.0)
        factor = weight * (stretch + rate * now_inv) * now_inv
        high = factor.astype(BF16)
        low = (factor - high.astype(F32)).astype(BF16)
        tile = split[spot]
        return dot_t(jnp.concatenate([high, low], 1), jnp.concatenate([tile, tile], 1))

    def cluster(c, buffer, after, after_buffer):
        sums = None
        for pair in range(SLOTS // 2):
            prepare(after, after_buffer, pair)
            for k in (2 * pair, 2 * pair + 1):
                term = pull(c, buffer, k)
                sums = term if sums is None else sums + term
        sums = jnp.transpose(sums)
        sums = sums[0:16] + sums[16:32] + sums[32:48]
        here = table[c]
        own = plain[c]
        acc = STIFFNESS * (sums[ROW_Y:ROW_Y + 3] - here[ROW_Y:ROW_Y + 3] * sums[ROW_ONE:ROW_ONE + 1])
        state_rows[c, 0:6] = own[0:6]
        state_rows[c, 6:9] = own[6:9] + 0.5 * TIME_STEP * acc
        state_rows[c, 9:12] = acc
        state_rows[c, 12:16] = own[12:16]

    tag_copies = [
        pltpu.make_async_copy(table.at[TAGS_AT[side]], tags.at[side], tag_sem.at[side]) for side in range(2)
    ]

    def send_pack(e, carry):
        c = leaver(e)
        pack[e, 0:16] = table[c]
        for k in range(SLOTS):
            spot = partner(c, k)
            pack[e, 16 + 8 * k:24 + 8 * k] = table[spot, 0:8]
            pack[e, 16 + 8 * SLOTS + k:17 + 8 * SLOTS + k] = inverse_limit(c, k, spot)
        pack[e, 16 + 9 * SLOTS:PACK_ROWS] = jnp.zeros((8 - SLOTS, POINTS), F32)
        pl.when(goes(e))(pack_copy(e).start)
        return carry

    def nth(i):
        inner = 5 + lax.rem(i, 2) + 4 * (i // 2)
        column = 4 + 4 * lax.rem(i, 2) + 3 * ((i - 4) // 2)
        row = 1 + lax.rem(i, 2) + 12 * ((i - 8) // 2)
        corner = 3 * lax.rem(i, 2) + 12 * ((i - 12) // 2)
        return jnp.where(i < 4, inner, jnp.where(i < 8, column, jnp.where(i < 12, row, corner)))

    for pair in range(SLOTS // 2):
        prepare(nth(0), 0, pair)

    def landed(sides):
        for n in sides:
            (dw, dn), copy = SIDES[n], halos[n]
            pl.when(jnp.logical_not(beyond(dw, dn)))(copy.wait_send)
            pl.when(jnp.logical_not(beyond(-dw, -dn)))(copy.wait_recv)

    def send_second(k):
        def go(e, carry):
            pl.when(goes(e))(functools.partial(send_hist, e, k, 3))
            return carry

        lax.fori_loop(2, 4, go, 0)

    def two(i, carry):
        @pl.when(i == 1)
        def _():
            send_second(0)
            landed(range(2, 4))
            lax.fori_loop(SIDE_AT[2], SIDE_AT[4], split_tile, 0, unroll=2)

        @pl.when(i == 3)
        def _():
            landed(range(0, 2))
            for copy in tag_copies:
                copy.start()
            lax.fori_loop(CLUSTERS, SIDE_AT[2], split_tile, 0, unroll=2)

        @pl.when(i == 4)
        def _():
            landed(range(4, 8))
            lax.fori_loop(0, 4, send_pack, 0)
            send_second(3)
            lax.fori_loop(SIDE_AT[4], TILES, split_tile, 0, unroll=2)

        first, second = nth(2 * i), nth(2 * i + 1)
        cluster(first, 0, second, 1)
        cluster(second, 1, nth(jnp.minimum(2 * i + 2, CLUSTERS - 1)), 0)
        return carry

    lax.fori_loop(0, CLUSTERS // 2, two, 0)

    def send_state(e, carry):
        sent_state[e] = state_rows[leaver(e)]
        pl.when(goes(e))(state_copy(e).start)
        return carry

    lax.fori_loop(0, 4, send_state, 0)

    tail = jnp.where(lax.broadcasted_iota(jnp.int32, (8, POINTS), 0) == ROW_ONE - 8, 1.0, 0.0)

    def expect(e, carry):
        pl.when(comes(e))(pack_copy(e).wait_recv)
        own = jnp.concatenate(split_parts(packed[e, 0:16]), 0)
        mine = left_rows(own, 2)[:, 0:96]
        for pair in range(SLOTS // 2):
            theirs = []
            for k in (2 * pair, 2 * pair + 1):
                tile = jnp.concatenate([packed[e, 16 + 8 * k:24 + 8 * k], tail], 0)
                theirs.append(right_side(jnp.concatenate(split_parts(tile), 0)))
            forms_in[e, pair] = dot(mine, jnp.concatenate(theirs, 1))
        return carry

    lax.fori_loop(0, 4, expect, 0, unroll=4)

    for copy in tag_copies:
        copy.wait()
    for o in range(CLUSTERS):
        source = o
        for e in range(4):
            source = jnp.where(tags[e % 2, 8 * (e // 2), 0] == float(o), CLUSTERS + e, source)
        sources[o] = source

    def arrive(entries, parts):
        for k, count in parts:
            for e in entries:
                pl.when(comes(e))(hist_copy(e, k, count).wait_recv)

    first, second = ((0, 1), (1, 1), (2, 2), (4, 2)), ((0, 3), (3, 3))
    arrive((0, 1), first)
    arrive((2, 3), second)

    for e in range(4):
        @pl.when(goes(e))
        def _():
            for k, count in first if e < 2 else second:
                hist_copy(e, k, count).wait_send()

    def finish(e, carry):
        pl.when(comes(e))(state_copy(e).wait_recv)

        @pl.when(goes(e))
        def _():
            pack_copy(e).wait_send()
            state_copy(e).wait_send()
        return carry

    lax.fori_loop(0, 4, finish, 0)


def place_kernel(
    hist_rows, state_rows, state_in, packed, forms, sources,
    ref_out, disp_out, vel_out, acc_out, hist_out,
    states, arrived, state_sem, sem,
):
    def stays(o):
        return pltpu.make_async_copy(hist_rows.at[o], hist_out.at[o], sem.at[o])

    def arrives(o):
        return pltpu.make_async_copy(arrived.at[jnp.maximum(sources[o] - CLUSTERS, 0)], hist_out.at[o], sem.at[o])

    for o in range(CLUSTERS):
        pl.when(sources[o] < CLUSTERS)(stays(o).start)

    sub = lax.broadcasted_iota(jnp.int32, (POINTS, POINTS), 0)
    lane = lax.broadcasted_iota(jnp.int32, (POINTS, POINTS), 1)
    same = jnp.where(sub == lane, APART, 0.0).astype(F32)

    def take(e, carry):
        for k in range(SLOTS):
            pair, at = k // 2, pl.ds((k % 2) * POINTS, POINTS)
            rest_sq = forms[e, pair, 0:POINTS, at]
            if k == 0:
                rest_sq = rest_sq + same
            now_sq = jnp.maximum(rest_sq + forms[e, pair, POINTS:2 * POINTS, at], TINY)
            stretch = now_sq * lax.rsqrt(now_sq) * lax.rsqrt(rest_sq) - 1.0
            scaled = stretch * packed[e, 16 + 8 * SLOTS + k:17 + 8 * SLOTS + k]
            if k == 0:
                scaled = scaled - same
            arrived[e, k] = jnp.maximum(hist_rows[CLUSTERS + e, k], scaled)
        return carry

    lax.fori_loop(0, 4, take, 0)
    for o in range(CLUSTERS):
        pl.when(sources[o] >= CLUSTERS)(arrives(o).start)
    for o in range(CLUSTERS):
        source = sources[o]
        rows = jnp.where(source < CLUSTERS, state_rows[o], state_in[jnp.maximum(source - CLUSTERS, 0)])
        for f in range(4):
            for d in range(3):
                states[f, d, o // CN, o % CN:o % CN + 1] = rows[3 * f + d:3 * f + d + 1]
    copies = []
    for f, ref in enumerate((ref_out, disp_out, vel_out, acc_out)):
        copies.append(pltpu.make_async_copy(states.at[f], ref, state_sem.at[f]))
        copies[-1].start()
    for copy in copies:
        copy.wait()
    for o in range(CLUSTERS):
        pl.when(sources[o] < CLUSTERS)(stays(o).wait)
        pl.when(sources[o] >= CLUSTERS)(arrives(o).wait)


def per_device(
    wide_size, narrow_size,
    ref_local, displacement, velocity, acceleration, history, critical, active, partners, move_src, move_dst,
):
    vmem, smem, anywhere = (pl.BlockSpec(memory_space=m) for m in (pltpu.VMEM, pltpu.SMEM, pl.ANY))
    total = CLUSTERS + 4
    hist_shape = (total, SLOTS, POINTS, POINTS)
    operands = [
        ref_local, displacement, velocity, acceleration, critical, active, partners, move_src, move_dst,
        jnp.asarray(pairing(), BF16), history.reshape(CLUSTERS, SLOTS, POINTS, POINTS),
    ]
    operands = [pltpu.with_memory_space_constraint(x, pltpu.HBM) for x in operands]
    *rows, sources = pl.pallas_call(
        functools.partial(step_kernel, wide_size, narrow_size),
        out_shape=(
            pltpu.VMEM(hist_shape, F32),
            pltpu.VMEM((CLUSTERS, 16, POINTS), F32),
            pltpu.VMEM((4, 16, POINTS), F32),
            pltpu.VMEM((4, PACK_ROWS, POINTS), F32),
            pltpu.VMEM((4, SLOTS // 2, 2 * POINTS, 2 * POINTS), F32),
            pltpu.SMEM((CLUSTERS,), jnp.int32),
        ),
        in_specs=[anywhere] * len(operands),
        out_specs=(vmem,) * 5 + (smem,),
        scratch_shapes=[
            *[pltpu.VMEM((CLUSTERS, POINTS, POINTS), F32)] * SLOTS,
            *[pltpu.VMEM(ref_local.shape, F32)] * 4,
            pltpu.SMEM(critical.shape, F32),
            pltpu.SMEM(active.shape, jnp.int32),
            pltpu.SMEM(partners.shape, jnp.int32),
            pltpu.SMEM(move_src.shape, jnp.int32),
            pltpu.SMEM(move_dst.shape, jnp.int32),
            pltpu.VMEM((48, 3 * POINTS), BF16),
            pltpu.SMEM(((CW + 2) * (CN + 2),), jnp.int32),
            pltpu.VMEM((CLUSTERS, 16, POINTS), F32),
            pltpu.VMEM((TILES + 1, 16, POINTS), F32),
            pltpu.VMEM((TILES - CLUSTERS, 16, POINTS), F32),
            pltpu.VMEM((TILES + 1, 48, POINTS), BF16),
            pltpu.VMEM((CLUSTERS, 3 * POINTS, 128), BF16),
            pltpu.VMEM((2, SLOTS // 2, 3 * POINTS, 2 * POINTS), F32),
            pltpu.VMEM((POINTS, POINTS), F32),
            pltpu.SMEM((2, 16, POINTS), F32),
            pltpu.VMEM((4, SLOTS, POINTS, POINTS), F32),
            pltpu.VMEM((4, PACK_ROWS, POINTS), F32),
            pltpu.VMEM((4, 16, POINTS), F32),
            pltpu.SemaphoreType.DMA((10,)),
            pltpu.SemaphoreType.DMA((2,)),
            pltpu.SemaphoreType.DMA((SLOTS,)),
            pltpu.SemaphoreType.DMA((8,)),
            pltpu.SemaphoreType.DMA((8,)),
            *[pltpu.SemaphoreType.DMA((4, SLOTS))] * 2,
            *[pltpu.SemaphoreType.DMA((4,))] * 4,
        ],
        compiler_params=pltpu.CompilerParams(
            collective_id=0, has_side_effects=True, vmem_limit_bytes=26 << 20
        ),
        name="step",
    )(*operands)
    rows = [pltpu.with_memory_space_constraint(x, pltpu.VMEM) for x in rows]
    sources = pltpu.with_memory_space_constraint(sources, pltpu.SMEM)
    state = jax.ShapeDtypeStruct(ref_local.shape, F32)
    outs = pl.pallas_call(
        place_kernel,
        out_shape=(state,) * 4 + (jax.ShapeDtypeStruct((CLUSTERS, SLOTS, POINTS, POINTS), F32),),
        in_specs=[vmem] * 5 + [smem],
        out_specs=(anywhere,) * 5,
        scratch_shapes=[
            pltpu.VMEM((4,) + ref_local.shape, F32),
            pltpu.VMEM((4, SLOTS, POINTS, POINTS), F32),
            pltpu.SemaphoreType.DMA((4,)),
            pltpu.SemaphoreType.DMA((CLUSTERS,)),
        ],
        compiler_params=pltpu.CompilerParams(vmem_limit_bytes=8 << 20),
        name="place",
    )(*rows, sources)
    return outs[:4] + (outs[4].reshape(history.shape),)


def solution(mesh):
    field = P(None, "wide", "narrow", None)
    blocks = P("wide", "narrow", None)
    hist = P("wide", "narrow", None, None, None)
    moves = P("wide", "narrow", None, None)
    return jax.shard_map(
        functools.partial(per_device, mesh.shape["wide"], mesh.shape["narrow"]),
        mesh=mesh,
        in_specs=(field,) * 4 + (hist,) + (blocks,) * 3 + (moves,) * 2,
        out_specs=(field,) * 4 + (hist,),
        check_vma=False,
    )
```

```python
import functools

import jax
import jax.numpy as jnp
import numpy as np
from jax import lax
from jax.experimental import pallas as pl
from jax.experimental.pallas import tpu as pltpu
from jax.sharding import PartitionSpec as P

STIFFNESS = 8.0
DAMPING = 0.8
TIME_STEP = 0.1
CELL_SPAN = 4.0
FALLOFF = float(-np.log2(np.e) / 9.0)
FAR = 1024.0
APART = 1.0e6
TINY = 1.0e-12

F32 = jnp.float32
BF16 = jnp.bfloat16
MESH = pl.DeviceIdType.MESH
CW = CN = 4
CLUSTERS = CW * CN
SLOTS = 6
POINTS = 128
TILES = CLUSTERS + 22
SIDES = ((-1, 0), (1, 0), (0, -1), (0, 1), (-1, -1), (-1, 1), (1, -1), (1, 1))
SIDE_AT = (16, 21, 26, 30, 34, 35, 36, 37)
SIDE_COUNT = (5, 5, 4, 4, 1, 1, 1, 1)
TAGS_AT = (20, 25)

ROW_R, ROW_U, ROW_V, ROW_Y, ROW_SQ, ROW_ONE = 0, 3, 8, 11, (6, 7, 14), 15
PACK_ROWS = 16 + 8 * SLOTS + 8
PARTS = ((0, 0), (1, 0), (0, 1), (1, 1), (2, 0), (0, 2))


def pairing():
    s = np.zeros((3, 128, 48), np.float32)
    for block, (q, p) in enumerate(PARTS):
        for d in range(3):
            s[0, block * 16 + ROW_R + d, p * 16 + ROW_R + d] = -2
            s[1, block * 16 + ROW_U + d, p * 16 + ROW_Y + d] = -2
            s[1, block * 16 + ROW_R + d, p * 16 + ROW_U + d] = -2
            s[2, block * 16 + ROW_Y + d, p * 16 + ROW_V + d] = -1
            s[2, block * 16 + ROW_V + d, p * 16 + ROW_Y + d] = -1
    for g in range(3):
        for part in range(3):
            s[g, PARTS.index((part, 0)) * 16 + ROW_SQ[g], ROW_ONE] = 1
            s[g, PARTS.index((0, part)) * 16 + ROW_ONE, part * 16 + ROW_SQ[g]] = 1
    return s.reshape(3 * 128, 48).T


def dot(a, b):
    return lax.dot_general(a, b, (((1,), (0,)), ((), ())), preferred_element_type=F32)


def dot_t(a, b):
    return lax.dot_general(a, b, (((1,), (1,)), ((), ())), preferred_element_type=F32)


def tile_index(i, j):
    if 0 <= i < CW and 0 <= j < CN:
        return i * CN + j
    if 0 <= j < CN:
        return (16 if i < 0 else 21) + j
    if 0 <= i < CW:
        return (26 if j < 0 else 30) + i
    return 34 + 2 * (i > 0) + (j > 0)


def step_kernel(
    wide_size, narrow_size,
    ref_hbm, disp_hbm, vel_hbm, acc_hbm, critical_hbm, active_hbm, partners_hbm, src_hbm, dst_hbm, pairs_hbm, history,
    hist_rows, state_rows, state_in, packed, forms_in, sources,
    held_0, held_1, held_2, held_3, held_4, held_5, ref_local, displacement, velocity, acceleration, critical, active, partners, move_src, move_dst, pairs, where_is,
    plain, table, leaving, split, left, forms, apart, tags, raw, pack, sent_state,
    small_sem, tag_sem, load_sem, halo_send, halo_recv, hist_send, hist_recv, pack_send, pack_recv, state_send, state_recv,
):
    held = (held_0, held_1, held_2, held_3, held_4, held_5)
    me_w, me_n = lax.axis_index("wide"), lax.axis_index("narrow")
    def device(dw, dn):
        return (me_w + dw, me_n + dn)

    at_edge = {-1: (me_w == 0, me_n == 0), 1: (me_w == wide_size - 1, me_n == narrow_size - 1)}

    def beyond(dw, dn):
        out = False
        if dw:
            out = out | at_edge[dw][0]
        if dn:
            out = out | at_edge[dn][1]
        return out

    barrier = pltpu.get_barrier_semaphore()
    greeted = 0
    for dw, dn in SIDES[::-1]:
        greeted = greeted + jnp.where(beyond(dw, dn), 0, 1)

        @pl.when(jnp.logical_not(beyond(dw, dn)))
        def _():
            pl.semaphore_signal(barrier, inc=1, device_id=device(dw, dn), device_id_type=MESH)

    small = [
        pltpu.make_async_copy(source, target, small_sem.at[n])
        for n, (source, target) in enumerate((
            (src_hbm, move_src), (ref_hbm, ref_local), (disp_hbm, displacement), (vel_hbm, velocity), (acc_hbm, acceleration),
            (dst_hbm, move_dst), (pairs_hbm, pairs), (critical_hbm, critical), (active_hbm, active), (partners_hbm, partners),
        ))
    ]
    for copy in small:
        copy.start()
    loads = [pltpu.make_async_copy(history.at[:, k], held[k], load_sem.at[k]) for k in range(SLOTS)]
    for copy in loads:
        copy.start()

    sub = lax.broadcasted_iota(jnp.int32, (POINTS, POINTS), 0)
    lane = lax.broadcasted_iota(jnp.int32, (POINTS, POINTS), 1)
    apart[...] = jnp.where(sub == lane, APART, 0.0).astype(F32)
    row = lax.broadcasted_iota(jnp.int32, (16, POINTS), 0)
    far = jnp.where((row == ROW_R) | (row == ROW_Y), FAR, 0.0)
    far = jnp.where(row == ROW_SQ[0], FAR * FAR, far)
    table[TILES] = jnp.where(row == ROW_ONE, 1.0, far)
    for i in range(CW + 2):
        for j in range(CN + 2):
            out = beyond((i == CW + 1) - (i == 0), (j == CN + 1) - (j == 0))
            where_is[i * (CN + 2) + j] = jnp.where(out, TILES, tile_index(i - 1, j - 1))

    def toward(e):
        return device(1 - 2 * lax.rem(e, 2), 0)

    def goes(e):
        return jnp.logical_not(jnp.where(lax.rem(e, 2) == 0, at_edge[1][0], at_edge[-1][0]))

    def comes(e):
        return jnp.logical_not(jnp.where(lax.rem(e, 2) == 0, at_edge[-1][0], at_edge[1][0]))

    def hist_copy(e, k, count):
        return pltpu.make_async_remote_copy(
            src_ref=raw.at[e, pl.ds(k, count)], dst_ref=hist_rows.at[CLUSTERS + e, pl.ds(k, count)],
            send_sem=hist_send.at[e, k], recv_sem=hist_recv.at[e, k],
            device_id=toward(e), device_id_type=MESH,
        )

    def pack_copy(e):
        return pltpu.make_async_remote_copy(
            src_ref=pack.at[e], dst_ref=packed.at[e], send_sem=pack_send.at[e], recv_sem=pack_recv.at[e],
            device_id=toward(e), device_id_type=MESH,
        )

    def state_copy(e):
        return pltpu.make_async_remote_copy(
            src_ref=sent_state.at[e], dst_ref=state_in.at[e],
            send_sem=state_send.at[e], recv_sem=state_recv.at[e],
            device_id=toward(e), device_id_type=MESH,
        )

    def leaver(e):
        return jnp.maximum(move_src[0, 0, lax.rem(e, 2), e // 2], 0)

    def send_hist(e, k, count):
        for n in range(k, k + count):
            raw[e, n] = held[n][leaver(e)]
        hist_copy(e, k, count).start()

    def send_first(k, count):
        for n in range(k, k + count):
            loads[n].wait()
        for e in range(2):
            pl.when(goes(e))(functools.partial(send_hist, e, k, count))

    small[0].wait()
    pl.semaphore_wait(barrier, greeted)
    send_first(0, 1)
    for copy in small[1:6]:
        copy.wait()
    column = lax.broadcasted_iota(jnp.int32, (CN, POINTS), 0)
    anchor_n = column.astype(F32) * CELL_SPAN - CELL_SPAN * CN / 2
    hop_n = jnp.where(column == 0, CELL_SPAN * CN, jnp.where(column == CN - 1, -CELL_SPAN * CN, 0.0))

    def advanced(a):
        base, u, half, v = [], [], [], []
        for d in range(3):
            speed, push = velocity[d, a], acceleration[d, a]
            base.append(ref_local[d, a])
            u.append(displacement[d, a] + TIME_STEP * speed + 0.5 * TIME_STEP * TIME_STEP * push)
            half.append(speed + 0.5 * TIME_STEP * push)
            v.append(half[d] * (DAMPING / STIFFNESS))
        return base, u, half, v

    def tile_rows(a, up_w, up_n, base, u, v):
        r = [base[0] + (CELL_SPAN * (a - CW / 2) + up_w), base[1] + (anchor_n + up_n), base[2] - CELL_SPAN]
        y = [r[d] + u[d] for d in range(3)]
        squares = [
            r[0] * r[0] + r[1] * r[1] + r[2] * r[2],
            u[0] * (r[0] + y[0]) + u[1] * (r[1] + y[1]) + u[2] * (r[2] + y[2]),
            v[0] * y[0] + v[1] * y[1] + v[2] * y[2],
        ]
        return r + u + squares[:2] + v + y + squares[2:] + [jnp.ones_like(u[0])]

    for a in range(CW):
        base, u, half, v = advanced(a)
        for f, row in enumerate(tile_rows(a, 0.0, hop_n, base, u, v)):
            leaving[SIDE_AT[2] - CLUSTERS + a, f:f + 1] = row[0:1]
            leaving[SIDE_AT[3] - CLUSTERS + a, f:f + 1] = row[CN - 1:CN]
        if a in (0, CW - 1):
            side, hop_w = (0, CELL_SPAN * CW) if a == 0 else (1, -CELL_SPAN * CW)
            at = SIDE_AT[side] - CLUSTERS
            for f, row in enumerate(tile_rows(a, hop_w, 0.0, base, u, v)):
                leaving[at:at + CN, f] = row
            at = SIDE_AT[4 + 2 * side] - CLUSTERS
            for f, row in enumerate(tile_rows(a, hop_w, hop_n, base, u, v)):
                leaving[at, f:f + 1] = row[0:1]
                leaving[at + 1, f:f + 1] = row[CN - 1:CN]
    for side in range(2):
        for m in range(2):
            tag = jnp.full((8, POINTS), move_dst[0, 0, 1 - side, m], jnp.int32).astype(F32)
            leaving[TAGS_AT[side] - CLUSTERS, 8 * m:8 * m + 8] = tag

    halos = []
    for n, (dw, dn) in enumerate(SIDES):
        landing = SIDE_AT[SIDES.index((-dw, -dn))]
        halos.append(pltpu.make_async_remote_copy(
            src_ref=leaving.at[pl.ds(SIDE_AT[n] - CLUSTERS, SIDE_COUNT[n])],
            dst_ref=table.at[pl.ds(landing, SIDE_COUNT[n])],
            send_sem=halo_send.at[n], recv_sem=halo_recv.at[n],
            device_id=device(dw, dn), device_id_type=MESH,
        ))
    for n in (0, 1, 4, 5, 6, 7, 2, 3):
        pl.when(jnp.logical_not(beyond(*SIDES[n])))(halos[n].start)
    for n in range(2):
        @pl.when(beyond(*SIDES[n]))
        def _():
            table[TAGS_AT[n]] = jnp.full((16, POINTS), -1.0, F32)


    def split_parts(tile):
        high = tile.astype(BF16)
        rest = tile - high.astype(F32)
        middle = rest.astype(BF16)
        return high, middle, (rest - middle.astype(F32)).astype(BF16)

    def split_tile(t, carry):
        for n, part in enumerate(split_parts(table[t])):
            split[t, n * 16:n * 16 + 16] = part
        return carry

    for copy in small[6:]:
        copy.wait()

    send_first(1, 1)
    for a in range(CW):
        base, u, half, v = advanced(a)
        here = pl.ds(a * CN, CN)
        for f, row in enumerate(base + u + half):
            plain[here, f] = row
        for f in range(9, 16):
            plain[here, f] = jnp.zeros((CN, POINTS), F32)
        for f, row in enumerate(tile_rows(a, 0.0, 0.0, base, u, v)):
            table[here, f] = row

    lax.fori_loop(0, CLUSTERS, split_tile, 0, unroll=4)
    split_tile(TILES, 0)
    send_first(2, 2)

    def left_rows(parts, count):
        turned = jnp.transpose(parts.astype(F32)).astype(BF16)
        wide = dot(turned, pairs[:, 0:count * POINTS]).astype(BF16)
        return jnp.concatenate([wide[:, g * POINTS:(g + 1) * POINTS] for g in range(count)], 0)

    def left_side(c, carry):
        left[c] = left_rows(split[c], 3)
        return carry

    lax.fori_loop(0, CLUSTERS, left_side, 0, unroll=4)
    send_first(4, 2)

    def place_of(c):
        a = lax.shift_right_logical(c, 2)
        return a, c - CN * a

    def partner(c, k):
        a, b = place_of(c)
        o = partners[a, b, k]
        third = lax.shift_right_logical(o * 11, 5)
        spot = where_is[(CN + 2) * (a + third) + b + o - 3 * third]
        return jnp.where(active[a, b, k] > 0, spot, TILES)

    def inverse_limit(c, k, spot):
        a, b = place_of(c)
        return jnp.where(spot == TILES, 0.0, 1.0) / jnp.full((1, POINTS), critical[a, b, k], F32)

    def right_side(tile):
        return jnp.concatenate([tile[q * 16:q * 16 + 16] for q, _ in PARTS], 0)

    def prepare(c, buffer, pair):
        theirs = [right_side(split[partner(c, k)]) for k in (2 * pair, 2 * pair + 1)]
        forms[buffer, pair] = dot(left[c, :, 0:96], jnp.concatenate(theirs, 1))

    def pull(c, buffer, k):
        pair, at = k // 2, pl.ds((k % 2) * POINTS, POINTS)
        spot = partner(c, k)
        rest_sq = forms[buffer, pair, 0:POINTS, at]
        if k == 0:
            rest_sq = rest_sq + apart[...]
        now_sq = jnp.maximum(rest_sq + forms[buffer, pair, POINTS:2 * POINTS, at], TINY)
        rate = forms[buffer, pair, 2 * POINTS:3 * POINTS, at]
        now_inv = lax.rsqrt(now_sq)
        stretch = now_sq * now_inv * lax.rsqrt(rest_sq) - 1.0
        scaled = stretch * inverse_limit(c, k, spot)
        if k == 0:
            scaled = scaled - apart[...]
        hist = jnp.maximum(held[k][c], scaled)
        hist_rows[c, k] = hist
        weight = jnp.exp2(rest_sq * FALLOFF) * jnp.minimum(jnp.maximum(2.0 - hist, 0.0), 1.0)
        factor = weight * (stretch + rate * now_inv) * now_inv
        high = factor.astype(BF16)
        low = (factor - high.astype(F32)).astype(BF16)
        tile = split[spot]
        return dot_t(jnp.concatenate([high, low], 1), jnp.concatenate([tile, tile], 1))

    def cluster(c, buffer, after, after_buffer):
        sums = None
        for pair in range(SLOTS // 2):
            prepare(after, after_buffer, pair)
            for k in (2 * pair, 2 * pair + 1):
                term = pull(c, buffer, k)
                sums = term if sums is None else sums + term
        sums = jnp.transpose(sums)
        sums = sums[0:16] + sums[16:32] + sums[32:48]
        here = table[c]
        own = plain[c]
        acc = STIFFNESS * (sums[ROW_Y:ROW_Y + 3] - here[ROW_Y:ROW_Y + 3] * sums[ROW_ONE:ROW_ONE + 1])
        state_rows[c, 0:6] = own[0:6]
        state_rows[c, 6:9] = own[6:9] + 0.5 * TIME_STEP * acc
        state_rows[c, 9:12] = acc
        state_rows[c, 12:16] = own[12:16]

    tag_copies = [
        pltpu.make_async_copy(table.at[TAGS_AT[side]], tags.at[side], tag_sem.at[side]) for side in range(2)
    ]

    def send_pack(e, carry):
        c = leaver(e)
        pack[e, 0:16] = table[c]
        for k in range(SLOTS):
            spot = partner(c, k)
            pack[e, 16 + 8 * k:24 + 8 * k] = table[spot, 0:8]
            pack[e, 16 + 8 * SLOTS + k:17 + 8 * SLOTS + k] = inverse_limit(c, k, spot)
        pack[e, 16 + 9 * SLOTS:PACK_ROWS] = jnp.zeros((8 - SLOTS, POINTS), F32)
        pl.when(goes(e))(pack_copy(e).start)
        return carry

    def nth(i):
        inner = 5 + lax.rem(i, 2) + 4 * (i // 2)
        column = 4 + 4 * lax.rem(i, 2) + 3 * ((i - 4) // 2)
        row = 1 + lax.rem(i, 2) + 12 * ((i - 8) // 2)
        corner = 3 * lax.rem(i, 2) + 12 * ((i - 12) // 2)
        return jnp.where(i < 4, inner, jnp.where(i < 8, column, jnp.where(i < 12, row, corner)))

    for pair in range(SLOTS // 2):
        prepare(nth(0), 0, pair)

    def landed(sides):
        for n in sides:
            (dw, dn), copy = SIDES[n], halos[n]
            pl.when(jnp.logical_not(beyond(dw, dn)))(copy.wait_send)
            pl.when(jnp.logical_not(beyond(-dw, -dn)))(copy.wait_recv)

    def send_second(k, count):
        def go(e, carry):
            pl.when(goes(e))(functools.partial(send_hist, e, k, count))
            return carry

        lax.fori_loop(2, 4, go, 0)

    def two(i, carry):
        @pl.when(i == 1)
        def _():
            send_second(0, 2)
            landed(range(2, 4))
            lax.fori_loop(SIDE_AT[2], SIDE_AT[4], split_tile, 0, unroll=2)

        @pl.when(i == 3)
        def _():
            landed(range(0, 2))
            for copy in tag_copies:
                copy.start()
            lax.fori_loop(CLUSTERS, SIDE_AT[2], split_tile, 0, unroll=2)

        @pl.when(i == 4)
        def _():
            landed(range(4, 8))
            lax.fori_loop(0, 4, send_pack, 0)
            send_second(2, 4)
            lax.fori_loop(SIDE_AT[4], TILES, split_tile, 0, unroll=2)

        first, second = nth(2 * i), nth(2 * i + 1)
        cluster(first, 0, second, 1)
        cluster(second, 1, nth(jnp.minimum(2 * i + 2, CLUSTERS - 1)), 0)
        return carry

    lax.fori_loop(0, CLUSTERS // 2, two, 0)

    def send_state(e, carry):
        sent_state[e] = state_rows[leaver(e)]
        pl.when(goes(e))(state_copy(e).start)
        return carry

    lax.fori_loop(0, 4, send_state, 0)

    tail = jnp.where(lax.broadcasted_iota(jnp.int32, (8, POINTS), 0) == ROW_ONE - 8, 1.0, 0.0)

    def expect(e, carry):
        pl.when(comes(e))(pack_copy(e).wait_recv)
        own = jnp.concatenate(split_parts(packed[e, 0:16]), 0)
        mine = left_rows(own, 2)[:, 0:96]
        for pair in range(SLOTS // 2):
            theirs = []
            for k in (2 * pair, 2 * pair + 1):
                tile = jnp.concatenate([packed[e, 16 + 8 * k:24 + 8 * k], tail], 0)
                theirs.append(right_side(jnp.concatenate(split_parts(tile), 0)))
            forms_in[e, pair] = dot(mine, jnp.concatenate(theirs, 1))
        return carry

    lax.fori_loop(0, 4, expect, 0, unroll=4)

    for copy in tag_copies:
        copy.wait()
    for o in range(CLUSTERS):
        source = o
        for e in range(4):
            source = jnp.where(tags[e % 2, 8 * (e // 2), 0] == float(o), CLUSTERS + e, source)
        sources[o] = source

    def arrive(entries, parts):
        for k, count in parts:
            for e in entries:
                pl.when(comes(e))(hist_copy(e, k, count).wait_recv)

    first, second = ((0, 1), (1, 1), (2, 2), (4, 2)), ((0, 2), (2, 4))
    arrive((0, 1), first)
    arrive((2, 3), second)

    for e in range(4):
        @pl.when(goes(e))
        def _():
            for k, count in first if e < 2 else second:
                hist_copy(e, k, count).wait_send()

    def finish(e, carry):
        pl.when(comes(e))(state_copy(e).wait_recv)

        @pl.when(goes(e))
        def _():
            pack_copy(e).wait_send()
            state_copy(e).wait_send()
        return carry

    lax.fori_loop(0, 4, finish, 0)


def place_kernel(
    hist_rows, state_rows, state_in, packed, forms, sources,
    ref_out, disp_out, vel_out, acc_out, hist_out,
    states, arrived, state_sem, sem,
):
    def stays(o):
        return pltpu.make_async_copy(hist_rows.at[o], hist_out.at[o], sem.at[o])

    def arrives(o):
        return pltpu.make_async_copy(arrived.at[jnp.maximum(sources[o] - CLUSTERS, 0)], hist_out.at[o], sem.at[o])

    for o in range(CLUSTERS):
        pl.when(sources[o] < CLUSTERS)(stays(o).start)

    sub = lax.broadcasted_iota(jnp.int32, (POINTS, POINTS), 0)
    lane = lax.broadcasted_iota(jnp.int32, (POINTS, POINTS), 1)
    same = jnp.where(sub == lane, APART, 0.0).astype(F32)

    def take(e, carry):
        for k in range(SLOTS):
            pair, at = k // 2, pl.ds((k % 2) * POINTS, POINTS)
            rest_sq = forms[e, pair, 0:POINTS, at]
            if k == 0:
                rest_sq = rest_sq + same
            now_sq = jnp.maximum(rest_sq + forms[e, pair, POINTS:2 * POINTS, at], TINY)
            stretch = now_sq * lax.rsqrt(now_sq) * lax.rsqrt(rest_sq) - 1.0
            scaled = stretch * packed[e, 16 + 8 * SLOTS + k:17 + 8 * SLOTS + k]
            if k == 0:
                scaled = scaled - same
            arrived[e, k] = jnp.maximum(hist_rows[CLUSTERS + e, k], scaled)
        return carry

    lax.fori_loop(0, 4, take, 0)
    for o in range(CLUSTERS):
        pl.when(sources[o] >= CLUSTERS)(arrives(o).start)
    for o in range(CLUSTERS):
        source = sources[o]
        rows = jnp.where(source < CLUSTERS, state_rows[o], state_in[jnp.maximum(source - CLUSTERS, 0)])
        for f in range(4):
            for d in range(3):
                states[f, d, o // CN, o % CN:o % CN + 1] = rows[3 * f + d:3 * f + d + 1]
    copies = []
    for f, ref in enumerate((ref_out, disp_out, vel_out, acc_out)):
        copies.append(pltpu.make_async_copy(states.at[f], ref, state_sem.at[f]))
        copies[-1].start()
    for copy in copies:
        copy.wait()
    for o in range(CLUSTERS):
        pl.when(sources[o] < CLUSTERS)(stays(o).wait)
        pl.when(sources[o] >= CLUSTERS)(arrives(o).wait)


def per_device(
    wide_size, narrow_size,
    ref_local, displacement, velocity, acceleration, history, critical, active, partners, move_src, move_dst,
):
    vmem, smem, anywhere = (pl.BlockSpec(memory_space=m) for m in (pltpu.VMEM, pltpu.SMEM, pl.ANY))
    total = CLUSTERS + 4
    hist_shape = (total, SLOTS, POINTS, POINTS)
    operands = [
        ref_local, displacement, velocity, acceleration, critical, active, partners, move_src, move_dst,
        jnp.asarray(pairing(), BF16), history.reshape(CLUSTERS, SLOTS, POINTS, POINTS),
    ]
    operands = [pltpu.with_memory_space_constraint(x, pltpu.HBM) for x in operands]
    *rows, sources = pl.pallas_call(
        functools.partial(step_kernel, wide_size, narrow_size),
        out_shape=(
            pltpu.VMEM(hist_shape, F32),
            pltpu.VMEM((CLUSTERS, 16, POINTS), F32),
            pltpu.VMEM((4, 16, POINTS), F32),
            pltpu.VMEM((4, PACK_ROWS, POINTS), F32),
            pltpu.VMEM((4, SLOTS // 2, 2 * POINTS, 2 * POINTS), F32),
            pltpu.SMEM((CLUSTERS,), jnp.int32),
        ),
        in_specs=[anywhere] * len(operands),
        out_specs=(vmem,) * 5 + (smem,),
        scratch_shapes=[
            *[pltpu.VMEM((CLUSTERS, POINTS, POINTS), F32)] * SLOTS,
            *[pltpu.VMEM(ref_local.shape, F32)] * 4,
            pltpu.SMEM(critical.shape, F32),
            pltpu.SMEM(active.shape, jnp.int32),
            pltpu.SMEM(partners.shape, jnp.int32),
            pltpu.SMEM(move_src.shape, jnp.int32),
            pltpu.SMEM(move_dst.shape, jnp.int32),
            pltpu.VMEM((48, 3 * POINTS), BF16),
            pltpu.SMEM(((CW + 2) * (CN + 2),), jnp.int32),
            pltpu.VMEM((CLUSTERS, 16, POINTS), F32),
            pltpu.VMEM((TILES + 1, 16, POINTS), F32),
            pltpu.VMEM((TILES - CLUSTERS, 16, POINTS), F32),
            pltpu.VMEM((TILES + 1, 48, POINTS), BF16),
            pltpu.VMEM((CLUSTERS, 3 * POINTS, 128), BF16),
            pltpu.VMEM((2, SLOTS // 2, 3 * POINTS, 2 * POINTS), F32),
            pltpu.VMEM((POINTS, POINTS), F32),
            pltpu.SMEM((2, 16, POINTS), F32),
            pltpu.VMEM((4, SLOTS, POINTS, POINTS), F32),
            pltpu.VMEM((4, PACK_ROWS, POINTS), F32),
            pltpu.VMEM((4, 16, POINTS), F32),
            pltpu.SemaphoreType.DMA((10,)),
            pltpu.SemaphoreType.DMA((2,)),
            pltpu.SemaphoreType.DMA((SLOTS,)),
            pltpu.SemaphoreType.DMA((8,)),
            pltpu.SemaphoreType.DMA((8,)),
            *[pltpu.SemaphoreType.DMA((4, SLOTS))] * 2,
            *[pltpu.SemaphoreType.DMA((4,))] * 4,
        ],
        compiler_params=pltpu.CompilerParams(
            collective_id=0, has_side_effects=True, vmem_limit_bytes=26 << 20
        ),
        name="step",
    )(*operands)
    rows = [pltpu.with_memory_space_constraint(x, pltpu.VMEM) for x in rows]
    sources = pltpu.with_memory_space_constraint(sources, pltpu.SMEM)
    state = jax.ShapeDtypeStruct(ref_local.shape, F32)
    outs = pl.pallas_call(
        place_kernel,
        out_shape=(state,) * 4 + (jax.ShapeDtypeStruct((CLUSTERS, SLOTS, POINTS, POINTS), F32),),
        in_specs=[vmem] * 5 + [smem],
        out_specs=(anywhere,) * 5,
        scratch_shapes=[
            pltpu.VMEM((4,) + ref_local.shape, F32),
            pltpu.VMEM((4, SLOTS, POINTS, POINTS), F32),
            pltpu.SemaphoreType.DMA((4,)),
            pltpu.SemaphoreType.DMA((CLUSTERS,)),
        ],
        compiler_params=pltpu.CompilerParams(vmem_limit_bytes=8 << 20),
        name="place",
    )(*rows, sources)
    return outs[:4] + (outs[4].reshape(history.shape),)


def solution(mesh):
    field = P(None, "wide", "narrow", None)
    blocks = P("wide", "narrow", None)
    hist = P("wide", "narrow", None, None, None)
    moves = P("wide", "narrow", None, None)
    return jax.shard_map(
        functools.partial(per_device, mesh.shape["wide"], mesh.shape["narrow"]),
        mesh=mesh,
        in_specs=(field,) * 4 + (hist,) + (blocks,) * 3 + (moves,) * 2,
        out_specs=(field,) * 4 + (hist,),
        check_vma=False,
    )
```

```python
import functools

import jax
import jax.numpy as jnp
import numpy as np
from jax import lax
from jax.experimental import pallas as pl
from jax.experimental.pallas import tpu as pltpu
from jax.sharding import PartitionSpec as P

STIFFNESS = 8.0
DAMPING = 0.8
TIME_STEP = 0.1
CELL_SPAN = 4.0
FALLOFF = float(-np.log2(np.e) / 9.0)
FAR = 1024.0
APART = 1.0e6
TINY = 1.0e-12

F32 = jnp.float32
BF16 = jnp.bfloat16
MESH = pl.DeviceIdType.MESH
CW = CN = 4
CLUSTERS = CW * CN
SLOTS = 6
POINTS = 128
TILES = CLUSTERS + 22
SIDES = ((-1, 0), (1, 0), (0, -1), (0, 1), (-1, -1), (-1, 1), (1, -1), (1, 1))
SIDE_AT = (16, 21, 26, 30, 34, 35, 36, 37)
SIDE_COUNT = (5, 5, 4, 4, 1, 1, 1, 1)
TAGS_AT = (20, 25)

ROW_R, ROW_U, ROW_V, ROW_Y, ROW_SQ, ROW_ONE = 0, 3, 8, 11, (6, 7, 14), 15
PACK_ROWS = 16 + 8 * SLOTS + 8
PARTS = ((0, 0), (1, 0), (0, 1), (1, 1), (2, 0), (0, 2))


def pairing():
    s = np.zeros((3, 128, 48), np.float32)
    for block, (q, p) in enumerate(PARTS):
        for d in range(3):
            s[0, block * 16 + ROW_R + d, p * 16 + ROW_R + d] = -2
            s[1, block * 16 + ROW_U + d, p * 16 + ROW_Y + d] = -2
            s[1, block * 16 + ROW_R + d, p * 16 + ROW_U + d] = -2
            s[2, block * 16 + ROW_Y + d, p * 16 + ROW_V + d] = -1
            s[2, block * 16 + ROW_V + d, p * 16 + ROW_Y + d] = -1
    for g in range(3):
        for part in range(3):
            s[g, PARTS.index((part, 0)) * 16 + ROW_SQ[g], ROW_ONE] = 1
            s[g, PARTS.index((0, part)) * 16 + ROW_ONE, part * 16 + ROW_SQ[g]] = 1
    return s.reshape(3 * 128, 48).T


def dot(a, b):
    return lax.dot_general(a, b, (((1,), (0,)), ((), ())), preferred_element_type=F32)


def dot_t(a, b):
    return lax.dot_general(a, b, (((1,), (1,)), ((), ())), preferred_element_type=F32)


def tile_index(i, j):
    if 0 <= i < CW and 0 <= j < CN:
        return i * CN + j
    if 0 <= j < CN:
        return (16 if i < 0 else 21) + j
    if 0 <= i < CW:
        return (26 if j < 0 else 30) + i
    return 34 + 2 * (i > 0) + (j > 0)


def step_kernel(
    wide_size, narrow_size,
    ref_hbm, disp_hbm, vel_hbm, acc_hbm, critical_hbm, active_hbm, partners_hbm, src_hbm, dst_hbm, pairs_hbm, history,
    hist_rows, state_rows, state_in, packed, forms_in, sources,
    held_0, held_1, held_2, held_3, held_4, held_5, ref_local, displacement, velocity, acceleration, critical, active, partners, move_src, move_dst, pairs, where_is,
    plain, table, leaving, split, left, forms, apart, tags, raw, pack, sent_state,
    small_sem, tag_sem, load_sem, halo_send, halo_recv, hist_send, hist_recv, pack_send, pack_recv, state_send, state_recv,
):
    held = (held_0, held_1, held_2, held_3, held_4, held_5)
    me_w, me_n = lax.axis_index("wide"), lax.axis_index("narrow")
    def device(dw, dn):
        return (me_w + dw, me_n + dn)

    at_edge = {-1: (me_w == 0, me_n == 0), 1: (me_w == wide_size - 1, me_n == narrow_size - 1)}

    def beyond(dw, dn):
        out = False
        if dw:
            out = out | at_edge[dw][0]
        if dn:
            out = out | at_edge[dn][1]
        return out

    barrier = pltpu.get_barrier_semaphore()
    greeted = 0
    for dw, dn in SIDES[::-1]:
        greeted = greeted + jnp.where(beyond(dw, dn), 0, 1)

        @pl.when(jnp.logical_not(beyond(dw, dn)))
        def _():
            pl.semaphore_signal(barrier, inc=1, device_id=device(dw, dn), device_id_type=MESH)

    small = [
        pltpu.make_async_copy(source, target, small_sem.at[n])
        for n, (source, target) in enumerate((
            (src_hbm, move_src), (ref_hbm, ref_local), (disp_hbm, displacement), (vel_hbm, velocity), (acc_hbm, acceleration),
            (dst_hbm, move_dst), (pairs_hbm, pairs), (critical_hbm, critical), (active_hbm, active), (partners_hbm, partners),
        ))
    ]
    loads = [pltpu.make_async_copy(history.at[:, k], held[k], load_sem.at[k]) for k in range(SLOTS)]
    for copy in [small[0], loads[0]] + small[1:] + loads[1:]:
        copy.start()

    sub = lax.broadcasted_iota(jnp.int32, (POINTS, POINTS), 0)
    lane = lax.broadcasted_iota(jnp.int32, (POINTS, POINTS), 1)
    apart[...] = jnp.where(sub == lane, APART, 0.0).astype(F32)
    row = lax.broadcasted_iota(jnp.int32, (16, POINTS), 0)
    far = jnp.where((row == ROW_R) | (row == ROW_Y), FAR, 0.0)
    far = jnp.where(row == ROW_SQ[0], FAR * FAR, far)
    table[TILES] = jnp.where(row == ROW_ONE, 1.0, far)
    for i in range(CW + 2):
        for j in range(CN + 2):
            out = beyond((i == CW + 1) - (i == 0), (j == CN + 1) - (j == 0))
            where_is[i * (CN + 2) + j] = jnp.where(out, TILES, tile_index(i - 1, j - 1))

    def toward(e):
        return device(1 - 2 * lax.rem(e, 2), 0)

    def goes(e):
        return jnp.logical_not(jnp.where(lax.rem(e, 2) == 0, at_edge[1][0], at_edge[-1][0]))

    def comes(e):
        return jnp.logical_not(jnp.where(lax.rem(e, 2) == 0, at_edge[-1][0], at_edge[1][0]))

    def hist_copy(e, k, count):
        return pltpu.make_async_remote_copy(
            src_ref=raw.at[e, pl.ds(k, count)], dst_ref=hist_rows.at[CLUSTERS + e, pl.ds(k, count)],
            send_sem=hist_send.at[e, k], recv_sem=hist_recv.at[e, k],
            device_id=toward(e), device_id_type=MESH,
        )

    def pack_copy(e):
        return pltpu.make_async_remote_copy(
            src_ref=pack.at[e], dst_ref=packed.at[e], send_sem=pack_send.at[e], recv_sem=pack_recv.at[e],
            device_id=toward(e), device_id_type=MESH,
        )

    def state_copy(e):
        return pltpu.make_async_remote_copy(
            src_ref=sent_state.at[e], dst_ref=state_in.at[e],
            send_sem=state_send.at[e], recv_sem=state_recv.at[e],
            device_id=toward(e), device_id_type=MESH,
        )

    def leaver(e):
        return jnp.maximum(move_src[0, 0, lax.rem(e, 2), e // 2], 0)

    def send_hist(e, k, count):
        for n in range(k, k + count):
            raw[e, n] = held[n][leaver(e)]
        hist_copy(e, k, count).start()

    def send_first(k, count):
        for n in range(k, k + count):
            loads[n].wait()
        for e in range(2):
            pl.when(goes(e))(functools.partial(send_hist, e, k, count))

    small[0].wait()
    pl.semaphore_wait(barrier, greeted)
    send_first(0, 1)
    for copy in small[1:6]:
        copy.wait()
    column = lax.broadcasted_iota(jnp.int32, (CN, POINTS), 0)
    anchor_n = column.astype(F32) * CELL_SPAN - CELL_SPAN * CN / 2
    hop_n = jnp.where(column == 0, CELL_SPAN * CN, jnp.where(column == CN - 1, -CELL_SPAN * CN, 0.0))

    def advanced(a):
        base, u, half, v = [], [], [], []
        for d in range(3):
            speed, push = velocity[d, a], acceleration[d, a]
            base.append(ref_local[d, a])
            u.append(displacement[d, a] + TIME_STEP * speed + 0.5 * TIME_STEP * TIME_STEP * push)
            half.append(speed + 0.5 * TIME_STEP * push)
            v.append(half[d] * (DAMPING / STIFFNESS))
        return base, u, half, v

    def tile_rows(a, up_w, up_n, base, u, v):
        r = [base[0] + (CELL_SPAN * (a - CW / 2) + up_w), base[1] + (anchor_n + up_n), base[2] - CELL_SPAN]
        y = [r[d] + u[d] for d in range(3)]
        squares = [
            r[0] * r[0] + r[1] * r[1] + r[2] * r[2],
            u[0] * (r[0] + y[0]) + u[1] * (r[1] + y[1]) + u[2] * (r[2] + y[2]),
            v[0] * y[0] + v[1] * y[1] + v[2] * y[2],
        ]
        return r + u + squares[:2] + v + y + squares[2:] + [jnp.ones_like(u[0])]

    for a in range(CW):
        base, u, half, v = advanced(a)
        for f, row in enumerate(tile_rows(a, 0.0, hop_n, base, u, v)):
            leaving[SIDE_AT[2] - CLUSTERS + a, f:f + 1] = row[0:1]
            leaving[SIDE_AT[3] - CLUSTERS + a, f:f + 1] = row[CN - 1:CN]
        if a in (0, CW - 1):
            side, hop_w = (0, CELL_SPAN * CW) if a == 0 else (1, -CELL_SPAN * CW)
            at = SIDE_AT[side] - CLUSTERS
            for f, row in enumerate(tile_rows(a, hop_w, 0.0, base, u, v)):
                leaving[at:at + CN, f] = row
            at = SIDE_AT[4 + 2 * side] - CLUSTERS
            for f, row in enumerate(tile_rows(a, hop_w, hop_n, base, u, v)):
                leaving[at, f:f + 1] = row[0:1]
                leaving[at + 1, f:f + 1] = row[CN - 1:CN]
    for side in range(2):
        for m in range(2):
            tag = jnp.full((8, POINTS), move_dst[0, 0, 1 - side, m], jnp.int32).astype(F32)
            leaving[TAGS_AT[side] - CLUSTERS, 8 * m:8 * m + 8] = tag

    halos = []
    for n, (dw, dn) in enumerate(SIDES):
        landing = SIDE_AT[SIDES.index((-dw, -dn))]
        halos.append(pltpu.make_async_remote_copy(
            src_ref=leaving.at[pl.ds(SIDE_AT[n] - CLUSTERS, SIDE_COUNT[n])],
            dst_ref=table.at[pl.ds(landing, SIDE_COUNT[n])],
            send_sem=halo_send.at[n], recv_sem=halo_recv.at[n],
            device_id=device(dw, dn), device_id_type=MESH,
        ))
    for n in (0, 1, 4, 5, 6, 7, 2, 3):
        pl.when(jnp.logical_not(beyond(*SIDES[n])))(halos[n].start)
    for n in range(2):
        @pl.when(beyond(*SIDES[n]))
        def _():
            table[TAGS_AT[n]] = jnp.full((16, POINTS), -1.0, F32)


    def split_parts(tile):
        high = tile.astype(BF16)
        rest = tile - high.astype(F32)
        middle = rest.astype(BF16)
        return high, middle, (rest - middle.astype(F32)).astype(BF16)

    def split_tile(t, carry):
        for n, part in enumerate(split_parts(table[t])):
            split[t, n * 16:n * 16 + 16] = part
        return carry

    for copy in small[6:]:
        copy.wait()

    send_first(1, 1)
    for a in range(CW):
        base, u, half, v = advanced(a)
        here = pl.ds(a * CN, CN)
        for f, row in enumerate(base + u + half):
            plain[here, f] = row
        for f in range(9, 16):
            plain[here, f] = jnp.zeros((CN, POINTS), F32)
        for f, row in enumerate(tile_rows(a, 0.0, 0.0, base, u, v)):
            table[here, f] = row

    lax.fori_loop(0, CLUSTERS, split_tile, 0, unroll=4)
    split_tile(TILES, 0)
    send_first(2, 2)

    def left_rows(parts, count):
        turned = jnp.transpose(parts.astype(F32)).astype(BF16)
        wide = dot(turned, pairs[:, 0:count * POINTS]).astype(BF16)
        return jnp.concatenate([wide[:, g * POINTS:(g + 1) * POINTS] for g in range(count)], 0)

    def left_side(c, carry):
        left[c] = left_rows(split[c], 3)
        return carry

    lax.fori_loop(0, CLUSTERS, left_side, 0, unroll=4)
    send_first(4, 2)

    def place_of(c):
        a = lax.shift_right_logical(c, 2)
        return a, c - CN * a

    def partner(c, k):
        a, b = place_of(c)
        o = partners[a, b, k]
        third = lax.shift_right_logical(o * 11, 5)
        spot = where_is[(CN + 2) * (a + third) + b + o - 3 * third]
        return jnp.where(active[a, b, k] > 0, spot, TILES)

    def inverse_limit(c, k, spot):
        a, b = place_of(c)
        return jnp.where(spot == TILES, 0.0, 1.0) / jnp.full((1, POINTS), critical[a, b, k], F32)

    def right_side(tile):
        return jnp.concatenate([tile[q * 16:q * 16 + 16] for q, _ in PARTS], 0)

    def prepare(c, buffer, pair):
        theirs = [right_side(split[partner(c, k)]) for k in (2 * pair, 2 * pair + 1)]
        forms[buffer, pair] = dot(left[c, :, 0:96], jnp.concatenate(theirs, 1))

    def pull(c, buffer, k):
        pair, at = k // 2, pl.ds((k % 2) * POINTS, POINTS)
        spot = partner(c, k)
        rest_sq = forms[buffer, pair, 0:POINTS, at]
        if k == 0:
            rest_sq = rest_sq + apart[...]
        now_sq = jnp.maximum(rest_sq + forms[buffer, pair, POINTS:2 * POINTS, at], TINY)
        rate = forms[buffer, pair, 2 * POINTS:3 * POINTS, at]
        now_inv = lax.rsqrt(now_sq)
        stretch = now_sq * now_inv * lax.rsqrt(rest_sq) - 1.0
        scaled = stretch * inverse_limit(c, k, spot)
        if k == 0:
            scaled = scaled - apart[...]
        hist = jnp.maximum(held[k][c], scaled)
        hist_rows[c, k] = hist
        weight = jnp.exp2(rest_sq * FALLOFF) * jnp.minimum(jnp.maximum(2.0 - hist, 0.0), 1.0)
        factor = weight * (stretch + rate * now_inv) * now_inv
        high = factor.astype(BF16)
        low = (factor - high.astype(F32)).astype(BF16)
        tile = split[spot]
        return dot_t(jnp.concatenate([high, low], 1), jnp.concatenate([tile, tile], 1))

    def cluster(c, buffer, after, after_buffer):
        sums = None
        for pair in range(SLOTS // 2):
            prepare(after, after_buffer, pair)
            for k in (2 * pair, 2 * pair + 1):
                term = pull(c, buffer, k)
                sums = term if sums is None else sums + term
        sums = jnp.transpose(sums)
        sums = sums[0:16] + sums[16:32] + sums[32:48]
        here = table[c]
        own = plain[c]
        acc = STIFFNESS * (sums[ROW_Y:ROW_Y + 3] - here[ROW_Y:ROW_Y + 3] * sums[ROW_ONE:ROW_ONE + 1])
        state_rows[c, 0:6] = own[0:6]
        state_rows[c, 6:9] = own[6:9] + 0.5 * TIME_STEP * acc
        state_rows[c, 9:12] = acc
        state_rows[c, 12:16] = own[12:16]

    tag_copies = [
        pltpu.make_async_copy(table.at[TAGS_AT[side]], tags.at[side], tag_sem.at[side]) for side in range(2)
    ]

    def send_pack(e, carry):
        c = leaver(e)
        pack[e, 0:16] = table[c]
        for k in range(SLOTS):
            spot = partner(c, k)
            pack[e, 16 + 8 * k:24 + 8 * k] = table[spot, 0:8]
            pack[e, 16 + 8 * SLOTS + k:17 + 8 * SLOTS + k] = inverse_limit(c, k, spot)
        pack[e, 16 + 9 * SLOTS:PACK_ROWS] = jnp.zeros((8 - SLOTS, POINTS), F32)
        pl.when(goes(e))(pack_copy(e).start)
        return carry

    def nth(i):
        inner = 5 + lax.rem(i, 2) + 4 * (i // 2)
        column = 4 + 4 * lax.rem(i, 2) + 3 * ((i - 4) // 2)
        row = 1 + lax.rem(i, 2) + 12 * ((i - 8) // 2)
        corner = 3 * lax.rem(i, 2) + 12 * ((i - 12) // 2)
        return jnp.where(i < 4, inner, jnp.where(i < 8, column, jnp.where(i < 12, row, corner)))

    for pair in range(SLOTS // 2):
        prepare(nth(0), 0, pair)

    def landed(sides):
        for n in sides:
            (dw, dn), copy = SIDES[n], halos[n]
            pl.when(jnp.logical_not(beyond(dw, dn)))(copy.wait_send)
            pl.when(jnp.logical_not(beyond(-dw, -dn)))(copy.wait_recv)

    def send_second(k, count):
        def go(e, carry):
            pl.when(goes(e))(functools.partial(send_hist, e, k, count))
            return carry

        lax.fori_loop(2, 4, go, 0)

    def two(i, carry):
        @pl.when(i == 1)
        def _():
            send_second(0, 2)
            landed(range(2, 4))
            lax.fori_loop(SIDE_AT[2], SIDE_AT[4], split_tile, 0, unroll=2)

        @pl.when(i == 3)
        def _():
            landed(range(0, 2))
            for copy in tag_copies:
                copy.start()
            lax.fori_loop(CLUSTERS, SIDE_AT[2], split_tile, 0, unroll=2)

        @pl.when(i == 4)
        def _():
            landed(range(4, 8))
            lax.fori_loop(0, 4, send_pack, 0)
            send_second(2, 4)
            lax.fori_loop(SIDE_AT[4], TILES, split_tile, 0, unroll=2)

        first, second = nth(2 * i), nth(2 * i + 1)
        cluster(first, 0, second, 1)
        cluster(second, 1, nth(jnp.minimum(2 * i + 2, CLUSTERS - 1)), 0)
        return carry

    lax.fori_loop(0, CLUSTERS // 2, two, 0)

    def send_state(e, carry):
        sent_state[e] = state_rows[leaver(e)]
        pl.when(goes(e))(state_copy(e).start)
        return carry

    lax.fori_loop(0, 4, send_state, 0)

    tail = jnp.where(lax.broadcasted_iota(jnp.int32, (8, POINTS), 0) == ROW_ONE - 8, 1.0, 0.0)

    def expect(e, carry):
        pl.when(comes(e))(pack_copy(e).wait_recv)
        own = jnp.concatenate(split_parts(packed[e, 0:16]), 0)
        mine = left_rows(own, 2)[:, 0:96]
        for pair in range(SLOTS // 2):
            theirs = []
            for k in (2 * pair, 2 * pair + 1):
                tile = jnp.concatenate([packed[e, 16 + 8 * k:24 + 8 * k], tail], 0)
                theirs.append(right_side(jnp.concatenate(split_parts(tile), 0)))
            forms_in[e, pair] = dot(mine, jnp.concatenate(theirs, 1))
        return carry

    lax.fori_loop(0, 4, expect, 0, unroll=4)

    for copy in tag_copies:
        copy.wait()
    for o in range(CLUSTERS):
        source = o
        for e in range(4):
            source = jnp.where(tags[e % 2, 8 * (e // 2), 0] == float(o), CLUSTERS + e, source)
        sources[o] = source

    def arrive(entries, parts):
        for k, count in parts:
            for e in entries:
                pl.when(comes(e))(hist_copy(e, k, count).wait_recv)

    first, second = ((0, 1), (1, 1), (2, 2), (4, 2)), ((0, 2), (2, 4))
    arrive((0, 1), first)
    arrive((2, 3), second)

    for e in range(4):
        @pl.when(goes(e))
        def _():
            for k, count in first if e < 2 else second:
                hist_copy(e, k, count).wait_send()

    def finish(e, carry):
        pl.when(comes(e))(state_copy(e).wait_recv)

        @pl.when(goes(e))
        def _():
            pack_copy(e).wait_send()
            state_copy(e).wait_send()
        return carry

    lax.fori_loop(0, 4, finish, 0)


def place_kernel(
    hist_rows, state_rows, state_in, packed, forms, sources,
    ref_out, disp_out, vel_out, acc_out, hist_out,
    states, arrived, state_sem, sem,
):
    def stays(o):
        return pltpu.make_async_copy(hist_rows.at[o], hist_out.at[o], sem.at[o])

    def arrives(o):
        return pltpu.make_async_copy(arrived.at[jnp.maximum(sources[o] - CLUSTERS, 0)], hist_out.at[o], sem.at[o])

    for o in range(CLUSTERS):
        pl.when(sources[o] < CLUSTERS)(stays(o).start)

    sub = lax.broadcasted_iota(jnp.int32, (POINTS, POINTS), 0)
    lane = lax.broadcasted_iota(jnp.int32, (POINTS, POINTS), 1)
    same = jnp.where(sub == lane, APART, 0.0).astype(F32)

    def take(e, carry):
        for k in range(SLOTS):
            pair, at = k // 2, pl.ds((k % 2) * POINTS, POINTS)
            rest_sq = forms[e, pair, 0:POINTS, at]
            if k == 0:
                rest_sq = rest_sq + same
            now_sq = jnp.maximum(rest_sq + forms[e, pair, POINTS:2 * POINTS, at], TINY)
            stretch = now_sq * lax.rsqrt(now_sq) * lax.rsqrt(rest_sq) - 1.0
            scaled = stretch * packed[e, 16 + 8 * SLOTS + k:17 + 8 * SLOTS + k]
            if k == 0:
                scaled = scaled - same
            arrived[e, k] = jnp.maximum(hist_rows[CLUSTERS + e, k], scaled)
        return carry

    lax.fori_loop(0, 4, take, 0)
    for o in range(CLUSTERS):
        pl.when(sources[o] >= CLUSTERS)(arrives(o).start)
    for o in range(CLUSTERS):
        source = sources[o]
        rows = jnp.where(source < CLUSTERS, state_rows[o], state_in[jnp.maximum(source - CLUSTERS, 0)])
        for f in range(4):
            for d in range(3):
                states[f, d, o // CN, o % CN:o % CN + 1] = rows[3 * f + d:3 * f + d + 1]
    copies = []
    for f, ref in enumerate((ref_out, disp_out, vel_out, acc_out)):
        copies.append(pltpu.make_async_copy(states.at[f], ref, state_sem.at[f]))
        copies[-1].start()
    for copy in copies:
        copy.wait()
    for o in range(CLUSTERS):
        pl.when(sources[o] < CLUSTERS)(stays(o).wait)
        pl.when(sources[o] >= CLUSTERS)(arrives(o).wait)


def per_device(
    wide_size, narrow_size,
    ref_local, displacement, velocity, acceleration, history, critical, active, partners, move_src, move_dst,
):
    vmem, smem, anywhere = (pl.BlockSpec(memory_space=m) for m in (pltpu.VMEM, pltpu.SMEM, pl.ANY))
    total = CLUSTERS + 4
    hist_shape = (total, SLOTS, POINTS, POINTS)
    operands = [
        ref_local, displacement, velocity, acceleration, critical, active, partners, move_src, move_dst,
        jnp.asarray(pairing(), BF16), history.reshape(CLUSTERS, SLOTS, POINTS, POINTS),
    ]
    operands = [pltpu.with_memory_space_constraint(x, pltpu.HBM) for x in operands]
    *rows, sources = pl.pallas_call(
        functools.partial(step_kernel, wide_size, narrow_size),
        out_shape=(
            pltpu.VMEM(hist_shape, F32),
            pltpu.VMEM((CLUSTERS, 16, POINTS), F32),
            pltpu.VMEM((4, 16, POINTS), F32),
            pltpu.VMEM((4, PACK_ROWS, POINTS), F32),
            pltpu.VMEM((4, SLOTS // 2, 2 * POINTS, 2 * POINTS), F32),
            pltpu.SMEM((CLUSTERS,), jnp.int32),
        ),
        in_specs=[anywhere] * len(operands),
        out_specs=(vmem,) * 5 + (smem,),
        scratch_shapes=[
            *[pltpu.VMEM((CLUSTERS, POINTS, POINTS), F32)] * SLOTS,
            *[pltpu.VMEM(ref_local.shape, F32)] * 4,
            pltpu.SMEM(critical.shape, F32),
            pltpu.SMEM(active.shape, jnp.int32),
            pltpu.SMEM(partners.shape, jnp.int32),
            pltpu.SMEM(move_src.shape, jnp.int32),
            pltpu.SMEM(move_dst.shape, jnp.int32),
            pltpu.VMEM((48, 3 * POINTS), BF16),
            pltpu.SMEM(((CW + 2) * (CN + 2),), jnp.int32),
            pltpu.VMEM((CLUSTERS, 16, POINTS), F32),
            pltpu.VMEM((TILES + 1, 16, POINTS), F32),
            pltpu.VMEM((TILES - CLUSTERS, 16, POINTS), F32),
            pltpu.VMEM((TILES + 1, 48, POINTS), BF16),
            pltpu.VMEM((CLUSTERS, 3 * POINTS, 128), BF16),
            pltpu.VMEM((2, SLOTS // 2, 3 * POINTS, 2 * POINTS), F32),
            pltpu.VMEM((POINTS, POINTS), F32),
            pltpu.SMEM((2, 16, POINTS), F32),
            pltpu.VMEM((4, SLOTS, POINTS, POINTS), F32),
            pltpu.VMEM((4, PACK_ROWS, POINTS), F32),
            pltpu.VMEM((4, 16, POINTS), F32),
            pltpu.SemaphoreType.DMA((10,)),
            pltpu.SemaphoreType.DMA((2,)),
            pltpu.SemaphoreType.DMA((SLOTS,)),
            pltpu.SemaphoreType.DMA((8,)),
            pltpu.SemaphoreType.DMA((8,)),
            *[pltpu.SemaphoreType.DMA((4, SLOTS))] * 2,
            *[pltpu.SemaphoreType.DMA((4,))] * 4,
        ],
        compiler_params=pltpu.CompilerParams(
            collective_id=0, has_side_effects=True, vmem_limit_bytes=26 << 20
        ),
        name="step",
    )(*operands)
    rows = [pltpu.with_memory_space_constraint(x, pltpu.VMEM) for x in rows]
    sources = pltpu.with_memory_space_constraint(sources, pltpu.SMEM)
    state = jax.ShapeDtypeStruct(ref_local.shape, F32)
    outs = pl.pallas_call(
        place_kernel,
        out_shape=(state,) * 4 + (jax.ShapeDtypeStruct((CLUSTERS, SLOTS, POINTS, POINTS), F32),),
        in_specs=[vmem] * 5 + [smem],
        out_specs=(anywhere,) * 5,
        scratch_shapes=[
            pltpu.VMEM((4,) + ref_local.shape, F32),
            pltpu.VMEM((4, SLOTS, POINTS, POINTS), F32),
            pltpu.SemaphoreType.DMA((4,)),
            pltpu.SemaphoreType.DMA((CLUSTERS,)),
        ],
        compiler_params=pltpu.CompilerParams(vmem_limit_bytes=8 << 20),
        name="place",
    )(*rows, sources)
    return outs[:4] + (outs[4].reshape(history.shape),)


def solution(mesh):
    field = P(None, "wide", "narrow", None)
    blocks = P("wide", "narrow", None)
    hist = P("wide", "narrow", None, None, None)
    moves = P("wide", "narrow", None, None)
    return jax.shard_map(
        functools.partial(per_device, mesh.shape["wide"], mesh.shape["narrow"]),
        mesh=mesh,
        in_specs=(field,) * 4 + (hist,) + (blocks,) * 3 + (moves,) * 2,
        out_specs=(field,) * 4 + (hist,),
        check_vma=False,
    )
```
